32 devices in a mesh: gx: 4 (over y, x), gy: 8 (over z, core).
Axes of the slice: x: 2, y: 2, z: 4, core: 2. Of those that a mesh axis runs over, the one named last changes fastest.
Arguments:
- prev_block: float32 [3, 8, 32, 64, 128], P(None, None, 'gx', 'gy'), may hold values from -20 to 20
- block: float32 [3, 8, 32, 64, 128], P(None, None, 'gx', 'gy'), may hold values from -20 to 20
- hop_seed: int32 [3, 32, 64, 128], P(None, 'gx', 'gy'), may hold values from 0 to 15
- levels: int32 [32, 64, 128], P('gx', 'gy'), may hold values from 0 to 15
- hop_table: float32 [3, 16, 3, 3], replicated, may hold values from -3 to 3
- onsite_table: float32 [16, 3], replicated, may hold values from -2 to 2
Outputs:
- next_block: float32 [3, 8, 32, 64, 128], P(None, None, 'gx', 'gy')
- alpha: float32 [8, 8], replicated
- beta: float32 [8, 8], replicated
The draws below stay inside these ranges and needn't reach their ends.
All inputs are finite; a program needn't handle non-finite values.
Results may differ from the reference program's by a relative error of at most 0.0003.
Values sent between devices are 32-bit elements; how exact they have to be, the bound alone decides.
No kernel may reach another device: no remote copies, remote signals or barrier semaphores. Data moves between devices by JAX's collectives and lax.ppermute only.
A program may use at most 64 MiB of HBM per device.

```python
import jax
import jax.numpy as jnp
from jax import lax

NZ = 128
ORB = 3
BLOCK = 8
KINDS = 16
LEVELS = 16
NX = 32
NY = 64


def pair_fields(key):
    shape = (ORB, BLOCK, NX, NY, NZ)
    key_one = jax.random.fold_in(key, 101)
    key_two = jax.random.fold_in(key, 102)
    first = jnp.clip(jax.random.normal(key_one, shape, jnp.float32), -5.0, 5.0)
    second = jnp.clip(jax.random.normal(key_two, shape, jnp.float32), -5.0, 5.0)
    xpos = jnp.arange(NX, dtype=jnp.float32)[:, None, None] / NX
    ypos = jnp.arange(NY, dtype=jnp.float32)[None, :, None] / NY
    ramp = 0.6 * jnp.exp(jnp.log(3.0) * 0.5 * (xpos + ypos))
    return (ramp * first, ramp * (0.4 * first + second))


def draw_prev_block(key, part):
    return pair_fields(key)[0]


def draw_block(key, part):
    return pair_fields(key)[1]


def touch_ends(array, stream_key, least, top_value):
    longest = array.shape.index(max(array.shape))
    spots = []
    for shift in (0, 1):
        where = [jax.random.randint(jax.random.fold_in(stream_key, axis), (), 0, length) for axis, length in enumerate(array.shape)]
        where[longest] = (where[longest] + shift) % array.shape[longest]
        spots.append(tuple(where))
    return array.at[spots[0]].set(least).at[spots[1]].set(top_value)


def normal_values(rng, shape, scale, bound, held_as=jnp.bfloat16):
    return jnp.clip(scale * jax.random.normal(rng, shape, jnp.float32), -bound, bound).astype(held_as)


def setup_inputs(seed: int = 0) -> dict:
    splits = jax.random.split(jax.random.key(seed), 7)
    return {
        "prev_block": draw_prev_block(jax.random.fold_in(splits[6], 71), 0),
        "block": draw_block(jax.random.fold_in(splits[6], 71), 0),
        "hop_seed": touch_ends(jax.random.randint(splits[2], (3, NX, NY, NZ), 0, KINDS), jax.random.fold_in(splits[2], 1), 0, KINDS - 1).astype(jnp.int32),
        "levels": touch_ends(jax.random.randint(splits[3], (NX, NY, NZ), 0, LEVELS), jax.random.fold_in(splits[3], 1), 0, LEVELS - 1).astype(jnp.int32),
        "hop_table": normal_values(splits[4], (3, KINDS, ORB, ORB), 0.5, 3.0, jnp.float32),
        "onsite_table": jnp.clip(jax.random.uniform(splits[5], (LEVELS, ORB), jnp.float32, -2.0, 2.0), -2.0, 2.0),
    }


HIGH = lax.Precision.HIGHEST

def apply_ham(field, hop_seed, levels, hop_table, onsite_table):
    energy = jnp.moveaxis(onsite_table[levels], -1, 0)
    image = energy[:, None] * field
    for direction in range(3):
        bonds = jnp.moveaxis(hop_table[direction][hop_seed[direction]], (-2, -1), (0, 1))
        ahead = jnp.roll(field, -1, axis=2 + direction)
        image = image + jnp.einsum('abxyz,bnxyz->anxyz', bonds, ahead, precision=HIGH)
        carried = jnp.einsum('abxyz,anxyz->bnxyz', bonds, field, precision=HIGH)
        image = image + jnp.roll(carried, 1, axis=2 + direction)
    return image

def inner(left, right):
    count = left.shape[0] * left.shape[2] * left.shape[3] * left.shape[4]
    return jnp.einsum('omxyz,onxyz->mn', left, right, precision=HIGH) / count

def combine(basis, coeffs):
    return jnp.einsum('okxyz,kn->onxyz', basis, coeffs, precision=HIGH)

def reference(prev_block, block, hop_seed, levels, hop_table, onsite_table):
    product = apply_ham(block, hop_seed, levels, hop_table, onsite_table)
    basis = jnp.concatenate([prev_block, block], axis=1)
    first = inner(basis, product)
    alpha = first[BLOCK:]
    residual_one = product - combine(basis, first)
    second = inner(basis, residual_one)
    residual_two = residual_one - combine(basis, second)
    gram = inner(residual_two, residual_two)
    lower = jnp.linalg.cholesky(gram)
    lower_inv = jax.scipy.linalg.solve_triangular(lower, jnp.eye(BLOCK, dtype=jnp.float32), lower=True)
    next_block = jnp.einsum('omxyz,nm->onxyz', residual_two, lower_inv, precision=HIGH)
    return (next_block, alpha, lower.T)
```

```python
import jax
import jax.numpy as jnp
from jax import lax
from jax.experimental import pallas as pl
from jax.experimental.pallas import tpu as pltpu
from jax.sharding import PartitionSpec as P

HIGH = lax.Precision.HIGHEST
F32 = jnp.float32
BF16 = jnp.bfloat16
LANES = 128
ROWS = 8
PARAMS = dict(vmem_limit_bytes=32 * 1024 * 1024)


def split(value):
    high = value.astype(BF16)
    low = (value - high.astype(F32)).astype(BF16)
    return high, low


def iota(shape, dim):
    return lax.broadcasted_iota(jnp.int32, shape, dim)


def dot(left, right, dims, precision=None):
    return lax.dot_general(
        left, right, (dims, ((), ())), precision=precision, preferred_element_type=F32
    )


def pick(table_ref, row, index):
    entries = jnp.broadcast_to(table_ref[row : row + 1, :], index.shape)
    return jnp.take_along_axis(entries, index, axis=1)


def bonds_of(table_ref, direction, index, orbs):
    base = direction * orbs * orbs
    return [
        [pick(table_ref, base + a * orbs + b, index) for b in range(orbs)] for a in range(orbs)
    ]


def times(bonds, field):
    return [sum(bonds[a][b] * field[b] for b in range(len(field))) for a in range(len(field))]


def times_transposed(bonds, field):
    return [sum(bonds[a][b] * field[a] for a in range(len(field))) for b in range(len(field))]


def pack_kernel(block_ref, seed_ref, xup_ref, xdown_ref, yup_ref, ydown_ref):
    orbs, width, nx, ny, _ = block_ref.shape
    for o in range(orbs):
        for n in range(width):
            spot = o * width + n
            xup_ref[spot] = block_ref[o, n, nx - 1]
            xdown_ref[spot] = block_ref[o, n, 0]
            yup_ref[spot] = block_ref[o, n, :, ny - 1, :]
            ydown_ref[spot] = block_ref[o, n, :, 0, :]
    xup_ref[orbs * width] = seed_ref[0, nx - 1].astype(F32)
    yup_ref[orbs * width] = seed_ref[1, :, ny - 1, :].astype(F32)


def small_sums(total, copies):
    rows, columns = total.shape
    same = (iota((rows, columns), 0) % ROWS) == (iota((rows, columns), 1) % ROWS)
    kept = jnp.where(same, total, 0.0)
    return kept.reshape(rows // ROWS, ROWS, columns).sum(axis=1)


def interior_kernel(
    prev_ref, block_ref, seed_ref, level_ref, table_ref, part_ref, high_ref, low_ref, gram_ref
):
    orbs, width, nx, ny, nz = block_ref.shape
    row = iota((ny, nz), 0)
    side = width * ny
    gram_ref[...] = jnp.zeros(gram_ref.shape, F32)

    def onsite(x, carry):
        index = [seed_ref[d, x] for d in range(3)]
        energy = [pick(table_ref, 3 * orbs * orbs + o, level_ref[x]) for o in range(orbs)]
        bond_y = bonds_of(table_ref, 1, index[1], orbs)
        bond_z = bonds_of(table_ref, 2, index[2], orbs)
        for n in range(width):
            here = [block_ref[o, n, x] for o in range(orbs)]
            image = [energy[o] * here[o] for o in range(orbs)]
            ahead = [jnp.where(row == ny - 1, 0.0, pltpu.roll(v, ny - 1, 0)) for v in here]
            image = [a + b for a, b in zip(image, times(bond_y, ahead))]
            carried = times_transposed(bond_y, here)
            image = [
                a + jnp.where(row == 0, 0.0, pltpu.roll(b, 1, 0)) for a, b in zip(image, carried)
            ]
            ahead = [pltpu.roll(v, nz - 1, 1) for v in here]
            image = [a + b for a, b in zip(image, times(bond_z, ahead))]
            carried = times_transposed(bond_z, here)
            image = [a + pltpu.roll(b, 1, 1) for a, b in zip(image, carried)]
            for o in range(orbs):
                part_ref[o, n, x] = image[o]
        return carry

    lax.fori_loop(0, nx, onsite, 0)

    def along_x(x, carry):
        bonds = bonds_of(table_ref, 0, seed_ref[0, x], orbs)
        for n in range(width):
            here = [block_ref[o, n, x] for o in range(orbs)]
            ahead = [block_ref[o, n, x + 1] for o in range(orbs)]
            forward = times(bonds, ahead)
            back = times_transposed(bonds, here)
            for o in range(orbs):
                part_ref[o, n, x] += forward[o]
                part_ref[o, n, x + 1] += back[o]
        return carry

    lax.fori_loop(0, nx - 1, along_x, 0)

    def products(pair, carry):
        for o in range(orbs):
            highs, lows = [], []
            for half in range(2):
                x = 2 * pair + half
                basis = jnp.concatenate(
                    [prev_ref[o, :, x].reshape(side, nz), block_ref[o, :, x].reshape(side, nz)], 0
                )
                high, low = split(basis)
                high_ref[o, x] = high
                low_ref[o, x] = low
                highs.append(high)
                lows.append(low)
            high = jnp.concatenate(highs, 1)
            low = jnp.concatenate(lows, 1)
            gram_ref[...] += (
                dot(high, high, ((1,), (1,)))
                + dot(high, low, ((1,), (1,)))
                + dot(low, high, ((1,), (1,)))
            )
        return carry

    lax.fori_loop(0, nx // 2, products, 0)


def halo_kernel(
    part_ref,
    seed_ref,
    table_ref,
    xlow_ref,
    xhigh_ref,
    ylow_ref,
    yhigh_ref,
    high_ref,
    low_ref,
    gram_ref,
    phigh_ref,
    plow_ref,
    sums_ref,
    image_ref,
    total_ref,
):
    orbs, width, nx, ny, nz = part_ref.shape
    side = width * ny
    last = orbs * width
    image_ref[...] = part_ref[...]

    bond_x = bonds_of(table_ref, 0, seed_ref[0, nx - 1], orbs)
    bond_xlow = bonds_of(table_ref, 0, xlow_ref[last].astype(jnp.int32), orbs)
    for n in range(width):
        forward = times(bond_x, [xhigh_ref[o * width + n] for o in range(orbs)])
        back = times_transposed(bond_xlow, [xlow_ref[o * width + n] for o in range(orbs)])
        for o in range(orbs):
            image_ref[o, n, nx - 1] += forward[o]
            image_ref[o, n, 0] += back[o]
    bond_y = bonds_of(table_ref, 1, seed_ref[1, :, ny - 1, :], orbs)
    bond_ylow = bonds_of(table_ref, 1, ylow_ref[last].astype(jnp.int32), orbs)
    for n in range(width):
        forward = times(bond_y, [yhigh_ref[o * width + n] for o in range(orbs)])
        back = times_transposed(bond_ylow, [ylow_ref[o * width + n] for o in range(orbs)])
        for o in range(orbs):
            image_ref[o, n, :, ny - 1, :] += forward[o]
            image_ref[o, n, :, 0, :] += back[o]

    total_ref[...] = jnp.zeros(total_ref.shape, F32)

    def products(pair, carry):
        for o in range(orbs):
            ins = [[], [], [], []]
            for half in range(2):
                x = 2 * pair + half
                high, low = split(image_ref[o, :, x].reshape(side, nz))
                phigh_ref[o, x] = high
                plow_ref[o, x] = low
                for group, value in zip(ins, (high, low, high_ref[o, x], low_ref[o, x])):
                    group.append(value)
            high, low, bhigh, blow = (jnp.concatenate(group, 1) for group in ins)
            both = jnp.concatenate([high, low], 0)
            total_ref[...] += dot(jnp.concatenate([bhigh, high], 0), both, ((1,), (1,))) + dot(
                jnp.concatenate([blow, low], 0), both, ((1,), (1,))
            )
        return carry

    lax.fori_loop(0, nx // 2, products, 0)

    first = small_sums(total_ref[...], 3)
    second = small_sums(gram_ref[...], 2)
    parts = [first[i * width : (i + 1) * width] for i in range(3)]
    parts += [second[i * width : (i + 1) * width] for i in range(2)]
    stacked = jnp.concatenate(parts, 1)
    spots = iota((LANES, LANES), 0)
    lanes = iota((LANES, LANES), 1)
    maps = []
    for i in range(3):
        maps.append(jnp.where(lanes == width * i + (spots // ny) % width, 1.0, 0.0))
    for i in range(2):
        maps.append(jnp.where(lanes == width * (3 + 2 * i) + spots // ny, 1.0, 0.0))
    sums = dot(stacked, jnp.concatenate(maps, 0), ((1,), (0,)), HIGH)
    half = width // 2
    folded = sums[:half] + pltpu.roll(sums, LANES // 2, 1)[half:]
    sums_ref[...] = jnp.broadcast_to(folded[None], sums_ref.shape)


def final_kernel(count, sums_ref, high_ref, low_ref, phigh_ref, plow_ref, next_ref, alpha_ref, beta_ref):
    orbs, nx, side, nz = phigh_ref.shape
    width = side // ROWS
    folded = jnp.sum(sums_ref[...], axis=0) / count
    sums = jnp.concatenate([folded, pltpu.roll(folded, LANES // 2, 1)], 0)
    first = jnp.concatenate([sums[:, 0:width], sums[:, width : 2 * width]], 0)
    norms = sums[:, 2 * width : 3 * width]
    metric = jnp.concatenate([sums[:, 3 * width : 5 * width], sums[:, 5 * width : 7 * width]], 0)
    alpha_ref[...] = first[width:]
    eye = jnp.where(iota((width, width), 0) == iota((width, width), 1), 1.0, 0.0)
    turned = dot(eye, first, ((1,), (1,)), HIGH)
    coeffs = 2.0 * turned - dot(turned, metric, ((1,), (0,)), HIGH)
    rest = turned - dot(coeffs, metric, ((1,), (0,)), HIGH)
    gram = norms - dot(
        jnp.concatenate([turned, coeffs], 1),
        jnp.concatenate([coeffs, rest], 1),
        ((1,), (1,)),
        HIGH,
    )
    pad = jnp.zeros((width, LANES - 4 * width), F32)
    table = jnp.concatenate([gram, eye, -coeffs, pad], 1)
    rows = iota((width, LANES), 0)
    scale = jnp.ones((width, LANES), F32)
    for k in range(width):
        pivot = jnp.broadcast_to(table[k : k + 1, k : k + 1], (width, LANES))
        column = jnp.broadcast_to(table[:, k : k + 1], (width, LANES))
        line = jnp.broadcast_to(table[k : k + 1, :], (width, LANES))
        table = jnp.where(rows > k, table - column / pivot * line, table)
        scale = jnp.where(rows == k, lax.rsqrt(pivot), scale)
    table = table * scale
    keep = iota((width, width), 0) <= iota((width, width), 1)
    beta_ref[...] = jnp.where(keep, table[:, :width], 0.0)
    lanes = iota((width, LANES), 1)
    basis_part = jnp.take_along_axis(table, 2 * width + lanes // ROWS, axis=1)
    product_part = jnp.take_along_axis(table, width + (lanes // ROWS) % width, axis=1)

    def spread(value, columns):
        grown = jnp.broadcast_to(value[:, None, :], (width, ROWS, LANES)).reshape(side, LANES)
        same = iota((side, LANES), 0) % ROWS == iota((side, LANES), 1) % ROWS
        return jnp.where(same, grown, 0.0)[:, :columns]

    mixed = jnp.concatenate([spread(basis_part, LANES), spread(product_part, side)], 1)
    mixed_high, mixed_low = split(mixed)

    def combine(pair, carry):
        for o in range(orbs):
            highs, lows = [], []
            for half in range(2):
                x = 2 * pair + half
                highs.append(jnp.concatenate([high_ref[o, x], phigh_ref[o, x]], 0))
                lows.append(jnp.concatenate([low_ref[o, x], plow_ref[o, x]], 0))
            high = jnp.concatenate(highs, 1)
            low = jnp.concatenate(lows, 1)
            dims = ((1,), (0,))
            out = dot(mixed_high, high, dims) + dot(mixed_low, high, dims) + dot(mixed_high, low, dims)
            for half in range(2):
                x = 2 * pair + half
                next_ref[o, :, x] = out[:, half * nz : (half + 1) * nz].reshape(width, ROWS, nz)
        return carry

    lax.fori_loop(0, nx // 2, combine, 0)


def shifted(value, axis, steps):
    count = lax.axis_size(axis)
    return lax.ppermute(value, axis, [(i, (i + steps) % count) for i in range(count)])


def per_device(prev_block, block, hop_seed, levels, hop_table, onsite_table):
    orbs, width, nx, ny, nz = block.shape
    devices = lax.axis_size("gx") * lax.axis_size("gy")
    count = orbs * nx * ny * nz * devices
    fields = orbs * width
    table = jnp.concatenate(
        [jnp.transpose(hop_table, (0, 2, 3, 1)).reshape(-1, hop_table.shape[1]), onsite_table.T], 0
    )
    table = jnp.pad(table, ((0, 0), (0, LANES - table.shape[1])))
    params = pltpu.CompilerParams(**PARAMS)

    xup, xdown, yup, ydown = pl.pallas_call(
        pack_kernel,
        out_shape=[
            pltpu.VMEM((fields + 1, ny, nz), F32),
            pltpu.VMEM((fields, ny, nz), F32),
            pltpu.VMEM((fields + 1, nx, nz), F32),
            pltpu.VMEM((fields, nx, nz), F32),
        ],
        compiler_params=params,
        name="pack",
    )(block, hop_seed)
    xlow = shifted(xup, "gx", 1)
    ylow = shifted(yup, "gy", 1)
    xhigh = shifted(xdown, "gx", -1)
    yhigh = shifted(ydown, "gy", -1)

    side = width * ny
    part, high, low, gram = pl.pallas_call(
        interior_kernel,
        out_shape=[
            pltpu.VMEM(block.shape, F32),
            pltpu.VMEM((orbs, nx, 2 * side, nz), BF16),
            pltpu.VMEM((orbs, nx, 2 * side, nz), BF16),
            pltpu.VMEM((2 * side, 2 * side), F32),
        ],
        compiler_params=params,
        cost_estimate=pl.CostEstimate(flops=10**8, bytes_accessed=4 * 10**6, transcendentals=0),
        name="interior",
    )(prev_block, block, hop_seed, levels, table)

    phigh, plow, sums = pl.pallas_call(
        halo_kernel,
        out_shape=[
            pltpu.VMEM((orbs, nx, side, nz), BF16),
            pltpu.VMEM((orbs, nx, side, nz), BF16),
            pltpu.VMEM((devices, width // 2, LANES), F32),
        ],
        scratch_shapes=[pltpu.VMEM(block.shape, F32), pltpu.VMEM((3 * side, 2 * side), F32)],
        compiler_params=params,
        name="halo",
    )(part, hop_seed, table, xlow, xhigh, ylow, yhigh, high, low, gram)

    sums = lax.all_to_all(sums, ("gx", "gy"), 0, 0)

    next_block, alpha, beta = pl.pallas_call(
        lambda *refs: final_kernel(count, *refs),
        out_shape=[
            jax.ShapeDtypeStruct(block.shape, F32),
            jax.ShapeDtypeStruct((width, width), F32),
            jax.ShapeDtypeStruct((width, width), F32),
        ],
        compiler_params=params,
        name="final",
    )(sums, high, low, phigh, plow)
    return next_block, alpha, beta


def solution(mesh):
    in_specs = (
        P(None, None, "gx", "gy", None),
        P(None, None, "gx", "gy", None),
        P(None, "gx", "gy", None),
        P("gx", "gy", None),
        P(),
        P(),
    )
    out_specs = (P(None, None, "gx", "gy", None), P(), P())
    return jax.shard_map(
        per_device, mesh=mesh, in_specs=in_specs, out_specs=out_specs, check_vma=False
    )
```

```python
import jax
import jax.numpy as jnp
from jax import lax
from jax.experimental import pallas as pl
from jax.experimental.pallas import tpu as pltpu
from jax.sharding import PartitionSpec as P

HIGH = lax.Precision.HIGHEST
F32 = jnp.float32
BF16 = jnp.bfloat16
LANES = 128
ROWS = 8
PARAMS = dict(vmem_limit_bytes=32 * 1024 * 1024)


def split(value):
    high = value.astype(BF16)
    low = (value - high.astype(F32)).astype(BF16)
    return high, low


def iota(shape, dim):
    return lax.broadcasted_iota(jnp.int32, shape, dim)


def dot(left, right, dims, precision=None):
    return lax.dot_general(
        left, right, (dims, ((), ())), precision=precision, preferred_element_type=F32
    )


def pick(table_ref, row, index):
    entries = jnp.broadcast_to(table_ref[row : row + 1, :], index.shape)
    return jnp.take_along_axis(entries, index, axis=1)


def bonds_of(table_ref, direction, index, orbs):
    base = direction * orbs * orbs
    return [
        [pick(table_ref, base + a * orbs + b, index) for b in range(orbs)] for a in range(orbs)
    ]


def fill_table(table_ref, hop_ref, onsite_ref):
    orbs, kinds = hop_ref.shape[1], hop_ref.shape[3]
    for d in range(3):
        for a in range(orbs):
            base = (d * orbs + a) * orbs
            table_ref[base : base + orbs, :kinds] = hop_ref[d, a]
    base = 3 * orbs * orbs
    table_ref[base : base + orbs, : onsite_ref.shape[1]] = onsite_ref[...]


def times(bonds, field):
    return [sum(bonds[a][b] * field[b] for b in range(len(field))) for a in range(len(field))]


def times_transposed(bonds, field):
    return [sum(bonds[a][b] * field[a] for a in range(len(field))) for b in range(len(field))]


def pack_kernel(
    block_in,
    seed_in,
    level_in,
    hop_in,
    onsite_in,
    block_ref,
    seed_ref,
    level_ref,
    hop_ref,
    onsite_ref,
    xup_ref,
    xdown_ref,
    yup_ref,
    ydown_ref,
    sems,
):
    orbs, width, nx, ny, _ = block_ref.shape
    pairs = [(block_in.at[o], block_ref.at[o]) for o in range(orbs)]
    pairs += [(seed_in, seed_ref), (level_in, level_ref), (hop_in, hop_ref), (onsite_in, onsite_ref)]
    loads = [pltpu.make_async_copy(*pair, sems.at[i]) for i, pair in enumerate(pairs)]
    for load in loads:
        load.start()
    for o in range(orbs):
        loads[o].wait()
        for n in range(width):
            spot = o * width + n
            xup_ref[spot] = block_ref[o, n, nx - 1]
            xdown_ref[spot] = block_ref[o, n, 0]
            yup_ref[spot] = block_ref[o, n, :, ny - 1, :]
            ydown_ref[spot] = block_ref[o, n, :, 0, :]
    loads[orbs].wait()
    xup_ref[orbs * width] = seed_ref[0, nx - 1].astype(F32)
    yup_ref[orbs * width] = seed_ref[1, :, ny - 1, :].astype(F32)
    for load in loads[orbs + 1 :]:
        load.wait()


def small_sums(total, copies):
    rows, columns = total.shape
    same = (iota((rows, columns), 0) % ROWS) == (iota((rows, columns), 1) % ROWS)
    kept = jnp.where(same, total, 0.0)
    return kept.reshape(rows // ROWS, ROWS, columns).sum(axis=1)


def interior_kernel(
    prev_ref,
    block_ref,
    seed_ref,
    level_ref,
    hop_ref,
    onsite_ref,
    part_ref,
    high_ref,
    low_ref,
    gram_ref,
    table_ref,
):
    orbs, width, nx, ny, nz = block_ref.shape
    fill_table(table_ref, hop_ref, onsite_ref)
    row = iota((ny, nz), 0)
    side = width * ny
    gram_ref[...] = jnp.zeros(gram_ref.shape, F32)

    def onsite(x, carry):
        index = [seed_ref[d, x] for d in range(3)]
        energy = [pick(table_ref, 3 * orbs * orbs + o, level_ref[x]) for o in range(orbs)]
        bond_y = bonds_of(table_ref, 1, index[1], orbs)
        bond_z = bonds_of(table_ref, 2, index[2], orbs)
        for n in range(width):
            here = [block_ref[o, n, x] for o in range(orbs)]
            image = [energy[o] * here[o] for o in range(orbs)]
            ahead = [jnp.where(row == ny - 1, 0.0, pltpu.roll(v, ny - 1, 0)) for v in here]
            image = [a + b for a, b in zip(image, times(bond_y, ahead))]
            carried = times_transposed(bond_y, here)
            image = [
                a + jnp.where(row == 0, 0.0, pltpu.roll(b, 1, 0)) for a, b in zip(image, carried)
            ]
            ahead = [pltpu.roll(v, nz - 1, 1) for v in here]
            image = [a + b for a, b in zip(image, times(bond_z, ahead))]
            carried = times_transposed(bond_z, here)
            image = [a + pltpu.roll(b, 1, 1) for a, b in zip(image, carried)]
            for o in range(orbs):
                part_ref[o, n, x] = image[o]
        return carry

    lax.fori_loop(0, nx, onsite, 0)

    def along_x(x, carry):
        bonds = bonds_of(table_ref, 0, seed_ref[0, x], orbs)
        for n in range(width):
            here = [block_ref[o, n, x] for o in range(orbs)]
            ahead = [block_ref[o, n, x + 1] for o in range(orbs)]
            forward = times(bonds, ahead)
            back = times_transposed(bonds, here)
            for o in range(orbs):
                part_ref[o, n, x] += forward[o]
                part_ref[o, n, x + 1] += back[o]
        return carry

    lax.fori_loop(0, nx - 1, along_x, 0)

    def products(pair, carry):
        for o in range(orbs):
            highs, lows = [], []
            for half in range(2):
                x = 2 * pair + half
                basis = jnp.concatenate(
                    [prev_ref[o, :, x].reshape(side, nz), block_ref[o, :, x].reshape(side, nz)], 0
                )
                high, low = split(basis)
                high_ref[o, x] = high
                low_ref[o, x] = low
                highs.append(high)
                lows.append(low)
            high = jnp.concatenate(highs, 1)
            low = jnp.concatenate(lows, 1)
            gram_ref[...] += (
                dot(high, high, ((1,), (1,)))
                + dot(high, low, ((1,), (1,)))
                + dot(low, high, ((1,), (1,)))
            )
        return carry

    lax.fori_loop(0, nx // 2, products, 0)


def halo_kernel(
    part_ref,
    seed_ref,
    table_ref,
    xlow_ref,
    xhigh_ref,
    ylow_ref,
    yhigh_ref,
    high_ref,
    low_ref,
    gram_ref,
    phigh_ref,
    plow_ref,
    sums_ref,
    image_ref,
    total_ref,
):
    orbs, width, nx, ny, nz = part_ref.shape
    side = width * ny
    last = orbs * width
    image_ref[...] = part_ref[...]

    bond_x = bonds_of(table_ref, 0, seed_ref[0, nx - 1], orbs)
    bond_xlow = bonds_of(table_ref, 0, xlow_ref[last].astype(jnp.int32), orbs)
    for n in range(width):
        forward = times(bond_x, [xhigh_ref[o * width + n] for o in range(orbs)])
        back = times_transposed(bond_xlow, [xlow_ref[o * width + n] for o in range(orbs)])
        for o in range(orbs):
            image_ref[o, n, nx - 1] += forward[o]
            image_ref[o, n, 0] += back[o]
    bond_y = bonds_of(table_ref, 1, seed_ref[1, :, ny - 1, :], orbs)
    bond_ylow = bonds_of(table_ref, 1, ylow_ref[last].astype(jnp.int32), orbs)
    for n in range(width):
        forward = times(bond_y, [yhigh_ref[o * width + n] for o in range(orbs)])
        back = times_transposed(bond_ylow, [ylow_ref[o * width + n] for o in range(orbs)])
        for o in range(orbs):
            image_ref[o, n, :, ny - 1, :] += forward[o]
            image_ref[o, n, :, 0, :] += back[o]

    total_ref[...] = jnp.zeros(total_ref.shape, F32)

    def products(pair, carry):
        for o in range(orbs):
            ins = [[], [], [], []]
            for half in range(2):
                x = 2 * pair + half
                high, low = split(image_ref[o, :, x].reshape(side, nz))
                phigh_ref[o, x] = high
                plow_ref[o, x] = low
                for group, value in zip(ins, (high, low, high_ref[o, x], low_ref[o, x])):
                    group.append(value)
            high, low, bhigh, blow = (jnp.concatenate(group, 1) for group in ins)
            both = jnp.concatenate([high, low], 0)
            total_ref[...] += dot(jnp.concatenate([bhigh, high], 0), both, ((1,), (1,))) + dot(
                jnp.concatenate([blow, low], 0), both, ((1,), (1,))
            )
        return carry

    lax.fori_loop(0, nx // 2, products, 0)

    first = small_sums(total_ref[...], 3)
    second = small_sums(gram_ref[...], 2)
    parts = [first[i * width : (i + 1) * width] for i in range(3)]
    parts += [second[i * width : (i + 1) * width] for i in range(2)]
    stacked = jnp.concatenate(parts, 1)
    spots = iota((LANES, LANES), 0)
    lanes = iota((LANES, LANES), 1)
    maps = []
    for i in range(3):
        maps.append(jnp.where(lanes == width * i + (spots // ny) % width, 1.0, 0.0))
    for i in range(2):
        maps.append(jnp.where(lanes == width * (3 + 2 * i) + spots // ny, 1.0, 0.0))
    sums = dot(stacked, jnp.concatenate(maps, 0), ((1,), (0,)), HIGH)
    half = width // 2
    folded = sums[:half] + pltpu.roll(sums, LANES // 2, 1)[half:]
    sums_ref[...] = jnp.broadcast_to(folded[None], sums_ref.shape)


def final_kernel(count, sums_ref, high_ref, low_ref, phigh_ref, plow_ref, next_ref, alpha_ref, beta_ref):
    orbs, nx, side, nz = phigh_ref.shape
    width = side // ROWS
    folded = jnp.sum(sums_ref[...], axis=0) / count
    sums = jnp.concatenate([folded, pltpu.roll(folded, LANES // 2, 1)], 0)
    first = jnp.concatenate([sums[:, 0:width], sums[:, width : 2 * width]], 0)
    norms = sums[:, 2 * width : 3 * width]
    metric = jnp.concatenate([sums[:, 3 * width : 5 * width], sums[:, 5 * width : 7 * width]], 0)
    alpha_ref[...] = first[width:]
    eye = jnp.where(iota((width, width), 0) == iota((width, width), 1), 1.0, 0.0)
    turned = dot(eye, first, ((1,), (1,)), HIGH)
    coeffs = 2.0 * turned - dot(turned, metric, ((1,), (0,)), HIGH)
    rest = turned - dot(coeffs, metric, ((1,), (0,)), HIGH)
    gram = norms - dot(
        jnp.concatenate([turned, coeffs], 1),
        jnp.concatenate([coeffs, rest], 1),
        ((1,), (1,)),
        HIGH,
    )
    pad = jnp.zeros((width, LANES - 4 * width), F32)
    table = jnp.concatenate([gram, eye, -coeffs, pad], 1)
    rows = iota((width, LANES), 0)
    scale = jnp.ones((width, LANES), F32)
    for k in range(width):
        pivot = jnp.broadcast_to(table[k : k + 1, k : k + 1], (width, LANES))
        column = jnp.broadcast_to(table[:, k : k + 1], (width, LANES))
        line = jnp.broadcast_to(table[k : k + 1, :], (width, LANES))
        table = jnp.where(rows > k, table - column / pivot * line, table)
        scale = jnp.where(rows == k, lax.rsqrt(pivot), scale)
    table = table * scale
    keep = iota((width, width), 0) <= iota((width, width), 1)
    beta_ref[...] = jnp.where(keep, table[:, :width], 0.0)
    lanes = iota((width, LANES), 1)
    basis_part = jnp.take_along_axis(table, 2 * width + lanes // ROWS, axis=1)
    product_part = jnp.take_along_axis(table, width + (lanes // ROWS) % width, axis=1)

    def spread(value, columns):
        grown = jnp.broadcast_to(value[:, None, :], (width, ROWS, LANES)).reshape(side, LANES)
        same = iota((side, LANES), 0) % ROWS == iota((side, LANES), 1) % ROWS
        return jnp.where(same, grown, 0.0)[:, :columns]

    mixed = jnp.concatenate([spread(basis_part, LANES), spread(product_part, side)], 1)
    mixed_high, mixed_low = split(mixed)

    def combine(pair, carry):
        for o in range(orbs):
            highs, lows = [], []
            for half in range(2):
                x = 2 * pair + half
                highs.append(jnp.concatenate([high_ref[o, x], phigh_ref[o, x]], 0))
                lows.append(jnp.concatenate([low_ref[o, x], plow_ref[o, x]], 0))
            high = jnp.concatenate(highs, 1)
            low = jnp.concatenate(lows, 1)
            dims = ((1,), (0,))
            out = dot(mixed_high, high, dims) + dot(mixed_low, high, dims) + dot(mixed_high, low, dims)
            for half in range(2):
                x = 2 * pair + half
                next_ref[o, :, x] = out[:, half * nz : (half + 1) * nz].reshape(width, ROWS, nz)
        return carry

    lax.fori_loop(0, nx // 2, combine, 0)


def shifted(value, axis, steps):
    count = lax.axis_size(axis)
    return lax.ppermute(value, axis, [(i, (i + steps) % count) for i in range(count)])


def per_device(prev_block, block, hop_seed, levels, hop_table, onsite_table):
    orbs, width, nx, ny, nz = block.shape
    devices = lax.axis_size("gx") * lax.axis_size("gy")
    count = orbs * nx * ny * nz * devices
    fields = orbs * width
    hops = jnp.transpose(hop_table, (0, 2, 3, 1))
    onsite = onsite_table.T
    table_rows = 3 * orbs * orbs + ROWS
    outside = pl.BlockSpec(memory_space=pltpu.HBM)

    def stay(value):
        return pltpu.with_memory_space_constraint(value, pltpu.HBM)

    params = pltpu.CompilerParams(**PARAMS)

    block_here, seed_here, levels_here, hops_here, onsite_here, xup, xdown, yup, ydown = pl.pallas_call(
        pack_kernel,
        in_specs=[outside] * 5,
        out_shape=[
            pltpu.VMEM(block.shape, F32),
            pltpu.VMEM(hop_seed.shape, jnp.int32),
            pltpu.VMEM(levels.shape, jnp.int32),
            pltpu.VMEM(hops.shape, F32),
            pltpu.VMEM(onsite.shape, F32),
            pltpu.VMEM((fields + 1, ny, nz), F32),
            pltpu.VMEM((fields, ny, nz), F32),
            pltpu.VMEM((fields + 1, nx, nz), F32),
            pltpu.VMEM((fields, nx, nz), F32),
        ],
        scratch_shapes=[pltpu.SemaphoreType.DMA((orbs + 4,))],
        compiler_params=params,
        name="pack",
    )(stay(block), stay(hop_seed), stay(levels), stay(hops), stay(onsite))
    xlow = shifted(xup, "gx", 1)
    ylow = shifted(yup, "gy", 1)
    xhigh = shifted(xdown, "gx", -1)
    yhigh = shifted(ydown, "gy", -1)

    side = width * ny
    part, high, low, gram, table = pl.pallas_call(
        interior_kernel,
        out_shape=[
            pltpu.VMEM(block.shape, F32),
            pltpu.VMEM((orbs, nx, 2 * side, nz), BF16),
            pltpu.VMEM((orbs, nx, 2 * side, nz), BF16),
            pltpu.VMEM((2 * side, 2 * side), F32),
            pltpu.VMEM((table_rows, LANES), F32),
        ],
        compiler_params=params,
        cost_estimate=pl.CostEstimate(flops=10**8, bytes_accessed=4 * 10**6, transcendentals=0),
        name="interior",
    )(prev_block, block_here, seed_here, levels_here, hops_here, onsite_here)

    phigh, plow, sums = pl.pallas_call(
        halo_kernel,
        out_shape=[
            pltpu.VMEM((orbs, nx, side, nz), BF16),
            pltpu.VMEM((orbs, nx, side, nz), BF16),
            pltpu.VMEM((devices, width // 2, LANES), F32),
        ],
        scratch_shapes=[pltpu.VMEM(block.shape, F32), pltpu.VMEM((3 * side, 2 * side), F32)],
        compiler_params=params,
        name="halo",
    )(part, seed_here, table, xlow, xhigh, ylow, yhigh, high, low, gram)

    sums = lax.all_to_all(sums, ("gx", "gy"), 0, 0)

    next_block, alpha, beta = pl.pallas_call(
        lambda *refs: final_kernel(count, *refs),
        out_shape=[
            jax.ShapeDtypeStruct(block.shape, F32),
            jax.ShapeDtypeStruct((width, width), F32),
            jax.ShapeDtypeStruct((width, width), F32),
        ],
        compiler_params=params,
        name="final",
    )(sums, high, low, phigh, plow)
    return next_block, alpha, beta


def solution(mesh):
    in_specs = (
        P(None, None, "gx", "gy", None),
        P(None, None, "gx", "gy", None),
        P(None, "gx", "gy", None),
        P("gx", "gy", None),
        P(),
        P(),
    )
    out_specs = (P(None, None, "gx", "gy", None), P(), P())
    return jax.shard_map(
        per_device, mesh=mesh, in_specs=in_specs, out_specs=out_specs, check_vma=False
    )
```

```python
import jax
import jax.numpy as jnp
from jax import lax
from jax.experimental import pallas as pl
from jax.experimental.pallas import tpu as pltpu
from jax.sharding import PartitionSpec as P

HIGH = lax.Precision.HIGHEST
F32 = jnp.float32
BF16 = jnp.bfloat16
LANES = 128
ROWS = 8
PARAMS = dict(vmem_limit_bytes=32 * 1024 * 1024)


def split(value):
    high = value.astype(BF16)
    low = (value - high.astype(F32)).astype(BF16)
    return high, low


def iota(shape, dim):
    return lax.broadcasted_iota(jnp.int32, shape, dim)


def dot(left, right, dims, precision=None):
    return lax.dot_general(
        left, right, (dims, ((), ())), precision=precision, preferred_element_type=F32
    )


def pick(table_ref, row, index):
    entries = jnp.broadcast_to(table_ref[row : row + 1, :], index.shape)
    return jnp.take_along_axis(entries, index, axis=1)


def bonds_of(table_ref, direction, index, orbs):
    base = direction * orbs * orbs
    return [
        [pick(table_ref, base + a * orbs + b, index) for b in range(orbs)] for a in range(orbs)
    ]


def fill_table(table_ref, hop_ref, onsite_ref):
    orbs, kinds = hop_ref.shape[1], hop_ref.shape[3]
    for d in range(3):
        for a in range(orbs):
            base = (d * orbs + a) * orbs
            table_ref[base : base + orbs, :kinds] = hop_ref[d, a]
    base = 3 * orbs * orbs
    table_ref[base : base + orbs, : onsite_ref.shape[1]] = onsite_ref[...]


def times(bonds, field):
    return [sum(bonds[a][b] * field[b] for b in range(len(field))) for a in range(len(field))]


def times_transposed(bonds, field):
    return [sum(bonds[a][b] * field[a] for a in range(len(field))) for b in range(len(field))]


def pack_kernel(
    block_in,
    seed_in,
    level_in,
    hop_in,
    onsite_in,
    block_ref,
    seed_ref,
    level_ref,
    hop_ref,
    onsite_ref,
    xup_ref,
    xdown_ref,
    yup_ref,
    ydown_ref,
    sems,
):
    orbs, width, nx, ny, _ = block_ref.shape
    pairs = [(block_in.at[o], block_ref.at[o]) for o in range(orbs)]
    pairs += [(seed_in, seed_ref), (level_in, level_ref), (hop_in, hop_ref), (onsite_in, onsite_ref)]
    loads = [pltpu.make_async_copy(*pair, sems.at[i]) for i, pair in enumerate(pairs)]
    for load in loads:
        load.start()
    for o in range(orbs):
        loads[o].wait()
        for n in range(width):
            spot = o * width + n
            xup_ref[spot] = block_ref[o, n, nx - 1]
            xdown_ref[spot] = block_ref[o, n, 0]
            yup_ref[spot] = block_ref[o, n, :, ny - 1, :]
            ydown_ref[spot] = block_ref[o, n, :, 0, :]
    loads[orbs].wait()
    xup_ref[orbs * width] = seed_ref[0, nx - 1].astype(F32)
    yup_ref[orbs * width] = seed_ref[1, :, ny - 1, :].astype(F32)
    for load in loads[orbs + 1 :]:
        load.wait()


def kept_sums(total):
    rows, columns = total.shape
    same = (iota((rows, columns), 0) % ROWS) == (iota((rows, columns), 1) % ROWS)
    kept = jnp.where(same, total, 0.0)
    return kept.reshape(rows // ROWS, ROWS, columns).sum(axis=1)


def gathered(value, spots):
    high, low = split(value)
    last = (value - high.astype(F32) - low.astype(F32)).astype(BF16)
    pieces = dot(jnp.concatenate([high, low, last], 0), spots.astype(BF16), ((1,), (0,)))
    rows = value.shape[0]
    return pieces[:rows] + pieces[rows : 2 * rows] + pieces[2 * rows :]


def interior_kernel(
    prev_ref,
    block_ref,
    seed_ref,
    level_ref,
    hop_ref,
    onsite_ref,
    part_ref,
    high_ref,
    low_ref,
    metric_ref,
    table_ref,
    gram_ref,
):
    orbs, width, nx, ny, nz = block_ref.shape
    fill_table(table_ref, hop_ref, onsite_ref)
    row = iota((ny, nz), 0)
    side = width * ny

    def stencil(x, carry):
        before = jnp.maximum(x - 1, 0)
        inside = jnp.where(x > 0, 1.0, 0.0)
        energy = [pick(table_ref, 3 * orbs * orbs + o, level_ref[x]) for o in range(orbs)]
        bond_x = bonds_of(table_ref, 0, seed_ref[0, before], orbs)
        bond_x = [[inside * value for value in line] for line in bond_x]
        bond_y = bonds_of(table_ref, 1, seed_ref[1, x], orbs)
        bond_z = bonds_of(table_ref, 2, seed_ref[2, x], orbs)
        for n in range(width):
            here = [block_ref[o, n, x] for o in range(orbs)]
            behind = [block_ref[o, n, before] for o in range(orbs)]
            forward = times(bond_x, here)
            for o in range(orbs):
                part_ref[o, n, before] += forward[o]
            image = [energy[o] * here[o] for o in range(orbs)]
            image = [a + b for a, b in zip(image, times_transposed(bond_x, behind))]
            ahead = [jnp.where(row == ny - 1, 0.0, pltpu.roll(v, ny - 1, 0)) for v in here]
            image = [a + b for a, b in zip(image, times(bond_y, ahead))]
            carried = times_transposed(bond_y, here)
            image = [
                a + jnp.where(row == 0, 0.0, pltpu.roll(b, 1, 0)) for a, b in zip(image, carried)
            ]
            ahead = [pltpu.roll(v, nz - 1, 1) for v in here]
            image = [a + b for a, b in zip(image, times(bond_z, ahead))]
            carried = times_transposed(bond_z, here)
            image = [a + pltpu.roll(b, 1, 1) for a, b in zip(image, carried)]
            for o in range(orbs):
                part_ref[o, n, x] = image[o]
        return carry

    lax.fori_loop(0, nx, stencil, 0)
    gram_ref[...] = jnp.zeros(gram_ref.shape, F32)

    def products(pair, carry):
        for o in range(orbs):
            highs, lows = [], []
            for half in range(2):
                x = 2 * pair + half
                basis = jnp.concatenate(
                    [prev_ref[o, :, x].reshape(side, nz), block_ref[o, :, x].reshape(side, nz)], 0
                )
                high, low = split(basis)
                high_ref[o, x] = high
                low_ref[o, x] = low
                highs.append(high)
                lows.append(low)
            high = jnp.concatenate(highs, 1)
            low = jnp.concatenate(lows, 1)
            gram_ref[...] += dot(high, jnp.concatenate([high, low], 0), ((1,), (1,)))
        return carry

    lax.fori_loop(0, nx // 2, products, 0)
    crossed = gram_ref[:, 2 * side :]
    sums = kept_sums(gram_ref[:, : 2 * side] + crossed + crossed.T)
    spots = iota((LANES, LANES), 0) // ny
    lanes = iota((LANES, LANES), 1) % (LANES // 2)
    maps = [jnp.where(lanes == width * (3 + 2 * i) + spots, 1.0, 0.0) for i in range(2)]
    parts = [sums[i * width : (i + 1) * width] for i in range(2)]
    metric_ref[...] = gathered(jnp.concatenate(parts, 1), jnp.concatenate(maps, 0))


def halo_kernel(
    part_in,
    seed_ref,
    table_ref,
    xlow_ref,
    xhigh_ref,
    ylow_ref,
    yhigh_ref,
    high_ref,
    low_ref,
    metric_ref,
    phigh_ref,
    plow_ref,
    sums_ref,
    part_ref,
    total_ref,
):
    orbs, width, nx, ny, nz = part_ref.shape
    side = width * ny
    last = orbs * width

    bond_x = bonds_of(table_ref, 0, seed_ref[0, nx - 1], orbs)
    bond_xlow = bonds_of(table_ref, 0, xlow_ref[last].astype(jnp.int32), orbs)
    for n in range(width):
        forward = times(bond_x, [xhigh_ref[o * width + n] for o in range(orbs)])
        back = times_transposed(bond_xlow, [xlow_ref[o * width + n] for o in range(orbs)])
        for o in range(orbs):
            part_ref[o, n, nx - 1] += forward[o]
            part_ref[o, n, 0] += back[o]
    bond_y = bonds_of(table_ref, 1, seed_ref[1, :, ny - 1, :], orbs)
    bond_ylow = bonds_of(table_ref, 1, ylow_ref[last].astype(jnp.int32), orbs)
    for n in range(width):
        forward = times(bond_y, [yhigh_ref[o * width + n] for o in range(orbs)])
        back = times_transposed(bond_ylow, [ylow_ref[o * width + n] for o in range(orbs)])
        for o in range(orbs):
            part_ref[o, n, :, ny - 1, :] += forward[o]
            part_ref[o, n, :, 0, :] += back[o]

    total_ref[...] = jnp.zeros(total_ref.shape, F32)

    def products(pair, carry):
        for o in range(orbs):
            ins = [[], [], [], []]
            for half in range(2):
                x = 2 * pair + half
                high, low = split(part_ref[o, :, x].reshape(side, nz))
                phigh_ref[o, x] = high
                plow_ref[o, x] = low
                for group, value in zip(ins, (high, low, high_ref[o, x], low_ref[o, x])):
                    group.append(value)
            high, low, bhigh, blow = (jnp.concatenate(group, 1) for group in ins)
            total_ref[...] += dot(
                jnp.concatenate([bhigh, high, blow, low], 0),
                jnp.concatenate([high, low], 0),
                ((1,), (1,)),
            )
        return carry

    lax.fori_loop(0, nx // 2, products, 0)

    sums = kept_sums(total_ref[: 3 * side] + total_ref[3 * side :])
    spots = (iota((LANES, LANES), 0) // ny) % width
    sums = gathered(sums, jnp.where(iota((LANES, LANES), 1) % width == spots, 1.0, 0.0))
    lanes = iota((width, LANES), 1)
    place = (lanes % (LANES // 2)) // width
    packed = metric_ref[...]
    for i in range(3):
        packed = jnp.where(place == i, sums[i * width : (i + 1) * width], packed)
    half = width // 2
    folded = jnp.where(lanes[:half] < LANES // 2, packed[:half], packed[half:])
    sums_ref[...] = jnp.broadcast_to(folded[None], sums_ref.shape)


def column(value, spot):
    return jnp.broadcast_to(value[:, spot : spot + 1], value.shape)


def line(value, spot):
    return jnp.broadcast_to(value[spot : spot + 1, :], value.shape)


def added(terms):
    while len(terms) > 1:
        terms = [sum(terms[i : i + 2][1:], terms[i]) for i in range(0, len(terms), 2)]
    return terms[0]


def final_kernel(
    count, sums_ref, high_ref, low_ref, phigh_ref, plow_ref, next_ref, alpha_ref, beta_ref, out_ref, sems
):
    orbs, nx, side, nz = phigh_ref.shape
    width = side // ROWS
    shape = (width, LANES)
    rows, lanes = iota(shape, 0), iota(shape, 1)
    folded = jnp.sum(sums_ref[...], axis=0) / count
    sums = jnp.concatenate([folded, pltpu.roll(folded, LANES // 2, 1)], 0)

    def moved(start, length):
        value = sums if start == 0 else pltpu.roll(sums, LANES - start, 1)
        return jnp.where(lanes < length, value, 0.0)

    first = [moved(0, width), moved(width, width)]
    norms = moved(2 * width, width)
    metric = [moved(3 * width, 2 * width), moved(5 * width, 2 * width)]
    alpha_ref[...] = first[1][:, :width]
    ones = [jnp.where(lanes == rows + i * width, 1.0, 0.0) for i in range(2)]
    lack = [one - value for one, value in zip(ones, metric)]
    lack_columns = [[column(value, k) for k in range(2 * width)] for value in lack]

    def lacking(pair):
        lines = [line(value, k) for value in pair for k in range(width)]
        return [added([a * b for a, b in zip(columns, lines)]) for columns in lack_columns]

    one = lacking(first)
    two = lacking(one)
    three = lacking(two)
    weighed = [added(list(terms)) for terms in zip(first, one, two, three)]
    turned = jnp.concatenate(first, 0).T[:width]
    turned_columns = [
        jnp.broadcast_to(turned[:, k : k + 1], shape) for k in range(2 * width)
    ]
    weighed_lines = [line(value, k) for value in weighed for k in range(width)]
    gram = norms - added([a * b for a, b in zip(turned_columns, weighed_lines)])
    twice = [a + b for a, b in zip(ones, lack)]
    twice_lines = [line(value, k) for value in twice for k in range(width)]
    coeffs = added([a * b for a, b in zip(turned_columns, twice_lines)])
    table = gram + jnp.where(lanes == rows + width, 1.0, 0.0) - pltpu.roll(coeffs, 2 * width, 1)

    entry = {}
    for k in range(width):
        spread = column(gram, k)
        for j in range(k, width):
            entry[j, k] = line(spread, j)
    lines = [line(table, k) for k in range(width)]
    for k in range(width):
        inverse = 1.0 / entry[k, k]
        for j in range(k + 1, width):
            ratio = entry[j, k] * inverse
            for i in range(k + 1, j + 1):
                entry[j, i] = entry[j, i] - ratio * entry[i, k]
            lines[j] = lines[j] - ratio * lines[k]
    lines = [value * lax.rsqrt(entry[k, k]) for k, value in enumerate(lines)]
    upper = jnp.zeros(shape, F32)
    for k in range(width):
        upper = jnp.where((rows == k) & (lanes >= k), lines[k], upper)
    beta_ref[...] = upper[:, :width]

    same = rows == lanes % ROWS
    spots = [2 * width + lanes // ROWS, width + (lanes // ROWS) % width]
    grown = [
        jnp.concatenate(
            [jnp.where(same, jnp.take_along_axis(value, spot, axis=1), 0.0) for value in lines], 0
        )
        for spot in spots
    ]
    mixed_high, mixed_low = split(jnp.concatenate([grown[0], grown[1][:, :side]], 1))
    mixed = jnp.concatenate([mixed_high, mixed_low], 0)
    dims = ((1,), (0,))
    stores = []
    for o in range(orbs):

        def combine(pair, carry):
            highs, lows = [], []
            for half in range(2):
                x = 2 * pair + half
                highs.append(jnp.concatenate([high_ref[o, x], phigh_ref[o, x]], 0))
                lows.append(jnp.concatenate([low_ref[o, x], plow_ref[o, x]], 0))
            both = dot(mixed, jnp.concatenate(highs, 1), dims)
            out = both[:side] + both[side:] + dot(mixed_high, jnp.concatenate(lows, 1), dims)
            for half in range(2):
                x = 2 * pair + half
                out_ref[o, :, x] = out[:, half * nz : (half + 1) * nz].reshape(width, ROWS, nz)
            return carry

        lax.fori_loop(0, nx // 2, combine, 0)
        stores.append(pltpu.make_async_copy(out_ref.at[o], next_ref.at[o], sems.at[o]))
        stores[-1].start()
    for store in stores:
        store.wait()


def shifted(value, axis, steps):
    count = lax.axis_size(axis)
    return lax.ppermute(value, axis, [(i, (i + steps) % count) for i in range(count)])


def per_device(prev_block, block, hop_seed, levels, hop_table, onsite_table):
    orbs, width, nx, ny, nz = block.shape
    devices = lax.axis_size("gx") * lax.axis_size("gy")
    count = orbs * nx * ny * nz * devices
    fields = orbs * width
    hops = jnp.transpose(hop_table, (0, 2, 3, 1))
    onsite = onsite_table.T
    table_rows = 3 * orbs * orbs + ROWS
    outside = pl.BlockSpec(memory_space=pltpu.HBM)

    def stay(value):
        return pltpu.with_memory_space_constraint(value, pltpu.HBM)

    params = pltpu.CompilerParams(**PARAMS)

    block_here, seed_here, levels_here, hops_here, onsite_here, xup, xdown, yup, ydown = pl.pallas_call(
        pack_kernel,
        in_specs=[outside] * 5,
        out_shape=[
            pltpu.VMEM(block.shape, F32),
            pltpu.VMEM(hop_seed.shape, jnp.int32),
            pltpu.VMEM(levels.shape, jnp.int32),
            pltpu.VMEM(hops.shape, F32),
            pltpu.VMEM(onsite.shape, F32),
            pltpu.VMEM((fields + 1, ny, nz), F32),
            pltpu.VMEM((fields, ny, nz), F32),
            pltpu.VMEM((fields + 1, nx, nz), F32),
            pltpu.VMEM((fields, nx, nz), F32),
        ],
        scratch_shapes=[pltpu.SemaphoreType.DMA((orbs + 4,))],
        compiler_params=params,
        name="pack",
    )(stay(block), stay(hop_seed), stay(levels), stay(hops), stay(onsite))
    xlow = shifted(xup, "gx", 1)
    ylow = shifted(yup, "gy", 1)
    xhigh = shifted(xdown, "gx", -1)
    yhigh = shifted(ydown, "gy", -1)

    side = width * ny
    part, high, low, metric, table = pl.pallas_call(
        interior_kernel,
        out_shape=[
            pltpu.VMEM(block.shape, F32),
            pltpu.VMEM((orbs, nx, 2 * side, nz), BF16),
            pltpu.VMEM((orbs, nx, 2 * side, nz), BF16),
            pltpu.VMEM((width, LANES), F32),
            pltpu.VMEM((table_rows, LANES), F32),
        ],
        scratch_shapes=[pltpu.VMEM((2 * side, 4 * side), F32)],
        compiler_params=params,
        cost_estimate=pl.CostEstimate(flops=10**8, bytes_accessed=4 * 10**6, transcendentals=0),
        name="interior",
    )(prev_block, block_here, seed_here, levels_here, hops_here, onsite_here)

    phigh, plow, sums, _ = pl.pallas_call(
        halo_kernel,
        out_shape=[
            pltpu.VMEM((orbs, nx, side, nz), BF16),
            pltpu.VMEM((orbs, nx, side, nz), BF16),
            pltpu.VMEM((devices, width // 2, LANES), F32),
            pltpu.VMEM(block.shape, F32),
        ],
        input_output_aliases={0: 3},
        scratch_shapes=[pltpu.VMEM((6 * side, 2 * side), F32)],
        compiler_params=params,
        name="halo",
    )(part, seed_here, table, xlow, xhigh, ylow, yhigh, high, low, metric)

    sums = lax.all_to_all(sums, ("gx", "gy"), 0, 0)

    next_block, alpha, beta = pl.pallas_call(
        lambda *refs: final_kernel(count, *refs),
        out_shape=[
            jax.ShapeDtypeStruct(block.shape, F32),
            jax.ShapeDtypeStruct((width, width), F32),
            jax.ShapeDtypeStruct((width, width), F32),
        ],
        out_specs=[outside, pl.BlockSpec(memory_space=pltpu.VMEM), pl.BlockSpec(memory_space=pltpu.VMEM)],
        scratch_shapes=[pltpu.VMEM(block.shape, F32), pltpu.SemaphoreType.DMA((orbs,))],
        compiler_params=params,
        name="final",
    )(sums, high, low, phigh, plow)
    return next_block, alpha, beta


def solution(mesh):
    in_specs = (
        P(None, None, "gx", "gy", None),
        P(None, None, "gx", "gy", None),
        P(None, "gx", "gy", None),
        P("gx", "gy", None),
        P(),
        P(),
    )
    out_specs = (P(None, None, "gx", "gy", None), P(), P())
    return jax.shard_map(
        per_device, mesh=mesh, in_specs=in_specs, out_specs=out_specs, check_vma=False
    )
```

```python
import jax
import jax.numpy as jnp
from jax import lax
from jax.experimental import pallas as pl
from jax.experimental.pallas import tpu as pltpu
from jax.sharding import PartitionSpec as P

HIGH = lax.Precision.HIGHEST
F32 = jnp.float32
BF16 = jnp.bfloat16
LANES = 128
ROWS = 8
PARAMS = dict(vmem_limit_bytes=32 * 1024 * 1024)


def split(value):
    high = value.astype(BF16)
    low = (value - high.astype(F32)).astype(BF16)
    return high, low


def iota(shape, dim):
    return lax.broadcasted_iota(jnp.int32, shape, dim)


def dot(left, right, dims, precision=None):
    return lax.dot_general(
        left, right, (dims, ((), ())), precision=precision, preferred_element_type=F32
    )


def pick(table_ref, row, index):
    entries = jnp.broadcast_to(table_ref[row : row + 1, :], index.shape)
    return jnp.take_along_axis(entries, index, axis=1)


def bonds_of(table_ref, direction, index, orbs):
    base = direction * orbs * orbs
    return [
        [pick(table_ref, base + a * orbs + b, index) for b in range(orbs)] for a in range(orbs)
    ]


def fill_table(table_ref, hop_ref, onsite_ref):
    orbs, kinds = hop_ref.shape[1], hop_ref.shape[3]
    for d in range(3):
        for a in range(orbs):
            base = (d * orbs + a) * orbs
            table_ref[base : base + orbs, :kinds] = hop_ref[d, a]
    base = 3 * orbs * orbs
    table_ref[base : base + orbs, : onsite_ref.shape[1]] = onsite_ref[...]


def times(bonds, field):
    return [sum(bonds[a][b] * field[b] for b in range(len(field))) for a in range(len(field))]


def times_transposed(bonds, field):
    return [sum(bonds[a][b] * field[a] for a in range(len(field))) for b in range(len(field))]


def pack_kernel(
    block_in,
    seed_in,
    level_in,
    hop_in,
    onsite_in,
    block_ref,
    seed_ref,
    level_ref,
    hop_ref,
    onsite_ref,
    xup_ref,
    xdown_ref,
    yup_ref,
    ydown_ref,
    sems,
):
    orbs, width, nx, ny, _ = block_ref.shape
    pairs = [(block_in.at[o], block_ref.at[o]) for o in range(orbs)]
    pairs += [(seed_in, seed_ref), (level_in, level_ref), (hop_in, hop_ref), (onsite_in, onsite_ref)]
    loads = [pltpu.make_async_copy(*pair, sems.at[i]) for i, pair in enumerate(pairs)]
    for load in loads:
        load.start()
    for o in range(orbs):
        loads[o].wait()
        for n in range(width):
            spot = o * width + n
            xup_ref[spot] = block_ref[o, n, nx - 1]
            xdown_ref[spot] = block_ref[o, n, 0]
            yup_ref[spot] = block_ref[o, n, :, ny - 1, :]
            ydown_ref[spot] = block_ref[o, n, :, 0, :]
    loads[orbs].wait()
    xup_ref[orbs * width] = seed_ref[0, nx - 1].astype(F32)
    yup_ref[orbs * width] = seed_ref[1, :, ny - 1, :].astype(F32)
    for load in loads[orbs + 1 :]:
        load.wait()


def kept_sums(total):
    rows, columns = total.shape
    same = (iota((rows, columns), 0) % ROWS) == (iota((rows, columns), 1) % ROWS)
    kept = jnp.where(same, total, 0.0)
    return kept.reshape(rows // ROWS, ROWS, columns).sum(axis=1)


def gathered(value, spots):
    high, low = split(value)
    last = (value - high.astype(F32) - low.astype(F32)).astype(BF16)
    pieces = dot(jnp.concatenate([high, low, last], 0), spots.astype(BF16), ((1,), (0,)))
    rows = value.shape[0]
    return pieces[:rows] + pieces[rows : 2 * rows] + pieces[2 * rows :]


def interior_kernel(
    prev_ref,
    block_ref,
    seed_ref,
    level_ref,
    hop_ref,
    onsite_ref,
    part_ref,
    high_ref,
    low_ref,
    metric_ref,
    table_ref,
    gram_ref,
):
    orbs, width, nx, ny, nz = block_ref.shape
    fill_table(table_ref, hop_ref, onsite_ref)
    row = iota((ny, nz), 0)
    side = width * ny

    def stencil(x, carry):
        before = jnp.maximum(x - 1, 0)
        inside = jnp.where(x > 0, 1.0, 0.0)
        energy = [pick(table_ref, 3 * orbs * orbs + o, level_ref[x]) for o in range(orbs)]
        bond_x = bonds_of(table_ref, 0, seed_ref[0, before], orbs)
        bond_x = [[inside * value for value in line] for line in bond_x]
        bond_y = bonds_of(table_ref, 1, seed_ref[1, x], orbs)
        bond_z = bonds_of(table_ref, 2, seed_ref[2, x], orbs)
        for n in range(width):
            here = [block_ref[o, n, x] for o in range(orbs)]
            behind = [block_ref[o, n, before] for o in range(orbs)]
            forward = times(bond_x, here)
            for o in range(orbs):
                part_ref[o, n, before] += forward[o]
            image = [energy[o] * here[o] for o in range(orbs)]
            image = [a + b for a, b in zip(image, times_transposed(bond_x, behind))]
            ahead = [jnp.where(row == ny - 1, 0.0, pltpu.roll(v, ny - 1, 0)) for v in here]
            image = [a + b for a, b in zip(image, times(bond_y, ahead))]
            carried = times_transposed(bond_y, here)
            image = [
                a + jnp.where(row == 0, 0.0, pltpu.roll(b, 1, 0)) for a, b in zip(image, carried)
            ]
            ahead = [pltpu.roll(v, nz - 1, 1) for v in here]
            image = [a + b for a, b in zip(image, times(bond_z, ahead))]
            carried = times_transposed(bond_z, here)
            image = [a + pltpu.roll(b, 1, 1) for a, b in zip(image, carried)]
            for o in range(orbs):
                part_ref[o, n, x] = image[o]
        return carry

    lax.fori_loop(0, nx, stencil, 0)
    gram_ref[...] = jnp.zeros(gram_ref.shape, F32)

    def products(pair):
        for o in range(orbs):
            highs, lows = [], []
            for half in range(2):
                x = 2 * pair + half
                basis = jnp.concatenate(
                    [prev_ref[o, :, x].reshape(side, nz), block_ref[o, :, x].reshape(side, nz)], 0
                )
                high, low = split(basis)
                high_ref[o, x] = high
                low_ref[o, x] = low
                highs.append(high)
                lows.append(low)
            high = jnp.concatenate(highs, 1)
            low = jnp.concatenate(lows, 1)
            gram_ref[...] += dot(high, jnp.concatenate([high, low], 0), ((1,), (1,)))

    for pair in range(nx // 2):
        products(pair)
    crossed = gram_ref[:, 2 * side :]
    sums = kept_sums(gram_ref[:, : 2 * side] + crossed + crossed.T)
    spots = iota((LANES, LANES), 0) // ny
    lanes = iota((LANES, LANES), 1) % (LANES // 2)
    maps = [jnp.where(lanes == width * (3 + 2 * i) + spots, 1.0, 0.0) for i in range(2)]
    parts = [sums[i * width : (i + 1) * width] for i in range(2)]
    metric_ref[...] = gathered(jnp.concatenate(parts, 1), jnp.concatenate(maps, 0))


def halo_kernel(
    part_in,
    seed_ref,
    table_ref,
    xlow_ref,
    xhigh_ref,
    ylow_ref,
    yhigh_ref,
    high_ref,
    low_ref,
    metric_ref,
    phigh_ref,
    plow_ref,
    sums_ref,
    part_ref,
    total_ref,
):
    orbs, width, nx, ny, nz = part_ref.shape
    side = width * ny
    last = orbs * width

    bond_x = bonds_of(table_ref, 0, seed_ref[0, nx - 1], orbs)
    bond_xlow = bonds_of(table_ref, 0, xlow_ref[last].astype(jnp.int32), orbs)
    for n in range(width):
        forward = times(bond_x, [xhigh_ref[o * width + n] for o in range(orbs)])
        back = times_transposed(bond_xlow, [xlow_ref[o * width + n] for o in range(orbs)])
        for o in range(orbs):
            part_ref[o, n, nx - 1] += forward[o]
            part_ref[o, n, 0] += back[o]
    bond_y = bonds_of(table_ref, 1, seed_ref[1, :, ny - 1, :], orbs)
    bond_ylow = bonds_of(table_ref, 1, ylow_ref[last].astype(jnp.int32), orbs)
    for n in range(width):
        forward = times(bond_y, [yhigh_ref[o * width + n] for o in range(orbs)])
        back = times_transposed(bond_ylow, [ylow_ref[o * width + n] for o in range(orbs)])
        for o in range(orbs):
            part_ref[o, n, :, ny - 1, :] += forward[o]
            part_ref[o, n, :, 0, :] += back[o]

    total_ref[...] = jnp.zeros(total_ref.shape, F32)

    def products(pair):
        for o in range(orbs):
            ins = [[], [], [], []]
            for half in range(2):
                x = 2 * pair + half
                high, low = split(part_ref[o, :, x].reshape(side, nz))
                phigh_ref[o, x] = high
                plow_ref[o, x] = low
                for group, value in zip(ins, (high, low, high_ref[o, x], low_ref[o, x])):
                    group.append(value)
            high, low, bhigh, blow = (jnp.concatenate(group, 1) for group in ins)
            total_ref[...] += dot(
                jnp.concatenate([bhigh, high, blow, low], 0),
                jnp.concatenate([high, low], 0),
                ((1,), (1,)),
            )

    for pair in range(nx // 2):
        products(pair)

    sums = kept_sums(total_ref[: 3 * side] + total_ref[3 * side :])
    spots = (iota((LANES, LANES), 0) // ny) % width
    sums = gathered(sums, jnp.where(iota((LANES, LANES), 1) % width == spots, 1.0, 0.0))
    lanes = iota((width, LANES), 1)
    place = (lanes % (LANES // 2)) // width
    packed = metric_ref[...]
    for i in range(3):
        packed = jnp.where(place == i, sums[i * width : (i + 1) * width], packed)
    half = width // 2
    folded = jnp.where(lanes[:half] < LANES // 2, packed[:half], packed[half:])
    sums_ref[...] = jnp.broadcast_to(folded[None], sums_ref.shape)


def column(value, spot):
    return jnp.broadcast_to(value[:, spot : spot + 1], value.shape)


def line(value, spot):
    return jnp.broadcast_to(value[spot : spot + 1, :], value.shape)


def added(terms):
    while len(terms) > 1:
        terms = [sum(terms[i : i + 2][1:], terms[i]) for i in range(0, len(terms), 2)]
    return terms[0]


def final_kernel(
    count,
    sums_ref,
    high_ref,
    low_ref,
    phigh_ref,
    plow_ref,
    next_ref,
    alpha_out,
    beta_out,
    out_ref,
    alpha_ref,
    beta_ref,
    sems,
):
    orbs, nx, side, nz = phigh_ref.shape
    width = side // ROWS
    shape = (width, LANES)
    rows, lanes = iota(shape, 0), iota(shape, 1)
    folded = jnp.sum(sums_ref[...], axis=0) / count
    sums = jnp.concatenate([folded, pltpu.roll(folded, LANES // 2, 1)], 0)

    def moved(start, length):
        value = sums if start == 0 else pltpu.roll(sums, LANES - start, 1)
        return jnp.where(lanes < length, value, 0.0)

    first = [moved(0, width), moved(width, width)]
    norms = moved(2 * width, width)
    metric = [moved(3 * width, 2 * width), moved(5 * width, 2 * width)]
    alpha_ref[...] = first[1][:, :width]
    stores = [pltpu.make_async_copy(alpha_ref, alpha_out, sems.at[orbs])]
    stores[-1].start()
    ones = [jnp.where(lanes == rows + i * width, 1.0, 0.0) for i in range(2)]
    lack = [one - value for one, value in zip(ones, metric)]
    lack_columns = [[column(value, k) for k in range(2 * width)] for value in lack]

    def lacking(pair):
        lines = [line(value, k) for value in pair for k in range(width)]
        return [added([a * b for a, b in zip(columns, lines)]) for columns in lack_columns]

    one = lacking(first)
    two = lacking(one)
    three = lacking(two)
    weighed = [added(list(terms)) for terms in zip(first, one, two, three)]
    turned = jnp.concatenate(first, 0).T[:width]
    turned_columns = [
        jnp.broadcast_to(turned[:, k : k + 1], shape) for k in range(2 * width)
    ]
    weighed_lines = [line(value, k) for value in weighed for k in range(width)]
    gram = norms - added([a * b for a, b in zip(turned_columns, weighed_lines)])
    twice = [a + b for a, b in zip(ones, lack)]
    twice_lines = [line(value, k) for value in twice for k in range(width)]
    coeffs = added([a * b for a, b in zip(turned_columns, twice_lines)])
    table = gram + jnp.where(lanes == rows + width, 1.0, 0.0) - pltpu.roll(coeffs, 2 * width, 1)

    entry = {}
    for k in range(width):
        spread = column(gram, k)
        for j in range(k, width):
            entry[j, k] = line(spread, j)
    lines = [line(table, k) for k in range(width)]
    for k in range(width):
        inverse = 1.0 / entry[k, k]
        for j in range(k + 1, width):
            ratio = entry[j, k] * inverse
            for i in range(k + 1, j + 1):
                entry[j, i] = entry[j, i] - ratio * entry[i, k]
            lines[j] = lines[j] - ratio * lines[k]
    lines = [value * lax.rsqrt(entry[k, k]) for k, value in enumerate(lines)]
    upper = jnp.zeros(shape, F32)
    for k in range(width):
        upper = jnp.where((rows == k) & (lanes >= k), lines[k], upper)
    beta_ref[...] = upper[:, :width]
    stores.append(pltpu.make_async_copy(beta_ref, beta_out, sems.at[orbs + 1]))
    stores[-1].start()

    same = rows == lanes % ROWS
    spots = [2 * width + lanes // ROWS, width + (lanes // ROWS) % width]
    grown = [
        jnp.concatenate(
            [jnp.where(same, jnp.take_along_axis(value, spot, axis=1), 0.0) for value in lines], 0
        )
        for spot in spots
    ]
    mixed_high, mixed_low = split(jnp.concatenate([grown[0], grown[1][:, :side]], 1))
    mixed = jnp.concatenate([mixed_high, mixed_low], 0)
    dims = ((1,), (0,))

    def chunk(o, pair):
        highs, lows = [], []
        for half in range(2):
            x = 2 * pair + half
            highs.append(jnp.concatenate([high_ref[o, x], phigh_ref[o, x]], 0))
            lows.append(jnp.concatenate([low_ref[o, x], plow_ref[o, x]], 0))
        both = dot(mixed, jnp.concatenate(highs, 1), dims)
        out = both[:side] + both[side:] + dot(mixed_high, jnp.concatenate(lows, 1), dims)
        for half in range(2):
            x = 2 * pair + half
            out_ref[o, :, x] = out[:, half * nz : (half + 1) * nz].reshape(width, ROWS, nz)

    for o in range(orbs):
        for pair in range(nx // 2):
            chunk(o, pair)
        stores.append(pltpu.make_async_copy(out_ref.at[o], next_ref.at[o], sems.at[o]))
        stores[-1].start()
    for store in stores:
        store.wait()


def shifted(value, axis, steps):
    count = lax.axis_size(axis)
    return lax.ppermute(value, axis, [(i, (i + steps) % count) for i in range(count)])


def per_device(prev_block, block, hop_seed, levels, hop_table, onsite_table):
    orbs, width, nx, ny, nz = block.shape
    devices = lax.axis_size("gx") * lax.axis_size("gy")
    count = orbs * nx * ny * nz * devices
    fields = orbs * width
    hops = jnp.transpose(hop_table, (0, 2, 3, 1))
    onsite = onsite_table.T
    table_rows = 3 * orbs * orbs + ROWS
    outside = pl.BlockSpec(memory_space=pltpu.HBM)

    def stay(value):
        return pltpu.with_memory_space_constraint(value, pltpu.HBM)

    params = pltpu.CompilerParams(**PARAMS)

    block_here, seed_here, levels_here, hops_here, onsite_here, xup, xdown, yup, ydown = pl.pallas_call(
        pack_kernel,
        in_specs=[outside] * 5,
        out_shape=[
            pltpu.VMEM(block.shape, F32),
            pltpu.VMEM(hop_seed.shape, jnp.int32),
            pltpu.VMEM(levels.shape, jnp.int32),
            pltpu.VMEM(hops.shape, F32),
            pltpu.VMEM(onsite.shape, F32),
            pltpu.VMEM((fields + 1, ny, nz), F32),
            pltpu.VMEM((fields, ny, nz), F32),
            pltpu.VMEM((fields + 1, nx, nz), F32),
            pltpu.VMEM((fields, nx, nz), F32),
        ],
        scratch_shapes=[pltpu.SemaphoreType.DMA((orbs + 4,))],
        compiler_params=params,
        name="pack",
    )(stay(block), stay(hop_seed), stay(levels), stay(hops), stay(onsite))
    xlow = shifted(xup, "gx", 1)
    ylow = shifted(yup, "gy", 1)
    xhigh = shifted(xdown, "gx", -1)
    yhigh = shifted(ydown, "gy", -1)

    side = width * ny
    part, high, low, metric, table = pl.pallas_call(
        interior_kernel,
        out_shape=[
            pltpu.VMEM(block.shape, F32),
            pltpu.VMEM((orbs, nx, 2 * side, nz), BF16),
            pltpu.VMEM((orbs, nx, 2 * side, nz), BF16),
            pltpu.VMEM((width, LANES), F32),
            pltpu.VMEM((table_rows, LANES), F32),
        ],
        scratch_shapes=[pltpu.VMEM((2 * side, 4 * side), F32)],
        compiler_params=params,
        cost_estimate=pl.CostEstimate(flops=10**8, bytes_accessed=4 * 10**6, transcendentals=0),
        name="interior",
    )(prev_block, block_here, seed_here, levels_here, hops_here, onsite_here)

    phigh, plow, sums, _ = pl.pallas_call(
        halo_kernel,
        out_shape=[
            pltpu.VMEM((orbs, nx, side, nz), BF16),
            pltpu.VMEM((orbs, nx, side, nz), BF16),
            pltpu.VMEM((devices, width // 2, LANES), F32),
            pltpu.VMEM(block.shape, F32),
        ],
        input_output_aliases={0: 3},
        scratch_shapes=[pltpu.VMEM((6 * side, 2 * side), F32)],
        compiler_params=params,
        name="halo",
    )(part, seed_here, table, xlow, xhigh, ylow, yhigh, high, low, metric)

    sums = lax.all_to_all(sums, ("gx", "gy"), 0, 0)

    next_block, alpha, beta = pl.pallas_call(
        lambda *refs: final_kernel(count, *refs),
        out_shape=[
            jax.ShapeDtypeStruct(block.shape, F32),
            jax.ShapeDtypeStruct((width, width), F32),
            jax.ShapeDtypeStruct((width, width), F32),
        ],
        out_specs=[outside] * 3,
        scratch_shapes=[
            pltpu.VMEM(block.shape, F32),
            pltpu.VMEM((width, width), F32),
            pltpu.VMEM((width, width), F32),
            pltpu.SemaphoreType.DMA((orbs + 2,)),
        ],
        compiler_params=params,
        name="final",
    )(sums, high, low, phigh, plow)
    return next_block, alpha, beta


def solution(mesh):
    in_specs = (
        P(None, None, "gx", "gy", None),
        P(None, None, "gx", "gy", None),
        P(None, "gx", "gy", None),
        P("gx", "gy", None),
        P(),
        P(),
    )
    out_specs = (P(None, None, "gx", "gy", None), P(), P())
    return jax.shard_map(
        per_device, mesh=mesh, in_specs=in_specs, out_specs=out_specs, check_vma=False
    )
```

```python
import jax
import jax.numpy as jnp
from jax import lax
from jax.experimental import pallas as pl
from jax.experimental.pallas import tpu as pltpu
from jax.sharding import PartitionSpec as P

HIGH = lax.Precision.HIGHEST
F32 = jnp.float32
BF16 = jnp.bfloat16
LANES = 128
ROWS = 8
PARAMS = dict(vmem_limit_bytes=32 * 1024 * 1024)


def split(value):
    high = value.astype(BF16)
    low = (value - high.astype(F32)).astype(BF16)
    return high, low


def iota(shape, dim):
    return lax.broadcasted_iota(jnp.int32, shape, dim)


def dot(left, right, dims, precision=None):
    return lax.dot_general(
        left, right, (dims, ((), ())), precision=precision, preferred_element_type=F32
    )


def pick(table_ref, row, index):
    entries = jnp.broadcast_to(table_ref[row : row + 1, :], index.shape)
    return jnp.take_along_axis(entries, index, axis=1)


def bonds_of(table_ref, direction, index, orbs):
    base = direction * orbs * orbs
    return [
        [pick(table_ref, base + a * orbs + b, index) for b in range(orbs)] for a in range(orbs)
    ]


def fill_table(table_ref, hop_ref, onsite_ref):
    orbs, kinds = hop_ref.shape[1], hop_ref.shape[3]
    for d in range(3):
        for a in range(orbs):
            base = (d * orbs + a) * orbs
            table_ref[base : base + orbs, :kinds] = hop_ref[d, a]
    base = 3 * orbs * orbs
    table_ref[base : base + orbs, : onsite_ref.shape[1]] = onsite_ref[...]


def times(bonds, field):
    return [sum(bonds[a][b] * field[b] for b in range(len(field))) for a in range(len(field))]


def times_transposed(bonds, field):
    return [sum(bonds[a][b] * field[a] for a in range(len(field))) for b in range(len(field))]


def pack_kernel(
    block_in,
    seed_in,
    level_in,
    hop_in,
    onsite_in,
    block_ref,
    seed_ref,
    level_ref,
    hop_ref,
    onsite_ref,
    xnear_ref,
    yfar_ref,
    ynear_ref,
    xfar_ref,
    sems,
):
    orbs, width, nx, ny, _ = block_ref.shape
    yeven = lax.axis_index("gy") % 2 == 0
    near = nx - 1
    pairs = [(block_in.at[o], block_ref.at[o]) for o in range(orbs)]
    pairs += [(seed_in, seed_ref), (level_in, level_ref), (hop_in, hop_ref), (onsite_in, onsite_ref)]
    loads = [pltpu.make_async_copy(*pair, sems.at[i]) for i, pair in enumerate(pairs)]
    for load in loads:
        load.start()
    for o in range(orbs):
        loads[o].wait()
        for n in range(width):
            spot = o * width + n
            xnear_ref[spot] = block_ref[o, n, near]
            xfar_ref[spot] = block_ref[o, n, nx - 1 - near]
            top, bottom = block_ref[o, n, :, ny - 1, :], block_ref[o, n, :, 0, :]
            ynear_ref[spot] = jnp.where(yeven, top, bottom)
            yfar_ref[spot] = jnp.where(yeven, bottom, top)
    loads[orbs].wait()
    for ref in (xnear_ref, xfar_ref):
        ref[orbs * width] = seed_ref[0, nx - 1].astype(F32)
    for ref in (ynear_ref, yfar_ref):
        ref[orbs * width] = seed_ref[1, :, ny - 1, :].astype(F32)
    for load in loads[orbs + 1 :]:
        load.wait()


def kept_sums(total):
    rows, columns = total.shape
    same = (iota((rows, columns), 0) % ROWS) == (iota((rows, columns), 1) % ROWS)
    kept = jnp.where(same, total, 0.0)
    return kept.reshape(rows // ROWS, ROWS, columns).sum(axis=1)


def gathered(value, spots):
    high, low = split(value)
    last = (value - high.astype(F32) - low.astype(F32)).astype(BF16)
    pieces = dot(jnp.concatenate([high, low, last], 0), spots.astype(BF16), ((1,), (0,)))
    rows = value.shape[0]
    return pieces[:rows] + pieces[rows : 2 * rows] + pieces[2 * rows :]


def interior_kernel(
    prev_ref,
    block_ref,
    seed_ref,
    level_ref,
    hop_ref,
    onsite_ref,
    part_ref,
    high_ref,
    low_ref,
    metric_ref,
    table_ref,
    gram_ref,
):
    orbs, width, nx, ny, nz = block_ref.shape
    fill_table(table_ref, hop_ref, onsite_ref)
    row = iota((ny, nz), 0)
    side = width * ny

    def stencil(x, carry):
        before = jnp.maximum(x - 1, 0)
        inside = jnp.where(x > 0, 1.0, 0.0)
        energy = [pick(table_ref, 3 * orbs * orbs + o, level_ref[x]) for o in range(orbs)]
        bond_x = bonds_of(table_ref, 0, seed_ref[0, before], orbs)
        bond_x = [[inside * value for value in line] for line in bond_x]
        bond_y = bonds_of(table_ref, 1, seed_ref[1, x], orbs)
        bond_z = bonds_of(table_ref, 2, seed_ref[2, x], orbs)
        for n in range(width):
            here = [block_ref[o, n, x] for o in range(orbs)]
            behind = [block_ref[o, n, before] for o in range(orbs)]
            forward = times(bond_x, here)
            for o in range(orbs):
                part_ref[o, n, before] += forward[o]
            image = [energy[o] * here[o] for o in range(orbs)]
            image = [a + b for a, b in zip(image, times_transposed(bond_x, behind))]
            ahead = [jnp.where(row == ny - 1, 0.0, pltpu.roll(v, ny - 1, 0)) for v in here]
            image = [a + b for a, b in zip(image, times(bond_y, ahead))]
            carried = times_transposed(bond_y, here)
            image = [
                a + jnp.where(row == 0, 0.0, pltpu.roll(b, 1, 0)) for a, b in zip(image, carried)
            ]
            ahead = [pltpu.roll(v, nz - 1, 1) for v in here]
            image = [a + b for a, b in zip(image, times(bond_z, ahead))]
            carried = times_transposed(bond_z, here)
            image = [a + pltpu.roll(b, 1, 1) for a, b in zip(image, carried)]
            for o in range(orbs):
                part_ref[o, n, x] = image[o]
        return carry

    lax.fori_loop(0, nx, stencil, 0)
    gram_ref[...] = jnp.zeros(gram_ref.shape, F32)

    def products(pair):
        for o in range(orbs):
            highs, lows = [], []
            for half in range(2):
                x = 2 * pair + half
                basis = jnp.concatenate(
                    [prev_ref[o, :, x].reshape(side, nz), block_ref[o, :, x].reshape(side, nz)], 0
                )
                high, low = split(basis)
                high_ref[o, x] = high
                low_ref[o, x] = low
                highs.append(high)
                lows.append(low)
            high = jnp.concatenate(highs, 1)
            low = jnp.concatenate(lows, 1)
            gram_ref[...] += dot(high, jnp.concatenate([high, low], 0), ((1,), (1,)))

    for pair in range(nx // 2):
        products(pair)
    crossed = gram_ref[:, 2 * side :]
    sums = kept_sums(gram_ref[:, : 2 * side] + crossed + crossed.T)
    spots = iota((LANES, LANES), 0) // ny
    lanes = iota((LANES, LANES), 1) % (LANES // 2)
    maps = [jnp.where(lanes == width * (3 + 2 * i) + spots, 1.0, 0.0) for i in range(2)]
    parts = [sums[i * width : (i + 1) * width] for i in range(2)]
    metric_ref[...] = gathered(jnp.concatenate(parts, 1), jnp.concatenate(maps, 0))


def halo_kernel(
    part_in,
    seed_ref,
    table_ref,
    xnear_ref,
    yfar_ref,
    ynear_ref,
    xfar_ref,
    high_ref,
    low_ref,
    metric_ref,
    phigh_ref,
    plow_ref,
    sums_ref,
    part_ref,
    total_ref,
):
    orbs, width, nx, ny, nz = part_ref.shape
    side = width * ny
    last = orbs * width

    def add_x(low_ref, high_ref):
        bond = bonds_of(table_ref, 0, seed_ref[0, nx - 1], orbs)
        bond_low = bonds_of(table_ref, 0, low_ref[last].astype(jnp.int32), orbs)
        for n in range(width):
            forward = times(bond, [high_ref[o * width + n] for o in range(orbs)])
            back = times_transposed(bond_low, [low_ref[o * width + n] for o in range(orbs)])
            for o in range(orbs):
                part_ref[o, n, nx - 1] += forward[o]
                part_ref[o, n, 0] += back[o]

    def add_y(low_ref, high_ref):
        bond = bonds_of(table_ref, 1, seed_ref[1, :, ny - 1, :], orbs)
        bond_low = bonds_of(table_ref, 1, low_ref[last].astype(jnp.int32), orbs)
        for n in range(width):
            forward = times(bond, [high_ref[o * width + n] for o in range(orbs)])
            back = times_transposed(bond_low, [low_ref[o * width + n] for o in range(orbs)])
            for o in range(orbs):
                part_ref[o, n, :, ny - 1, :] += forward[o]
                part_ref[o, n, :, 0, :] += back[o]

    yeven = lax.axis_index("gy") % 2 == 0
    add_x(xnear_ref, xfar_ref)
    pl.when(yeven)(lambda: add_y(yfar_ref, ynear_ref))
    pl.when(jnp.logical_not(yeven))(lambda: add_y(ynear_ref, yfar_ref))

    total_ref[...] = jnp.zeros(total_ref.shape, F32)

    def products(pair):
        for o in range(orbs):
            ins = [[], [], [], []]
            for half in range(2):
                x = 2 * pair + half
                high, low = split(part_ref[o, :, x].reshape(side, nz))
                phigh_ref[o, x] = high
                plow_ref[o, x] = low
                for group, value in zip(ins, (high, low, high_ref[o, x], low_ref[o, x])):
                    group.append(value)
            high, low, bhigh, blow = (jnp.concatenate(group, 1) for group in ins)
            total_ref[...] += dot(
                jnp.concatenate([bhigh, high, blow, low], 0),
                jnp.concatenate([high, low], 0),
                ((1,), (1,)),
            )

    for pair in range(nx // 2):
        products(pair)

    sums = kept_sums(total_ref[: 3 * side] + total_ref[3 * side :])
    spots = (iota((LANES, LANES), 0) // ny) % width
    sums = gathered(sums, jnp.where(iota((LANES, LANES), 1) % width == spots, 1.0, 0.0))
    lanes = iota((width, LANES), 1)
    place = (lanes % (LANES // 2)) // width
    packed = metric_ref[...]
    for i in range(3):
        packed = jnp.where(place == i, sums[i * width : (i + 1) * width], packed)
    half = width // 2
    folded = jnp.where(lanes[:half] < LANES // 2, packed[:half], packed[half:])
    sums_ref[...] = jnp.broadcast_to(folded[None], sums_ref.shape)


def column(value, spot):
    return jnp.broadcast_to(value[:, spot : spot + 1], value.shape)


def line(value, spot):
    return jnp.broadcast_to(value[spot : spot + 1, :], value.shape)


def added(terms):
    while len(terms) > 1:
        terms = [sum(terms[i : i + 2][1:], terms[i]) for i in range(0, len(terms), 2)]
    return terms[0]


def final_kernel(
    count,
    sums_ref,
    high_ref,
    low_ref,
    phigh_ref,
    plow_ref,
    next_ref,
    alpha_out,
    beta_out,
    out_ref,
    alpha_ref,
    beta_ref,
    sems,
):
    orbs, nx, side, nz = phigh_ref.shape
    width = side // ROWS
    shape = (width, LANES)
    rows, lanes = iota(shape, 0), iota(shape, 1)
    folded = jnp.sum(sums_ref[...], axis=0) / count
    sums = jnp.concatenate([folded, pltpu.roll(folded, LANES // 2, 1)], 0)

    def moved(start, length):
        value = sums if start == 0 else pltpu.roll(sums, LANES - start, 1)
        return jnp.where(lanes < length, value, 0.0)

    first = [moved(0, width), moved(width, width)]
    norms = moved(2 * width, width)
    metric = [moved(3 * width, 2 * width), moved(5 * width, 2 * width)]
    alpha_ref[...] = first[1][:, :width]
    stores = [pltpu.make_async_copy(alpha_ref, alpha_out, sems.at[orbs])]
    stores[-1].start()
    ones = [jnp.where(lanes == rows + i * width, 1.0, 0.0) for i in range(2)]
    lack = [one - value for one, value in zip(ones, metric)]
    lack_columns = [[column(value, k) for k in range(2 * width)] for value in lack]

    def lacking(pair):
        lines = [line(value, k) for value in pair for k in range(width)]
        return [added([a * b for a, b in zip(columns, lines)]) for columns in lack_columns]

    one = lacking(first)
    two = lacking(one)
    three = lacking(two)
    weighed = [added(list(terms)) for terms in zip(first, one, two, three)]
    turned = jnp.concatenate(first, 0).T[:width]
    turned_columns = [
        jnp.broadcast_to(turned[:, k : k + 1], shape) for k in range(2 * width)
    ]
    weighed_lines = [line(value, k) for value in weighed for k in range(width)]
    gram = norms - added([a * b for a, b in zip(turned_columns, weighed_lines)])
    twice = [a + b for a, b in zip(ones, lack)]
    twice_lines = [line(value, k) for value in twice for k in range(width)]
    coeffs = added([a * b for a, b in zip(turned_columns, twice_lines)])
    table = gram + jnp.where(lanes == rows + width, 1.0, 0.0) - pltpu.roll(coeffs, 2 * width, 1)

    entry = {}
    for k in range(width):
        spread = column(gram, k)
        for j in range(k, width):
            entry[j, k] = line(spread, j)
    lines = [line(table, k) for k in range(width)]
    for k in range(width):
        inverse = 1.0 / entry[k, k]
        for j in range(k + 1, width):
            ratio = entry[j, k] * inverse
            for i in range(k + 1, j + 1):
                entry[j, i] = entry[j, i] - ratio * entry[i, k]
            lines[j] = lines[j] - ratio * lines[k]
    lines = [value * lax.rsqrt(entry[k, k]) for k, value in enumerate(lines)]
    upper = jnp.zeros(shape, F32)
    for k in range(width):
        upper = jnp.where((rows == k) & (lanes >= k), lines[k], upper)
    beta_ref[...] = upper[:, :width]
    stores.append(pltpu.make_async_copy(beta_ref, beta_out, sems.at[orbs + 1]))
    stores[-1].start()

    same = rows == lanes % ROWS
    spots = [2 * width + lanes // ROWS, width + (lanes // ROWS) % width]
    grown = [
        jnp.concatenate(
            [jnp.where(same, jnp.take_along_axis(value, spot, axis=1), 0.0) for value in lines], 0
        )
        for spot in spots
    ]
    mixed_high, mixed_low = split(jnp.concatenate([grown[0], grown[1][:, :side]], 1))
    mixed = jnp.concatenate([mixed_high, mixed_low], 0)
    dims = ((1,), (0,))

    def chunk(o, pair):
        highs, lows = [], []
        for half in range(2):
            x = 2 * pair + half
            highs.append(jnp.concatenate([high_ref[o, x], phigh_ref[o, x]], 0))
            lows.append(jnp.concatenate([low_ref[o, x], plow_ref[o, x]], 0))
        both = dot(mixed, jnp.concatenate(highs, 1), dims)
        out = both[:side] + both[side:] + dot(mixed_high, jnp.concatenate(lows, 1), dims)
        for half in range(2):
            x = 2 * pair + half
            out_ref[o, :, x] = out[:, half * nz : (half + 1) * nz].reshape(width, ROWS, nz)

    for o in range(orbs):
        for pair in range(nx // 2):
            chunk(o, pair)
        stores.append(pltpu.make_async_copy(out_ref.at[o], next_ref.at[o], sems.at[o]))
        stores[-1].start()
    for store in stores:
        store.wait()


def shifted(value, axis, steps):
    count = lax.axis_size(axis)
    return lax.ppermute(value, axis, [(i, (i + steps) % count) for i in range(count)])


def swapped(value, axis, far):
    count = lax.axis_size(axis)
    return lax.ppermute(
        value, axis, [(i, (i + (1 if i % 2 == far else -1)) % count) for i in range(count)]
    )


def per_device(prev_block, block, hop_seed, levels, hop_table, onsite_table):
    orbs, width, nx, ny, nz = block.shape
    devices = lax.axis_size("gx") * lax.axis_size("gy")
    count = orbs * nx * ny * nz * devices
    fields = orbs * width
    hops = jnp.transpose(hop_table, (0, 2, 3, 1))
    onsite = onsite_table.T
    table_rows = 3 * orbs * orbs + ROWS
    outside = pl.BlockSpec(memory_space=pltpu.HBM)

    def stay(value):
        return pltpu.with_memory_space_constraint(value, pltpu.HBM)

    params = pltpu.CompilerParams(**PARAMS)

    block_here, seed_here, levels_here, hops_here, onsite_here, xnear, yfar, ynear, xfar = pl.pallas_call(
        pack_kernel,
        in_specs=[outside] * 5,
        out_shape=[
            pltpu.VMEM(block.shape, F32),
            pltpu.VMEM(hop_seed.shape, jnp.int32),
            pltpu.VMEM(levels.shape, jnp.int32),
            pltpu.VMEM(hops.shape, F32),
            pltpu.VMEM(onsite.shape, F32),
            pltpu.VMEM((fields + 1, ny, nz), F32),
            pltpu.VMEM((fields + 1, nx, nz), F32),
            pltpu.VMEM((fields + 1, nx, nz), F32),
            pltpu.VMEM((fields + 1, ny, nz), F32),
        ],
        scratch_shapes=[pltpu.SemaphoreType.DMA((orbs + 4,))],
        compiler_params=params,
        name="pack",
    )(stay(block), stay(hop_seed), stay(levels), stay(hops), stay(onsite))
    xnear = shifted(xnear, "gx", 1)
    yfar = swapped(yfar, "gy", 1)
    ynear = swapped(ynear, "gy", 0)
    xfar = shifted(xfar, "gx", -1)

    side = width * ny
    part, high, low, metric, table = pl.pallas_call(
        interior_kernel,
        out_shape=[
            pltpu.VMEM(block.shape, F32),
            pltpu.VMEM((orbs, nx, 2 * side, nz), BF16),
            pltpu.VMEM((orbs, nx, 2 * side, nz), BF16),
            pltpu.VMEM((width, LANES), F32),
            pltpu.VMEM((table_rows, LANES), F32),
        ],
        scratch_shapes=[pltpu.VMEM((2 * side, 4 * side), F32)],
        compiler_params=params,
        cost_estimate=pl.CostEstimate(flops=10**8, bytes_accessed=4 * 10**6, transcendentals=0),
        name="interior",
    )(prev_block, block_here, seed_here, levels_here, hops_here, onsite_here)

    phigh, plow, sums, _ = pl.pallas_call(
        halo_kernel,
        out_shape=[
            pltpu.VMEM((orbs, nx, side, nz), BF16),
            pltpu.VMEM((orbs, nx, side, nz), BF16),
            pltpu.VMEM((devices, width // 2, LANES), F32),
            pltpu.VMEM(block.shape, F32),
        ],
        input_output_aliases={0: 3},
        scratch_shapes=[pltpu.VMEM((6 * side, 2 * side), F32)],
        compiler_params=params,
        name="halo",
    )(part, seed_here, table, xnear, yfar, ynear, xfar, high, low, metric)

    sums = lax.all_to_all(sums, ("gx", "gy"), 0, 0)

    next_block, alpha, beta = pl.pallas_call(
        lambda *refs: final_kernel(count, *refs),
        out_shape=[
            jax.ShapeDtypeStruct(block.shape, F32),
            jax.ShapeDtypeStruct((width, width), F32),
            jax.ShapeDtypeStruct((width, width), F32),
        ],
        out_specs=[outside] * 3,
        scratch_shapes=[
            pltpu.VMEM(block.shape, F32),
            pltpu.VMEM((width, width), F32),
            pltpu.VMEM((width, width), F32),
            pltpu.SemaphoreType.DMA((orbs + 2,)),
        ],
        compiler_params=params,
        name="final",
    )(sums, high, low, phigh, plow)
    return next_block, alpha, beta


def solution(mesh):
    in_specs = (
        P(None, None, "gx", "gy", None),
        P(None, None, "gx", "gy", None),
        P(None, "gx", "gy", None),
        P("gx", "gy", None),
        P(),
        P(),
    )
    out_specs = (P(None, None, "gx", "gy", None), P(), P())
    return jax.shard_map(
        per_device, mesh=mesh, in_specs=in_specs, out_specs=out_specs, check_vma=False
    )
```

```python
import jax
import jax.numpy as jnp
from jax import lax
from jax.experimental import pallas as pl
from jax.experimental.pallas import tpu as pltpu
from jax.sharding import PartitionSpec as P

HIGH = lax.Precision.HIGHEST
F32 = jnp.float32
BF16 = jnp.bfloat16
LANES = 128
ROWS = 8
PARAMS = dict(vmem_limit_bytes=32 * 1024 * 1024)


def split(value):
    high = value.astype(BF16)
    low = (value - high.astype(F32)).astype(BF16)
    return high, low


def iota(shape, dim):
    return lax.broadcasted_iota(jnp.int32, shape, dim)


def dot(left, right, dims, precision=None):
    return lax.dot_general(
        left, right, (dims, ((), ())), precision=precision, preferred_element_type=F32
    )


def pick(table_ref, row, index):
    entries = jnp.broadcast_to(table_ref[row : row + 1, :], index.shape)
    return jnp.take_along_axis(entries, index, axis=1)


def bonds_of(table_ref, direction, index, orbs):
    base = direction * orbs * orbs
    return [
        [pick(table_ref, base + a * orbs + b, index) for b in range(orbs)] for a in range(orbs)
    ]


def fill_table(table_ref, hop_ref, onsite_ref):
    orbs, kinds = hop_ref.shape[1], hop_ref.shape[3]
    for d in range(3):
        for a in range(orbs):
            base = (d * orbs + a) * orbs
            table_ref[base : base + orbs, :kinds] = hop_ref[d, a]
    base = 3 * orbs * orbs
    table_ref[base : base + orbs, : onsite_ref.shape[1]] = onsite_ref[...]


def times(bonds, field):
    return [sum(bonds[a][b] * field[b] for b in range(len(field))) for a in range(len(field))]


def times_transposed(bonds, field):
    return [sum(bonds[a][b] * field[a] for a in range(len(field))) for b in range(len(field))]


def pack_kernel(
    block_in,
    seed_in,
    level_in,
    hop_in,
    onsite_in,
    block_ref,
    seed_ref,
    level_ref,
    hop_ref,
    onsite_ref,
    xup_ref,
    yfar_ref,
    ynear_ref,
    xdown_ref,
    sems,
):
    orbs, width, nx, ny, _ = block_ref.shape
    yeven = lax.axis_index("gy") % 2 == 0
    pairs = [(block_in.at[o], block_ref.at[o]) for o in range(orbs)]
    pairs += [(seed_in, seed_ref), (level_in, level_ref), (hop_in, hop_ref), (onsite_in, onsite_ref)]
    loads = [pltpu.make_async_copy(*pair, sems.at[i]) for i, pair in enumerate(pairs)]
    for load in loads:
        load.start()
    for o in range(orbs):
        loads[o].wait()
        for n in range(width):
            spot = o * width + n
            xup_ref[spot] = block_ref[o, n, nx - 1]
            xdown_ref[spot] = block_ref[o, n, 0]
            top, bottom = block_ref[o, n, :, ny - 1, :], block_ref[o, n, :, 0, :]
            ynear_ref[spot] = jnp.where(yeven, top, bottom)
            yfar_ref[spot] = jnp.where(yeven, bottom, top)
    loads[orbs].wait()
    xup_ref[orbs * width] = seed_ref[0, nx - 1].astype(F32)
    for ref in (ynear_ref, yfar_ref):
        ref[orbs * width] = seed_ref[1, :, ny - 1, :].astype(F32)
    for load in loads[orbs + 1 :]:
        load.wait()


def kept_sums(total):
    rows, columns = total.shape
    same = (iota((rows, columns), 0) % ROWS) == (iota((rows, columns), 1) % ROWS)
    kept = jnp.where(same, total, 0.0)
    return kept.reshape(rows // ROWS, ROWS, columns).sum(axis=1)


def gathered(value, spots):
    high, low = split(value)
    last = (value - high.astype(F32) - low.astype(F32)).astype(BF16)
    pieces = dot(jnp.concatenate([high, low, last], 0), spots.astype(BF16), ((1,), (0,)))
    rows = value.shape[0]
    return pieces[:rows] + pieces[rows : 2 * rows] + pieces[2 * rows :]


def interior_kernel(
    prev_in,
    block_ref,
    seed_ref,
    level_ref,
    hop_ref,
    onsite_ref,
    part_ref,
    high_ref,
    low_ref,
    metric_ref,
    table_ref,
    gram_ref,
    prev_ref,
    sem,
):
    orbs, width, nx, ny, nz = block_ref.shape
    load = pltpu.make_async_copy(prev_in, prev_ref, sem)
    load.start()
    fill_table(table_ref, hop_ref, onsite_ref)
    row = iota((ny, nz), 0)
    side = width * ny

    def stencil(x, carry):
        before = jnp.maximum(x - 1, 0)
        inside = jnp.where(x > 0, 1.0, 0.0)
        energy = [pick(table_ref, 3 * orbs * orbs + o, level_ref[x]) for o in range(orbs)]
        bond_x = bonds_of(table_ref, 0, seed_ref[0, before], orbs)
        bond_x = [[inside * value for value in line] for line in bond_x]
        bond_y = bonds_of(table_ref, 1, seed_ref[1, x], orbs)
        bond_z = bonds_of(table_ref, 2, seed_ref[2, x], orbs)
        for n in range(width):
            here = [block_ref[o, n, x] for o in range(orbs)]
            behind = [block_ref[o, n, before] for o in range(orbs)]
            forward = times(bond_x, here)
            for o in range(orbs):
                part_ref[o, n, before] += forward[o]
            image = [energy[o] * here[o] for o in range(orbs)]
            image = [a + b for a, b in zip(image, times_transposed(bond_x, behind))]
            ahead = [jnp.where(row == ny - 1, 0.0, pltpu.roll(v, ny - 1, 0)) for v in here]
            image = [a + b for a, b in zip(image, times(bond_y, ahead))]
            carried = times_transposed(bond_y, here)
            image = [
                a + jnp.where(row == 0, 0.0, pltpu.roll(b, 1, 0)) for a, b in zip(image, carried)
            ]
            ahead = [pltpu.roll(v, nz - 1, 1) for v in here]
            image = [a + b for a, b in zip(image, times(bond_z, ahead))]
            carried = times_transposed(bond_z, here)
            image = [a + pltpu.roll(b, 1, 1) for a, b in zip(image, carried)]
            for o in range(orbs):
                part_ref[o, n, x] = image[o]
        return carry

    lax.fori_loop(0, nx, stencil, 0)
    load.wait()
    gram_ref[...] = jnp.zeros(gram_ref.shape, F32)

    def products(pair):
        for o in range(orbs):
            highs, lows = [], []
            for half in range(2):
                x = 2 * pair + half
                basis = jnp.concatenate(
                    [prev_ref[o, :, x].reshape(side, nz), block_ref[o, :, x].reshape(side, nz)], 0
                )
                high, low = split(basis)
                high_ref[o, x] = high
                low_ref[o, x] = low
                highs.append(high)
                lows.append(low)
            high = jnp.concatenate(highs, 1)
            low = jnp.concatenate(lows, 1)
            gram_ref[...] += dot(high, jnp.concatenate([high, low], 0), ((1,), (1,)))

    for pair in range(nx // 2):
        products(pair)
    crossed = gram_ref[:, 2 * side :]
    sums = kept_sums(gram_ref[:, : 2 * side] + crossed + crossed.T)
    spots = iota((LANES, LANES), 0) // ny
    lanes = iota((LANES, LANES), 1) % (LANES // 2)
    maps = [jnp.where(lanes == width * (3 + 2 * i) + spots, 1.0, 0.0) for i in range(2)]
    parts = [sums[i * width : (i + 1) * width] for i in range(2)]
    metric_ref[...] = gathered(jnp.concatenate(parts, 1), jnp.concatenate(maps, 0))


def placed(total, base):
    width = base.shape[0]
    sums = kept_sums(total)
    spots = (iota((LANES, LANES), 0) // ROWS) % width
    sums = gathered(sums, jnp.where(iota((LANES, LANES), 1) % width == spots, 1.0, 0.0))
    place = (iota(base.shape, 1) % (LANES // 2)) // width
    for i in range(3):
        base = base + jnp.where(place == i, sums[i * width : (i + 1) * width], 0.0)
    return base


def product_sums(bhigh, blow, high, low):
    both = dot(
        jnp.concatenate([bhigh, high, blow, low], 0), jnp.concatenate([high, low], 0), ((1,), (1,))
    )
    half = both.shape[0] // 2
    return both[:half] + both[half:]


def y_kernel(
    part_in,
    seed_ref,
    table_ref,
    up_ref,
    far_ref,
    near_ref,
    high_ref,
    low_ref,
    metric_ref,
    phigh_ref,
    plow_ref,
    packed_ref,
    part_ref,
    total_ref,
):
    orbs, width, nx, ny, nz = part_ref.shape
    side = width * ny
    last = orbs * width

    bond_low = bonds_of(table_ref, 0, up_ref[last].astype(jnp.int32), orbs)
    for n in range(width):
        back = times_transposed(bond_low, [up_ref[o * width + n] for o in range(orbs)])
        for o in range(orbs):
            part_ref[o, n, 0] += back[o]

    def add_faces(low_face, high_face):
        bond = bonds_of(table_ref, 1, seed_ref[1, :, ny - 1, :], orbs)
        bond_low = bonds_of(table_ref, 1, low_face[last].astype(jnp.int32), orbs)
        for n in range(width):
            forward = times(bond, [high_face[o * width + n] for o in range(orbs)])
            back = times_transposed(bond_low, [low_face[o * width + n] for o in range(orbs)])
            for o in range(orbs):
                part_ref[o, n, :, ny - 1, :] += forward[o]
                part_ref[o, n, :, 0, :] += back[o]

    even = lax.axis_index("gy") % 2 == 0
    pl.when(even)(lambda: add_faces(far_ref, near_ref))
    pl.when(jnp.logical_not(even))(lambda: add_faces(near_ref, far_ref))

    total_ref[...] = jnp.zeros(total_ref.shape, F32)
    for first in range(1, nx - 1, 2):
        for o in range(orbs):
            ins = [[], [], [], []]
            for x in (first, first + 1):
                high, low = split(part_ref[o, :, x].reshape(side, nz))
                phigh_ref[o, x] = high
                plow_ref[o, x] = low
                for group, value in zip(ins, (high_ref[o, x], low_ref[o, x], high, low)):
                    group.append(value)
            total_ref[...] += product_sums(*(jnp.concatenate(group, 1) for group in ins))
    packed_ref[...] = placed(total_ref[...], metric_ref[...])


def x_kernel(
    part_ref,
    seed_ref,
    table_ref,
    down_ref,
    high_ref,
    low_ref,
    packed_ref,
    phigh_in,
    plow_in,
    phigh_ref,
    plow_ref,
    sums_ref,
    face_ref,
):
    orbs, width, nx, ny, nz = part_ref.shape
    bond = bonds_of(table_ref, 0, seed_ref[0, nx - 1], orbs)
    for n in range(width):
        forward = times(bond, [down_ref[o * width + n] for o in range(orbs)])
        for o in range(orbs):
            face_ref[o, n * ny : (n + 1) * ny, :nz] = part_ref[o, n, 0]
            face_ref[o, n * ny : (n + 1) * ny, nz:] = part_ref[o, n, nx - 1] + forward[o]
    total = 0.0
    for o in range(orbs):
        high, low = split(face_ref[o])
        for i, x in enumerate((0, nx - 1)):
            phigh_ref[o, x] = high[:, i * nz : (i + 1) * nz]
            plow_ref[o, x] = low[:, i * nz : (i + 1) * nz]
        bhigh, blow = (
            jnp.concatenate([ref[o, 0], ref[o, nx - 1]], 1) for ref in (high_ref, low_ref)
        )
        total = total + product_sums(bhigh, blow, high, low)
    packed = placed(total, packed_ref[...])
    half = width // 2
    lanes = iota((half, LANES), 1)
    folded = jnp.where(lanes < LANES // 2, packed[:half], packed[half:])
    sums_ref[...] = jnp.broadcast_to(folded[None], sums_ref.shape)


def column(value, spot):
    return jnp.broadcast_to(value[:, spot : spot + 1], value.shape)


def line(value, spot):
    return jnp.broadcast_to(value[spot : spot + 1, :], value.shape)


def added(terms):
    while len(terms) > 1:
        terms = [sum(terms[i : i + 2][1:], terms[i]) for i in range(0, len(terms), 2)]
    return terms[0]


def final_kernel(
    count,
    sums_ref,
    high_ref,
    low_ref,
    phigh_ref,
    plow_ref,
    next_ref,
    alpha_out,
    beta_out,
    out_ref,
    alpha_ref,
    beta_ref,
    sems,
):
    orbs, nx, side, nz = phigh_ref.shape
    width = side // ROWS
    shape = (width, LANES)
    rows, lanes = iota(shape, 0), iota(shape, 1)
    folded = jnp.sum(sums_ref[...], axis=0) / count
    sums = jnp.concatenate([folded, pltpu.roll(folded, LANES // 2, 1)], 0)

    def moved(start, length):
        value = sums if start == 0 else pltpu.roll(sums, LANES - start, 1)
        return jnp.where(lanes < length, value, 0.0)

    first = [moved(0, width), moved(width, width)]
    norms = moved(2 * width, width)
    metric = [moved(3 * width, 2 * width), moved(5 * width, 2 * width)]
    alpha_ref[...] = first[1][:, :width]
    stores = [pltpu.make_async_copy(alpha_ref, alpha_out, sems.at[orbs])]
    stores[-1].start()
    ones = [jnp.where(lanes == rows + i * width, 1.0, 0.0) for i in range(2)]
    lack = [one - value for one, value in zip(ones, metric)]
    lack_columns = [[column(value, k) for k in range(2 * width)] for value in lack]

    def lacking(pair):
        lines = [line(value, k) for value in pair for k in range(width)]
        return [added([a * b for a, b in zip(columns, lines)]) for columns in lack_columns]

    one = lacking(first)
    two = lacking(one)
    three = lacking(two)
    weighed = [added(list(terms)) for terms in zip(first, one, two, three)]
    turned = jnp.concatenate(first, 0).T[:width]
    turned_columns = [
        jnp.broadcast_to(turned[:, k : k + 1], shape) for k in range(2 * width)
    ]
    weighed_lines = [line(value, k) for value in weighed for k in range(width)]
    gram = norms - added([a * b for a, b in zip(turned_columns, weighed_lines)])
    twice = [a + b for a, b in zip(ones, lack)]
    twice_lines = [line(value, k) for value in twice for k in range(width)]
    coeffs = added([a * b for a, b in zip(turned_columns, twice_lines)])
    table = gram + jnp.where(lanes == rows + width, 1.0, 0.0) - pltpu.roll(coeffs, 2 * width, 1)

    entry = {}
    for k in range(width):
        spread = column(gram, k)
        for j in range(k, width):
            entry[j, k] = line(spread, j)
    lines = [line(table, k) for k in range(width)]
    for k in range(width):
        inverse = 1.0 / entry[k, k]
        for j in range(k + 1, width):
            ratio = entry[j, k] * inverse
            for i in range(k + 1, j + 1):
                entry[j, i] = entry[j, i] - ratio * entry[i, k]
            lines[j] = lines[j] - ratio * lines[k]
    lines = [value * lax.rsqrt(entry[k, k]) for k, value in enumerate(lines)]
    upper = jnp.zeros(shape, F32)
    for k in range(width):
        upper = jnp.where((rows == k) & (lanes >= k), lines[k], upper)
    beta_ref[...] = upper[:, :width]
    stores.append(pltpu.make_async_copy(beta_ref, beta_out, sems.at[orbs + 1]))
    stores[-1].start()

    same = rows == lanes % ROWS
    spots = [2 * width + lanes // ROWS, width + (lanes // ROWS) % width]
    grown = [
        jnp.concatenate(
            [jnp.where(same, jnp.take_along_axis(value, spot, axis=1), 0.0) for value in lines], 0
        )
        for spot in spots
    ]
    mixed_high, mixed_low = split(jnp.concatenate([grown[0], grown[1][:, :side]], 1))
    mixed = jnp.concatenate([mixed_high, mixed_low], 0)
    dims = ((1,), (0,))

    def chunk(o, pair):
        highs, lows = [], []
        for half in range(2):
            x = 2 * pair + half
            highs.append(jnp.concatenate([high_ref[o, x], phigh_ref[o, x]], 0))
            lows.append(jnp.concatenate([low_ref[o, x], plow_ref[o, x]], 0))
        both = dot(mixed, jnp.concatenate(highs, 1), dims)
        out = both[:side] + both[side:] + dot(mixed_high, jnp.concatenate(lows, 1), dims)
        for half in range(2):
            x = 2 * pair + half
            out_ref[o, :, x] = out[:, half * nz : (half + 1) * nz].reshape(width, ROWS, nz)

    for o in range(orbs):
        for pair in range(nx // 2):
            chunk(o, pair)
        stores.append(pltpu.make_async_copy(out_ref.at[o], next_ref.at[o], sems.at[o]))
        stores[-1].start()
    for store in stores:
        store.wait()


def shifted(value, axis, steps):
    count = lax.axis_size(axis)
    return lax.ppermute(value, axis, [(i, (i + steps) % count) for i in range(count)])


def swapped(value, axis, far):
    count = lax.axis_size(axis)
    return lax.ppermute(
        value, axis, [(i, (i + (1 if i % 2 == far else -1)) % count) for i in range(count)]
    )


def per_device(prev_block, block, hop_seed, levels, hop_table, onsite_table):
    orbs, width, nx, ny, nz = block.shape
    devices = lax.axis_size("gx") * lax.axis_size("gy")
    count = orbs * nx * ny * nz * devices
    fields = orbs * width
    hops = jnp.transpose(hop_table, (0, 2, 3, 1))
    onsite = onsite_table.T
    table_rows = 3 * orbs * orbs + ROWS
    outside = pl.BlockSpec(memory_space=pltpu.HBM)

    def stay(value):
        return pltpu.with_memory_space_constraint(value, pltpu.HBM)

    params = pltpu.CompilerParams(**PARAMS)

    block_here, seed_here, levels_here, hops_here, onsite_here, xup, yfar, ynear, xdown = pl.pallas_call(
        pack_kernel,
        in_specs=[outside] * 5,
        out_shape=[
            pltpu.VMEM(block.shape, F32),
            pltpu.VMEM(hop_seed.shape, jnp.int32),
            pltpu.VMEM(levels.shape, jnp.int32),
            pltpu.VMEM(hops.shape, F32),
            pltpu.VMEM(onsite.shape, F32),
            pltpu.VMEM((fields + 1, ny, nz), F32),
            pltpu.VMEM((fields + 1, nx, nz), F32),
            pltpu.VMEM((fields + 1, nx, nz), F32),
            pltpu.VMEM((fields, ny, nz), F32),
        ],
        scratch_shapes=[pltpu.SemaphoreType.DMA((orbs + 4,))],
        compiler_params=params,
        name="pack",
    )(stay(block), stay(hop_seed), stay(levels), stay(hops), stay(onsite))
    xup = shifted(xup, "gx", 1)
    yfar = swapped(yfar, "gy", 1)
    ynear = swapped(ynear, "gy", 0)
    xdown = shifted(xdown, "gx", -1)

    side = width * ny
    part, high, low, metric, table = pl.pallas_call(
        interior_kernel,
        out_shape=[
            pltpu.VMEM(block.shape, F32),
            pltpu.VMEM((orbs, nx, 2 * side, nz), BF16),
            pltpu.VMEM((orbs, nx, 2 * side, nz), BF16),
            pltpu.VMEM((width, LANES), F32),
            pltpu.VMEM((table_rows, LANES), F32),
        ],
        in_specs=[outside] + [pl.BlockSpec(memory_space=pltpu.VMEM)] * 5,
        scratch_shapes=[
            pltpu.VMEM((2 * side, 4 * side), F32),
            pltpu.VMEM(block.shape, F32),
            pltpu.SemaphoreType.DMA(()),
        ],
        compiler_params=params,
        cost_estimate=pl.CostEstimate(flops=10**8, bytes_accessed=4 * 10**6, transcendentals=0),
        name="interior",
    )(stay(prev_block), block_here, seed_here, levels_here, hops_here, onsite_here)

    product_halves = [pltpu.VMEM((orbs, nx, side, nz), BF16)] * 2
    phigh, plow, packed, part = pl.pallas_call(
        y_kernel,
        out_shape=product_halves
        + [pltpu.VMEM((width, LANES), F32), pltpu.VMEM(block.shape, F32)],
        input_output_aliases={0: 3},
        scratch_shapes=[pltpu.VMEM((3 * side, 2 * side), F32)],
        compiler_params=params,
        cost_estimate=pl.CostEstimate(flops=10**8, bytes_accessed=4 * 10**6, transcendentals=0),
        name="y_faces",
    )(part, seed_here, table, xup, yfar, ynear, high, low, metric)

    phigh, plow, sums = pl.pallas_call(
        x_kernel,
        out_shape=product_halves + [pltpu.VMEM((devices, width // 2, LANES), F32)],
        input_output_aliases={7: 0, 8: 1},
        scratch_shapes=[pltpu.VMEM((orbs, side, 2 * nz), F32)],
        compiler_params=params,
        name="x_faces",
    )(part, seed_here, table, xdown, high, low, packed, phigh, plow)

    sums = lax.all_to_all(sums, ("gx", "gy"), 0, 0)

    next_block, alpha, beta = pl.pallas_call(
        lambda *refs: final_kernel(count, *refs),
        out_shape=[
            jax.ShapeDtypeStruct(block.shape, F32),
            jax.ShapeDtypeStruct((width, width), F32),
            jax.ShapeDtypeStruct((width, width), F32),
        ],
        out_specs=[outside] * 3,
        scratch_shapes=[
            pltpu.VMEM(block.shape, F32),
            pltpu.VMEM((width, width), F32),
            pltpu.VMEM((width, width), F32),
            pltpu.SemaphoreType.DMA((orbs + 2,)),
        ],
        compiler_params=params,
        name="final",
    )(sums, high, low, phigh, plow)
    return next_block, alpha, beta


def solution(mesh):
    in_specs = (
        P(None, None, "gx", "gy", None),
        P(None, None, "gx", "gy", None),
        P(None, "gx", "gy", None),
        P("gx", "gy", None),
        P(),
        P(),
    )
    out_specs = (P(None, None, "gx", "gy", None), P(), P())
    return jax.shard_map(
        per_device, mesh=mesh, in_specs=in_specs, out_specs=out_specs, check_vma=False
    )
```

```python
import jax
import jax.numpy as jnp
from jax import lax
from jax.experimental import pallas as pl
from jax.experimental.pallas import tpu as pltpu
from jax.sharding import PartitionSpec as P

HIGH = lax.Precision.HIGHEST
F32 = jnp.float32
BF16 = jnp.bfloat16
LANES = 128
ROWS = 8
PARAMS = dict(vmem_limit_bytes=32 * 1024 * 1024)


def split(value):
    high = value.astype(BF16)
    low = (value - high.astype(F32)).astype(BF16)
    return high, low


def iota(shape, dim):
    return lax.broadcasted_iota(jnp.int32, shape, dim)


def dot(left, right, dims, precision=None):
    return lax.dot_general(
        left, right, (dims, ((), ())), precision=precision, preferred_element_type=F32
    )


def pick(table_ref, row, index):
    entries = jnp.broadcast_to(table_ref[row : row + 1, :], index.shape)
    return jnp.take_along_axis(entries, index, axis=1)


def bonds_of(table_ref, direction, index, orbs):
    base = direction * orbs * orbs
    return [
        [pick(table_ref, base + a * orbs + b, index) for b in range(orbs)] for a in range(orbs)
    ]


def kept_bonds(edge_ref, direction, orbs):
    base = direction * orbs * orbs
    return [[edge_ref[base + a * orbs + b] for b in range(orbs)] for a in range(orbs)]


def fill_table(table_ref, hop_ref, onsite_ref):
    orbs, kinds = hop_ref.shape[1], hop_ref.shape[3]
    for d in range(3):
        for a in range(orbs):
            base = (d * orbs + a) * orbs
            table_ref[base : base + orbs, :kinds] = hop_ref[d, a]
    base = 3 * orbs * orbs
    table_ref[base : base + orbs, : onsite_ref.shape[1]] = onsite_ref[...]


def times(bonds, field):
    return [sum(bonds[a][b] * field[b] for b in range(len(field))) for a in range(len(field))]


def times_transposed(bonds, field):
    return [sum(bonds[a][b] * field[a] for a in range(len(field))) for b in range(len(field))]


def pack_kernel(
    block_in,
    seed_in,
    level_in,
    hop_in,
    onsite_in,
    block_ref,
    seed_ref,
    level_ref,
    hop_ref,
    onsite_ref,
    xup_ref,
    yfar_ref,
    ynear_ref,
    xdown_ref,
    sems,
):
    orbs, width, nx, ny, _ = block_ref.shape
    yeven = lax.axis_index("gy") % 2 == 0
    pairs = [(block_in.at[o], block_ref.at[o]) for o in range(orbs)]
    pairs += [(seed_in, seed_ref), (level_in, level_ref), (hop_in, hop_ref), (onsite_in, onsite_ref)]
    loads = [pltpu.make_async_copy(*pair, sems.at[i]) for i, pair in enumerate(pairs)]
    for load in loads:
        load.start()
    for o in range(orbs):
        loads[o].wait()
        for n in range(width):
            spot = o * width + n
            xup_ref[spot] = block_ref[o, n, nx - 1]
            xdown_ref[spot] = block_ref[o, n, 0]
            top, bottom = block_ref[o, n, :, ny - 1, :], block_ref[o, n, :, 0, :]
            ynear_ref[spot] = jnp.where(yeven, top, bottom)
            yfar_ref[spot] = jnp.where(yeven, bottom, top)
    loads[orbs].wait()
    xup_ref[orbs * width] = seed_ref[0, nx - 1].astype(F32)
    for ref in (ynear_ref, yfar_ref):
        ref[orbs * width] = seed_ref[1, :, ny - 1, :].astype(F32)
    for load in loads[orbs + 1 :]:
        load.wait()


def kept_sums(total):
    rows, columns = total.shape
    same = (iota((rows, columns), 0) % ROWS) == (iota((rows, columns), 1) % ROWS)
    kept = jnp.where(same, total, 0.0)
    return kept.reshape(rows // ROWS, ROWS, columns).sum(axis=1)


def gathered(value, spots):
    high, low = split(value)
    last = (value - high.astype(F32) - low.astype(F32)).astype(BF16)
    pieces = dot(jnp.concatenate([high, low, last], 0), spots.astype(BF16), ((1,), (0,)))
    rows = value.shape[0]
    return pieces[:rows] + pieces[rows : 2 * rows] + pieces[2 * rows :]


def interior_kernel(
    prev_in,
    block_ref,
    seed_ref,
    level_ref,
    hop_ref,
    onsite_ref,
    part_ref,
    high_ref,
    low_ref,
    metric_ref,
    table_ref,
    edge_ref,
    gram_ref,
    prev_ref,
    sem,
):
    orbs, width, nx, ny, nz = block_ref.shape
    load = pltpu.make_async_copy(prev_in, prev_ref, sem)
    load.start()
    fill_table(table_ref, hop_ref, onsite_ref)
    row = iota((ny, nz), 0)
    side = width * ny

    def stencil(x, carry):
        before = jnp.maximum(x - 1, 0)
        inside = jnp.where(x > 0, 1.0, 0.0)
        energy = [pick(table_ref, 3 * orbs * orbs + o, level_ref[x]) for o in range(orbs)]
        bond_x = bonds_of(table_ref, 0, seed_ref[0, before], orbs)
        bond_x = [[inside * value for value in line] for line in bond_x]
        bond_y = bonds_of(table_ref, 1, seed_ref[1, x], orbs)
        bond_z = bonds_of(table_ref, 2, seed_ref[2, x], orbs)
        for n in range(width):
            here = [block_ref[o, n, x] for o in range(orbs)]
            behind = [block_ref[o, n, before] for o in range(orbs)]
            forward = times(bond_x, here)
            for o in range(orbs):
                part_ref[o, n, before] += forward[o]
            image = [energy[o] * here[o] for o in range(orbs)]
            image = [a + b for a, b in zip(image, times_transposed(bond_x, behind))]
            ahead = [jnp.where(row == ny - 1, 0.0, pltpu.roll(v, ny - 1, 0)) for v in here]
            image = [a + b for a, b in zip(image, times(bond_y, ahead))]
            carried = times_transposed(bond_y, here)
            image = [
                a + jnp.where(row == 0, 0.0, pltpu.roll(b, 1, 0)) for a, b in zip(image, carried)
            ]
            ahead = [pltpu.roll(v, nz - 1, 1) for v in here]
            image = [a + b for a, b in zip(image, times(bond_z, ahead))]
            carried = times_transposed(bond_z, here)
            image = [a + pltpu.roll(b, 1, 1) for a, b in zip(image, carried)]
            for o in range(orbs):
                part_ref[o, n, x] = image[o]
        return carry

    lax.fori_loop(0, nx, stencil, 0)
    for d, index in enumerate((seed_ref[0, nx - 1], seed_ref[1, :, ny - 1, :])):
        for i, bond in enumerate(sum(bonds_of(table_ref, d, index, orbs), [])):
            edge_ref[d * orbs * orbs + i] = bond
    load.wait()
    gram_ref[...] = jnp.zeros(gram_ref.shape, F32)

    def products(pair):
        for o in range(orbs):
            highs, lows = [], []
            for half in range(2):
                x = 2 * pair + half
                basis = jnp.concatenate(
                    [prev_ref[o, :, x].reshape(side, nz), block_ref[o, :, x].reshape(side, nz)], 0
                )
                high, low = split(basis)
                high_ref[o, x] = high
                low_ref[o, x] = low
                highs.append(high)
                lows.append(low)
            high = jnp.concatenate(highs, 1)
            low = jnp.concatenate(lows, 1)
            gram_ref[...] += dot(high, jnp.concatenate([high, low], 0), ((1,), (1,)))

    for pair in range(nx // 2):
        products(pair)
    crossed = gram_ref[:, 2 * side :]
    sums = kept_sums(gram_ref[:, : 2 * side] + crossed + crossed.T)
    spots = iota((LANES, LANES), 0) // ny
    lanes = iota((LANES, LANES), 1) % (LANES // 2)
    maps = [jnp.where(lanes == width * (3 + 2 * i) + spots, 1.0, 0.0) for i in range(2)]
    parts = [sums[i * width : (i + 1) * width] for i in range(2)]
    metric_ref[...] = gathered(jnp.concatenate(parts, 1), jnp.concatenate(maps, 0))


def placed(total, base):
    width = base.shape[0]
    sums = kept_sums(total)
    spots = (iota((LANES, LANES), 0) // ROWS) % width
    sums = gathered(sums, jnp.where(iota((LANES, LANES), 1) % width == spots, 1.0, 0.0))
    place = (iota(base.shape, 1) % (LANES // 2)) // width
    for i in range(3):
        base = base + jnp.where(place == i, sums[i * width : (i + 1) * width], 0.0)
    return base


def product_sums(bhigh, blow, high, low):
    both = dot(
        jnp.concatenate([bhigh, high, blow, low], 0), jnp.concatenate([high, low], 0), ((1,), (1,))
    )
    half = both.shape[0] // 2
    return both[:half] + both[half:]


def y_kernel(
    part_in,
    edge_ref,
    table_ref,
    up_ref,
    far_ref,
    near_ref,
    high_ref,
    low_ref,
    phigh_ref,
    plow_ref,
    total_ref,
    part_ref,
):
    orbs, width, nx, ny, nz = part_ref.shape
    side = width * ny
    last = orbs * width

    bond_low = bonds_of(table_ref, 0, up_ref[last].astype(jnp.int32), orbs)
    for n in range(width):
        back = times_transposed(bond_low, [up_ref[o * width + n] for o in range(orbs)])
        for o in range(orbs):
            part_ref[o, n, 0] += back[o]

    def add_faces(low_face, high_face):
        bond = kept_bonds(edge_ref, 1, orbs)
        bond_low = bonds_of(table_ref, 1, low_face[last].astype(jnp.int32), orbs)
        for n in range(width):
            forward = times(bond, [high_face[o * width + n] for o in range(orbs)])
            back = times_transposed(bond_low, [low_face[o * width + n] for o in range(orbs)])
            for o in range(orbs):
                part_ref[o, n, :, ny - 1, :] += forward[o]
                part_ref[o, n, :, 0, :] += back[o]

    even = lax.axis_index("gy") % 2 == 0
    pl.when(even)(lambda: add_faces(far_ref, near_ref))
    pl.when(jnp.logical_not(even))(lambda: add_faces(near_ref, far_ref))

    total_ref[...] = jnp.zeros(total_ref.shape, F32)
    for first in range(1, nx - 1, 2):
        for o in range(orbs):
            ins = [[], [], [], []]
            for x in (first, first + 1):
                high, low = split(part_ref[o, :, x].reshape(side, nz))
                phigh_ref[o, x] = high
                plow_ref[o, x] = low
                for group, value in zip(ins, (high_ref[o, x], low_ref[o, x], high, low)):
                    group.append(value)
            total_ref[...] += product_sums(*(jnp.concatenate(group, 1) for group in ins))


def x_kernel(
    part_ref,
    edge_ref,
    down_ref,
    high_ref,
    low_ref,
    total_ref,
    metric_ref,
    phigh_in,
    plow_in,
    phigh_ref,
    plow_ref,
    sums_ref,
    face_ref,
):
    orbs, width, nx, ny, nz = part_ref.shape
    bond = kept_bonds(edge_ref, 0, orbs)
    for n in range(width):
        forward = times(bond, [down_ref[o * width + n] for o in range(orbs)])
        for o in range(orbs):
            face_ref[o, n * ny : (n + 1) * ny, :nz] = part_ref[o, n, 0]
            face_ref[o, n * ny : (n + 1) * ny, nz:] = part_ref[o, n, nx - 1] + forward[o]
    total = total_ref[...]
    for o in range(orbs):
        high, low = split(face_ref[o])
        for i, x in enumerate((0, nx - 1)):
            phigh_ref[o, x] = high[:, i * nz : (i + 1) * nz]
            plow_ref[o, x] = low[:, i * nz : (i + 1) * nz]
        bhigh, blow = (
            jnp.concatenate([ref[o, 0], ref[o, nx - 1]], 1) for ref in (high_ref, low_ref)
        )
        total = total + product_sums(bhigh, blow, high, low)
    packed = placed(total, metric_ref[...])
    half = width // 2
    lanes = iota((half, LANES), 1)
    folded = jnp.where(lanes < LANES // 2, packed[:half], packed[half:])
    sums_ref[...] = jnp.broadcast_to(folded[None], sums_ref.shape)


def column(value, spot):
    return jnp.broadcast_to(value[:, spot : spot + 1], value.shape)


def line(value, spot):
    return jnp.broadcast_to(value[spot : spot + 1, :], value.shape)


def added(terms):
    while len(terms) > 1:
        terms = [sum(terms[i : i + 2][1:], terms[i]) for i in range(0, len(terms), 2)]
    return terms[0]


def final_kernel(
    count,
    sums_ref,
    high_ref,
    low_ref,
    phigh_ref,
    plow_ref,
    next_ref,
    alpha_out,
    beta_out,
    out_ref,
    alpha_ref,
    beta_ref,
    sems,
):
    orbs, nx, side, nz = phigh_ref.shape
    width = side // ROWS
    shape = (width, LANES)
    rows, lanes = iota(shape, 0), iota(shape, 1)
    folded = jnp.sum(sums_ref[...], axis=0) / count
    sums = jnp.concatenate([folded, pltpu.roll(folded, LANES // 2, 1)], 0)

    def moved(start, length):
        value = sums if start == 0 else pltpu.roll(sums, LANES - start, 1)
        return jnp.where(lanes < length, value, 0.0)

    first = [moved(0, width), moved(width, width)]
    norms = moved(2 * width, width)
    metric = [moved(3 * width, 2 * width), moved(5 * width, 2 * width)]
    alpha_ref[...] = first[1][:, :width]
    stores = [pltpu.make_async_copy(alpha_ref, alpha_out, sems.at[2 * orbs])]
    stores[-1].start()
    ones = [jnp.where(lanes == rows + i * width, 1.0, 0.0) for i in range(2)]
    lack = [one - value for one, value in zip(ones, metric)]
    lack_columns = [[column(value, k) for k in range(2 * width)] for value in lack]

    def lacking(pair):
        lines = [line(value, k) for value in pair for k in range(width)]
        return [added([a * b for a, b in zip(columns, lines)]) for columns in lack_columns]

    one = lacking(first)
    two = lacking(one)
    three = lacking(two)
    weighed = [added(list(terms)) for terms in zip(first, one, two, three)]
    turned = jnp.concatenate(first, 0).T[:width]
    turned_columns = [
        jnp.broadcast_to(turned[:, k : k + 1], shape) for k in range(2 * width)
    ]
    weighed_lines = [line(value, k) for value in weighed for k in range(width)]
    gram = norms - added([a * b for a, b in zip(turned_columns, weighed_lines)])
    twice = [a + b for a, b in zip(ones, lack)]
    twice_lines = [line(value, k) for value in twice for k in range(width)]
    coeffs = added([a * b for a, b in zip(turned_columns, twice_lines)])
    table = gram + jnp.where(lanes == rows + width, 1.0, 0.0) - pltpu.roll(coeffs, 2 * width, 1)

    entry = {}
    for k in range(width):
        spread = column(gram, k)
        for j in range(k, width):
            entry[j, k] = line(spread, j)
    lines = [line(table, k) for k in range(width)]
    for k in range(width):
        inverse = 1.0 / entry[k, k]
        for j in range(k + 1, width):
            ratio = entry[j, k] * inverse
            for i in range(k + 1, j + 1):
                entry[j, i] = entry[j, i] - ratio * entry[i, k]
            lines[j] = lines[j] - ratio * lines[k]
    lines = [value * lax.rsqrt(entry[k, k]) for k, value in enumerate(lines)]
    upper = jnp.zeros(shape, F32)
    for k in range(width):
        upper = jnp.where((rows == k) & (lanes >= k), lines[k], upper)
    beta_ref[...] = upper[:, :width]
    stores.append(pltpu.make_async_copy(beta_ref, beta_out, sems.at[2 * orbs + 1]))
    stores[-1].start()

    same = rows == lanes % ROWS
    spots = [2 * width + lanes // ROWS, width + (lanes // ROWS) % width]
    grown = [
        jnp.concatenate(
            [jnp.where(same, jnp.take_along_axis(value, spot, axis=1), 0.0) for value in lines], 0
        )
        for spot in spots
    ]
    mixed_high, mixed_low = split(jnp.concatenate([grown[0], grown[1][:, :side]], 1))
    mixed = jnp.concatenate([mixed_high, mixed_low], 0)
    dims = ((1,), (0,))

    def chunk(o, pair):
        highs, lows = [], []
        for half in range(2):
            x = 2 * pair + half
            highs.append(jnp.concatenate([high_ref[o, x], phigh_ref[o, x]], 0))
            lows.append(jnp.concatenate([low_ref[o, x], plow_ref[o, x]], 0))
        both = dot(mixed, jnp.concatenate(highs, 1), dims)
        out = both[:side] + both[side:] + dot(mixed_high, jnp.concatenate(lows, 1), dims)
        for half in range(2):
            x = 2 * pair + half
            out_ref[o, :, x] = out[:, half * nz : (half + 1) * nz].reshape(width, ROWS, nz)

    for o in range(orbs):
        for pair in range(nx // 2):
            chunk(o, pair)
            if pair % 2:
                spot = pl.ds(2 * pair - 2, 4)
                place = 2 * o + pair // 2
                stores.append(
                    pltpu.make_async_copy(out_ref.at[o, :, spot], next_ref.at[o, :, spot], sems.at[place])
                )
                stores[-1].start()
    for store in stores:
        store.wait()


def shifted(value, axis, steps):
    count = lax.axis_size(axis)
    return lax.ppermute(value, axis, [(i, (i + steps) % count) for i in range(count)])


def swapped(value, axis, far):
    count = lax.axis_size(axis)
    return lax.ppermute(
        value, axis, [(i, (i + (1 if i % 2 == far else -1)) % count) for i in range(count)]
    )


def per_device(prev_block, block, hop_seed, levels, hop_table, onsite_table):
    orbs, width, nx, ny, nz = block.shape
    devices = lax.axis_size("gx") * lax.axis_size("gy")
    count = orbs * nx * ny * nz * devices
    fields = orbs * width
    hops = jnp.transpose(hop_table, (0, 2, 3, 1))
    onsite = onsite_table.T
    table_rows = 3 * orbs * orbs + ROWS
    outside = pl.BlockSpec(memory_space=pltpu.HBM)

    def stay(value):
        return pltpu.with_memory_space_constraint(value, pltpu.HBM)

    params = pltpu.CompilerParams(**PARAMS)

    block_here, seed_here, levels_here, hops_here, onsite_here, xup, yfar, ynear, xdown = pl.pallas_call(
        pack_kernel,
        in_specs=[outside] * 5,
        out_shape=[
            pltpu.VMEM(block.shape, F32),
            pltpu.VMEM(hop_seed.shape, jnp.int32),
            pltpu.VMEM(levels.shape, jnp.int32),
            pltpu.VMEM(hops.shape, F32),
            pltpu.VMEM(onsite.shape, F32),
            pltpu.VMEM((fields + 1, ny, nz), F32),
            pltpu.VMEM((fields + 1, nx, nz), F32),
            pltpu.VMEM((fields + 1, nx, nz), F32),
            pltpu.VMEM((fields, ny, nz), F32),
        ],
        scratch_shapes=[pltpu.SemaphoreType.DMA((orbs + 4,))],
        compiler_params=params,
        name="pack",
    )(stay(block), stay(hop_seed), stay(levels), stay(hops), stay(onsite))
    xup = shifted(xup, "gx", 1)
    yfar = swapped(yfar, "gy", 1)
    ynear = swapped(ynear, "gy", 0)
    xdown = shifted(xdown, "gx", -1)

    side = width * ny
    part, high, low, metric, table, edges = pl.pallas_call(
        interior_kernel,
        out_shape=[
            pltpu.VMEM(block.shape, F32),
            pltpu.VMEM((orbs, nx, 2 * side, nz), BF16),
            pltpu.VMEM((orbs, nx, 2 * side, nz), BF16),
            pltpu.VMEM((width, LANES), F32),
            pltpu.VMEM((table_rows, LANES), F32),
            pltpu.VMEM((2 * orbs * orbs, ny, nz), F32),
        ],
        in_specs=[outside] + [pl.BlockSpec(memory_space=pltpu.VMEM)] * 5,
        scratch_shapes=[
            pltpu.VMEM((2 * side, 4 * side), F32),
            pltpu.VMEM(block.shape, F32),
            pltpu.SemaphoreType.DMA(()),
        ],
        compiler_params=params,
        cost_estimate=pl.CostEstimate(flops=10**8, bytes_accessed=4 * 10**6, transcendentals=0),
        name="interior",
    )(stay(prev_block), block_here, seed_here, levels_here, hops_here, onsite_here)

    product_halves = [pltpu.VMEM((orbs, nx, side, nz), BF16)] * 2
    phigh, plow, total, part = pl.pallas_call(
        y_kernel,
        out_shape=product_halves
        + [pltpu.VMEM((3 * side, 2 * side), F32), pltpu.VMEM(block.shape, F32)],
        input_output_aliases={0: 3},
        compiler_params=params,
        cost_estimate=pl.CostEstimate(flops=10**8, bytes_accessed=4 * 10**6, transcendentals=0),
        name="y_faces",
    )(part, edges, table, xup, yfar, ynear, high, low)

    phigh, plow, sums = pl.pallas_call(
        x_kernel,
        out_shape=product_halves + [pltpu.VMEM((devices, width // 2, LANES), F32)],
        input_output_aliases={7: 0, 8: 1},
        scratch_shapes=[pltpu.VMEM((orbs, side, 2 * nz), F32)],
        compiler_params=params,
        name="x_faces",
    )(part, edges, xdown, high, low, total, metric, phigh, plow)

    sums = lax.all_to_all(sums, ("gx", "gy"), 0, 0)

    next_block, alpha, beta = pl.pallas_call(
        lambda *refs: final_kernel(count, *refs),
        out_shape=[
            jax.ShapeDtypeStruct(block.shape, F32),
            jax.ShapeDtypeStruct((width, width), F32),
            jax.ShapeDtypeStruct((width, width), F32),
        ],
        out_specs=[outside] * 3,
        scratch_shapes=[
            pltpu.VMEM(block.shape, F32),
            pltpu.VMEM((width, width), F32),
            pltpu.VMEM((width, width), F32),
            pltpu.SemaphoreType.DMA((2 * orbs + 2,)),
        ],
        compiler_params=params,
        name="final",
    )(sums, high, low, phigh, plow)
    return next_block, alpha, beta


def solution(mesh):
    in_specs = (
        P(None, None, "gx", "gy", None),
        P(None, None, "gx", "gy", None),
        P(None, "gx", "gy", None),
        P("gx", "gy", None),
        P(),
        P(),
    )
    out_specs = (P(None, None, "gx", "gy", None), P(), P())
    return jax.shard_map(
        per_device, mesh=mesh, in_specs=in_specs, out_specs=out_specs, check_vma=False
    )
```

```python
import jax
import jax.numpy as jnp
from jax import lax
from jax.experimental import pallas as pl
from jax.experimental.pallas import tpu as pltpu
from jax.sharding import PartitionSpec as P

HIGH = lax.Precision.HIGHEST
F32 = jnp.float32
BF16 = jnp.bfloat16
LANES = 128
ROWS = 8
PARAMS = dict(vmem_limit_bytes=32 * 1024 * 1024)


def split(value):
    high = value.astype(BF16)
    low = (value - high.astype(F32)).astype(BF16)
    return high, low


def iota(shape, dim):
    return lax.broadcasted_iota(jnp.int32, shape, dim)


def dot(left, right, dims, precision=None):
    return lax.dot_general(
        left, right, (dims, ((), ())), precision=precision, preferred_element_type=F32
    )


def pick(table_ref, row, index):
    entries = jnp.broadcast_to(table_ref[row : row + 1, :], index.shape)
    return jnp.take_along_axis(entries, index, axis=1)


def bonds_of(table_ref, direction, index, orbs):
    base = direction * orbs * orbs
    return [
        [pick(table_ref, base + a * orbs + b, index) for b in range(orbs)] for a in range(orbs)
    ]


def kept_bonds(edge_ref, direction, orbs):
    base = direction * orbs * orbs
    return [[edge_ref[base + a * orbs + b] for b in range(orbs)] for a in range(orbs)]


def fill_table(table_ref, hop_ref, onsite_ref):
    orbs, kinds = hop_ref.shape[1], hop_ref.shape[3]
    for d in range(3):
        for a in range(orbs):
            base = (d * orbs + a) * orbs
            table_ref[base : base + orbs, :kinds] = hop_ref[d, a]
    base = 3 * orbs * orbs
    table_ref[base : base + orbs, : onsite_ref.shape[1]] = onsite_ref[...]


def times(bonds, field):
    return [sum(bonds[a][b] * field[b] for b in range(len(field))) for a in range(len(field))]


def times_transposed(bonds, field):
    return [sum(bonds[a][b] * field[a] for a in range(len(field))) for b in range(len(field))]


def pack_kernel(
    block_in,
    seed_in,
    level_in,
    hop_in,
    onsite_in,
    block_ref,
    seed_ref,
    level_ref,
    hop_ref,
    onsite_ref,
    xup_ref,
    yfar_ref,
    ynear_ref,
    xdown_ref,
    sems,
):
    orbs, width, nx, ny, _ = block_ref.shape
    yeven = lax.axis_index("gy") % 2 == 0
    pairs = [(block_in.at[o], block_ref.at[o]) for o in range(orbs)]
    pairs += [(seed_in, seed_ref), (level_in, level_ref), (hop_in, hop_ref), (onsite_in, onsite_ref)]
    loads = [pltpu.make_async_copy(*pair, sems.at[i]) for i, pair in enumerate(pairs)]
    for load in loads:
        load.start()
    for o in range(orbs):
        loads[o].wait()
        for n in range(width):
            spot = o * width + n
            xup_ref[spot] = block_ref[o, n, nx - 1]
            xdown_ref[spot] = block_ref[o, n, 0]
            top, bottom = block_ref[o, n, :, ny - 1, :], block_ref[o, n, :, 0, :]
            ynear_ref[spot] = jnp.where(yeven, top, bottom)
            yfar_ref[spot] = jnp.where(yeven, bottom, top)
    loads[orbs].wait()
    xup_ref[orbs * width] = seed_ref[0, nx - 1].astype(F32)
    for ref in (ynear_ref, yfar_ref):
        ref[orbs * width] = seed_ref[1, :, ny - 1, :].astype(F32)
    for load in loads[orbs + 1 :]:
        load.wait()


def kept_sums(total):
    rows, columns = total.shape
    same = (iota((rows, columns), 0) % ROWS) == (iota((rows, columns), 1) % ROWS)
    kept = jnp.where(same, total, 0.0)
    return kept.reshape(rows // ROWS, ROWS, columns).sum(axis=1)


def gathered(value, spots):
    high, low = split(value)
    last = (value - high.astype(F32) - low.astype(F32)).astype(BF16)
    pieces = dot(jnp.concatenate([high, low, last], 0), spots.astype(BF16), ((1,), (0,)))
    rows = value.shape[0]
    return pieces[:rows] + pieces[rows : 2 * rows] + pieces[2 * rows :]


def interior_kernel(
    prev_in,
    block_ref,
    seed_ref,
    level_ref,
    hop_ref,
    onsite_ref,
    part_ref,
    high_ref,
    low_ref,
    metric_ref,
    table_ref,
    edge_ref,
    gram_ref,
    prev_ref,
    sem,
):
    orbs, width, nx, ny, nz = block_ref.shape
    load = pltpu.make_async_copy(prev_in, prev_ref, sem)
    load.start()
    fill_table(table_ref, hop_ref, onsite_ref)
    row = iota((ny, nz), 0)
    side = width * ny

    def stencil(x, carry):
        before = jnp.maximum(x - 1, 0)
        inside = jnp.where(x > 0, 1.0, 0.0)
        energy = [pick(table_ref, 3 * orbs * orbs + o, level_ref[x]) for o in range(orbs)]
        bond_x = bonds_of(table_ref, 0, seed_ref[0, before], orbs)
        bond_x = [[inside * value for value in line] for line in bond_x]
        bond_y = bonds_of(table_ref, 1, seed_ref[1, x], orbs)
        bond_z = bonds_of(table_ref, 2, seed_ref[2, x], orbs)
        for n in range(width):
            here = [block_ref[o, n, x] for o in range(orbs)]
            behind = [block_ref[o, n, before] for o in range(orbs)]
            forward = times(bond_x, here)
            for o in range(orbs):
                part_ref[o, n, before] += forward[o]
            image = [energy[o] * here[o] for o in range(orbs)]
            image = [a + b for a, b in zip(image, times_transposed(bond_x, behind))]
            ahead = [jnp.where(row == ny - 1, 0.0, pltpu.roll(v, ny - 1, 0)) for v in here]
            image = [a + b for a, b in zip(image, times(bond_y, ahead))]
            carried = times_transposed(bond_y, here)
            image = [
                a + jnp.where(row == 0, 0.0, pltpu.roll(b, 1, 0)) for a, b in zip(image, carried)
            ]
            ahead = [pltpu.roll(v, nz - 1, 1) for v in here]
            image = [a + b for a, b in zip(image, times(bond_z, ahead))]
            carried = times_transposed(bond_z, here)
            image = [a + pltpu.roll(b, 1, 1) for a, b in zip(image, carried)]
            for o in range(orbs):
                part_ref[o, n, x] = image[o]
        return carry

    lax.fori_loop(0, nx, stencil, 0, unroll=2)
    for d, index in enumerate((seed_ref[0, nx - 1], seed_ref[1, :, ny - 1, :])):
        for i, bond in enumerate(sum(bonds_of(table_ref, d, index, orbs), [])):
            edge_ref[d * orbs * orbs + i] = bond
    load.wait()
    gram_ref[...] = jnp.zeros(gram_ref.shape, F32)

    def products(pair):
        for o in range(orbs):
            highs, lows = [], []
            for half in range(2):
                x = 2 * pair + half
                basis = jnp.concatenate(
                    [prev_ref[o, :, x].reshape(side, nz), block_ref[o, :, x].reshape(side, nz)], 0
                )
                high, low = split(basis)
                high_ref[o, x] = high
                low_ref[o, x] = low
                highs.append(high)
                lows.append(low)
            high = jnp.concatenate(highs, 1)
            low = jnp.concatenate(lows, 1)
            gram_ref[...] += dot(high, jnp.concatenate([high, low], 0), ((1,), (1,)))

    for pair in range(nx // 2):
        products(pair)
    crossed = gram_ref[:, 2 * side :]
    sums = kept_sums(gram_ref[:, : 2 * side] + crossed + crossed.T)
    spots = iota((LANES, LANES), 0) // ny
    lanes = iota((LANES, LANES), 1) % (LANES // 2)
    maps = [jnp.where(lanes == width * (3 + 2 * i) + spots, 1.0, 0.0) for i in range(2)]
    parts = [sums[i * width : (i + 1) * width] for i in range(2)]
    metric_ref[...] = gathered(jnp.concatenate(parts, 1), jnp.concatenate(maps, 0))


def placed(total, base):
    width = base.shape[0]
    sums = kept_sums(total)
    spots = (iota((LANES, LANES), 0) // ROWS) % width
    sums = gathered(sums, jnp.where(iota((LANES, LANES), 1) % width == spots, 1.0, 0.0))
    place = (iota(base.shape, 1) % (LANES // 2)) // width
    for i in range(3):
        base = base + jnp.where(place == i, sums[i * width : (i + 1) * width], 0.0)
    return base


def product_sums(bhigh, blow, high, low):
    both = dot(
        jnp.concatenate([bhigh, high, blow, low], 0), jnp.concatenate([high, low], 0), ((1,), (1,))
    )
    half = both.shape[0] // 2
    return both[:half] + both[half:]


def y_kernel(
    part_in,
    edge_ref,
    table_ref,
    up_ref,
    far_ref,
    near_ref,
    high_ref,
    low_ref,
    phigh_ref,
    plow_ref,
    total_ref,
    part_ref,
):
    orbs, width, nx, ny, nz = part_ref.shape
    side = width * ny
    last = orbs * width

    bond_low = bonds_of(table_ref, 0, up_ref[last].astype(jnp.int32), orbs)
    for n in range(width):
        back = times_transposed(bond_low, [up_ref[o * width + n] for o in range(orbs)])
        for o in range(orbs):
            part_ref[o, n, 0] += back[o]

    def add_faces(low_face, high_face):
        bond = kept_bonds(edge_ref, 1, orbs)
        bond_low = bonds_of(table_ref, 1, low_face[last].astype(jnp.int32), orbs)
        for n in range(width):
            forward = times(bond, [high_face[o * width + n] for o in range(orbs)])
            back = times_transposed(bond_low, [low_face[o * width + n] for o in range(orbs)])
            for o in range(orbs):
                part_ref[o, n, :, ny - 1, :] += forward[o]
                part_ref[o, n, :, 0, :] += back[o]

    even = lax.axis_index("gy") % 2 == 0
    pl.when(even)(lambda: add_faces(far_ref, near_ref))
    pl.when(jnp.logical_not(even))(lambda: add_faces(near_ref, far_ref))

    total_ref[...] = jnp.zeros(total_ref.shape, F32)
    for first in range(1, nx - 1, 2):
        for o in range(orbs):
            ins = [[], [], [], []]
            for x in (first, first + 1):
                high, low = split(part_ref[o, :, x].reshape(side, nz))
                phigh_ref[o, x] = high
                plow_ref[o, x] = low
                for group, value in zip(ins, (high_ref[o, x], low_ref[o, x], high, low)):
                    group.append(value)
            total_ref[...] += product_sums(*(jnp.concatenate(group, 1) for group in ins))


def x_kernel(
    part_ref,
    edge_ref,
    down_ref,
    high_ref,
    low_ref,
    total_ref,
    metric_ref,
    phigh_in,
    plow_in,
    phigh_ref,
    plow_ref,
    sums_ref,
    face_ref,
):
    orbs, width, nx, ny, nz = part_ref.shape
    bond = kept_bonds(edge_ref, 0, orbs)
    for n in range(width):
        forward = times(bond, [down_ref[o * width + n] for o in range(orbs)])
        for o in range(orbs):
            face_ref[o, n * ny : (n + 1) * ny, :nz] = part_ref[o, n, 0]
            face_ref[o, n * ny : (n + 1) * ny, nz:] = part_ref[o, n, nx - 1] + forward[o]
    total = total_ref[...]
    for o in range(orbs):
        high, low = split(face_ref[o])
        for i, x in enumerate((0, nx - 1)):
            phigh_ref[o, x] = high[:, i * nz : (i + 1) * nz]
            plow_ref[o, x] = low[:, i * nz : (i + 1) * nz]
        bhigh, blow = (
            jnp.concatenate([ref[o, 0], ref[o, nx - 1]], 1) for ref in (high_ref, low_ref)
        )
        total = total + product_sums(bhigh, blow, high, low)
    packed = placed(total, metric_ref[...])
    half = width // 2
    lanes = iota((half, LANES), 1)
    folded = jnp.where(lanes < LANES // 2, packed[:half], packed[half:])
    sums_ref[...] = jnp.broadcast_to(folded[None], sums_ref.shape)


def column(value, spot):
    return jnp.broadcast_to(value[:, spot : spot + 1], value.shape)


def line(value, spot):
    return jnp.broadcast_to(value[spot : spot + 1, :], value.shape)


def added(terms):
    while len(terms) > 1:
        terms = [sum(terms[i : i + 2][1:], terms[i]) for i in range(0, len(terms), 2)]
    return terms[0]


def final_kernel(
    count,
    sums_ref,
    high_ref,
    low_ref,
    phigh_ref,
    plow_ref,
    next_ref,
    alpha_out,
    beta_out,
    out_ref,
    alpha_ref,
    beta_ref,
    row_ref,
    sems,
):
    orbs, nx, side, nz = phigh_ref.shape
    width = side // ROWS
    shape = (width, LANES)
    rows, lanes = iota(shape, 0), iota(shape, 1)
    folded = jnp.sum(sums_ref[...], axis=0) / count
    sums = jnp.concatenate([folded, pltpu.roll(folded, LANES // 2, 1)], 0)

    def moved(start, length):
        value = sums if start == 0 else pltpu.roll(sums, LANES - start, 1)
        return jnp.where(lanes < length, value, 0.0)

    first = [moved(0, width), moved(width, width)]
    norms = moved(2 * width, width)
    metric = [moved(3 * width, 2 * width), moved(5 * width, 2 * width)]
    alpha_ref[...] = first[1][:, :width]
    stores = [pltpu.make_async_copy(alpha_ref, alpha_out, sems.at[2 * orbs])]
    stores[-1].start()
    ones = [jnp.where(lanes == rows + i * width, 1.0, 0.0) for i in range(2)]
    lack = [one - value for one, value in zip(ones, metric)]
    lack_columns = [[column(value, k) for k in range(2 * width)] for value in lack]

    slots = iter(range(row_ref.shape[0]))

    def lines_of(values):
        lines = []
        for value in values:
            slot = next(slots)
            row_ref[slot] = value
            lines += [jnp.broadcast_to(row_ref[slot, k : k + 1, :], shape) for k in range(width)]
        return lines

    def lacking(pair):
        lines = lines_of(pair)
        return [added([a * b for a, b in zip(columns, lines)]) for columns in lack_columns]

    one = lacking(first)
    two = lacking(one)
    three = lacking(two)
    weighed = [added(list(terms)) for terms in zip(first, one, two, three)]
    turned = jnp.concatenate(first, 0).T[:width]
    turned_columns = [
        jnp.broadcast_to(turned[:, k : k + 1], shape) for k in range(2 * width)
    ]
    weighed_lines = lines_of(weighed)
    gram = norms - added([a * b for a, b in zip(turned_columns, weighed_lines)])
    twice = [a + b for a, b in zip(ones, lack)]
    twice_lines = lines_of(twice)
    coeffs = added([a * b for a, b in zip(turned_columns, twice_lines)])
    table = gram + jnp.where(lanes == rows + width, 1.0, 0.0) - pltpu.roll(coeffs, 2 * width, 1)

    entry = {}
    for k in range(width):
        spread = lines_of([column(gram, k)])
        for j in range(k, width):
            entry[j, k] = spread[j]
    lines = lines_of([table])
    for k in range(width):
        inverse = 1.0 / entry[k, k]
        for j in range(k + 1, width):
            ratio = entry[j, k] * inverse
            for i in range(k + 1, j + 1):
                entry[j, i] = entry[j, i] - ratio * entry[i, k]
            lines[j] = lines[j] - ratio * lines[k]
    lines = [value * lax.rsqrt(entry[k, k]) for k, value in enumerate(lines)]
    upper = jnp.zeros(shape, F32)
    for k in range(width):
        upper = jnp.where((rows == k) & (lanes >= k), lines[k], upper)
    beta_ref[...] = upper[:, :width]
    stores.append(pltpu.make_async_copy(beta_ref, beta_out, sems.at[2 * orbs + 1]))
    stores[-1].start()

    same = rows == lanes % ROWS
    spots = [2 * width + lanes // ROWS, width + (lanes // ROWS) % width]
    grown = [
        jnp.concatenate(
            [jnp.where(same, jnp.take_along_axis(value, spot, axis=1), 0.0) for value in lines], 0
        )
        for spot in spots
    ]
    mixed_high, mixed_low = split(jnp.concatenate([grown[0], grown[1][:, :side]], 1))
    mixed = jnp.concatenate([mixed_high, mixed_low], 0)
    dims = ((1,), (0,))

    def chunk(o, pair):
        highs, lows = [], []
        for half in range(2):
            x = 2 * pair + half
            highs.append(jnp.concatenate([high_ref[o, x], phigh_ref[o, x]], 0))
            lows.append(jnp.concatenate([low_ref[o, x], plow_ref[o, x]], 0))
        both = dot(mixed, jnp.concatenate(highs, 1), dims)
        out = both[:side] + both[side:] + dot(mixed_high, jnp.concatenate(lows, 1), dims)
        for half in range(2):
            x = 2 * pair + half
            out_ref[o, :, x] = out[:, half * nz : (half + 1) * nz].reshape(width, ROWS, nz)

    for o in range(orbs):
        for pair in range(nx // 2):
            chunk(o, pair)
            if pair % 2:
                spot = pl.ds(2 * pair - 2, 4)
                place = 2 * o + pair // 2
                stores.append(
                    pltpu.make_async_copy(out_ref.at[o, :, spot], next_ref.at[o, :, spot], sems.at[place])
                )
                stores[-1].start()
    for store in stores:
        store.wait()


def shifted(value, axis, steps):
    count = lax.axis_size(axis)
    return lax.ppermute(value, axis, [(i, (i + steps) % count) for i in range(count)])


def swapped(value, axis, far):
    count = lax.axis_size(axis)
    return lax.ppermute(
        value, axis, [(i, (i + (1 if i % 2 == far else -1)) % count) for i in range(count)]
    )


def per_device(prev_block, block, hop_seed, levels, hop_table, onsite_table):
    orbs, width, nx, ny, nz = block.shape
    devices = lax.axis_size("gx") * lax.axis_size("gy")
    count = orbs * nx * ny * nz * devices
    fields = orbs * width
    hops = jnp.transpose(hop_table, (0, 2, 3, 1))
    onsite = onsite_table.T
    table_rows = 3 * orbs * orbs + ROWS
    outside = pl.BlockSpec(memory_space=pltpu.HBM)

    def stay(value):
        return pltpu.with_memory_space_constraint(value, pltpu.HBM)

    params = pltpu.CompilerParams(**PARAMS)

    block_here, seed_here, levels_here, hops_here, onsite_here, xup, yfar, ynear, xdown = pl.pallas_call(
        pack_kernel,
        in_specs=[outside] * 5,
        out_shape=[
            pltpu.VMEM(block.shape, F32),
            pltpu.VMEM(hop_seed.shape, jnp.int32),
            pltpu.VMEM(levels.shape, jnp.int32),
            pltpu.VMEM(hops.shape, F32),
            pltpu.VMEM(onsite.shape, F32),
            pltpu.VMEM((fields + 1, ny, nz), F32),
            pltpu.VMEM((fields + 1, nx, nz), F32),
            pltpu.VMEM((fields + 1, nx, nz), F32),
            pltpu.VMEM((fields, ny, nz), F32),
        ],
        scratch_shapes=[pltpu.SemaphoreType.DMA((orbs + 4,))],
        compiler_params=params,
        name="pack",
    )(stay(block), stay(hop_seed), stay(levels), stay(hops), stay(onsite))
    xup = shifted(xup, "gx", 1)
    yfar = swapped(yfar, "gy", 1)
    ynear = swapped(ynear, "gy", 0)
    xdown = shifted(xdown, "gx", -1)

    side = width * ny
    part, high, low, metric, table, edges = pl.pallas_call(
        interior_kernel,
        out_shape=[
            pltpu.VMEM(block.shape, F32),
            pltpu.VMEM((orbs, nx, 2 * side, nz), BF16),
            pltpu.VMEM((orbs, nx, 2 * side, nz), BF16),
            pltpu.VMEM((width, LANES), F32),
            pltpu.VMEM((table_rows, LANES), F32),
            pltpu.VMEM((2 * orbs * orbs, ny, nz), F32),
        ],
        in_specs=[outside] + [pl.BlockSpec(memory_space=pltpu.VMEM)] * 5,
        scratch_shapes=[
            pltpu.VMEM((2 * side, 4 * side), F32),
            pltpu.VMEM(block.shape, F32),
            pltpu.SemaphoreType.DMA(()),
        ],
        compiler_params=params,
        cost_estimate=pl.CostEstimate(flops=10**8, bytes_accessed=4 * 10**6, transcendentals=0),
        name="interior",
    )(stay(prev_block), block_here, seed_here, levels_here, hops_here, onsite_here)

    product_halves = [pltpu.VMEM((orbs, nx, side, nz), BF16)] * 2
    phigh, plow, total, part = pl.pallas_call(
        y_kernel,
        out_shape=product_halves
        + [pltpu.VMEM((3 * side, 2 * side), F32), pltpu.VMEM(block.shape, F32)],
        input_output_aliases={0: 3},
        compiler_params=params,
        cost_estimate=pl.CostEstimate(flops=10**8, bytes_accessed=4 * 10**6, transcendentals=0),
        name="y_faces",
    )(part, edges, table, xup, yfar, ynear, high, low)

    phigh, plow, sums = pl.pallas_call(
        x_kernel,
        out_shape=product_halves + [pltpu.VMEM((devices, width // 2, LANES), F32)],
        input_output_aliases={7: 0, 8: 1},
        scratch_shapes=[pltpu.VMEM((orbs, side, 2 * nz), F32)],
        compiler_params=params,
        name="x_faces",
    )(part, edges, xdown, high, low, total, metric, phigh, plow)

    sums = lax.all_to_all(sums, ("gx", "gy"), 0, 0)

    next_block, alpha, beta = pl.pallas_call(
        lambda *refs: final_kernel(count, *refs),
        out_shape=[
            jax.ShapeDtypeStruct(block.shape, F32),
            jax.ShapeDtypeStruct((width, width), F32),
            jax.ShapeDtypeStruct((width, width), F32),
        ],
        out_specs=[outside] * 3,
        scratch_shapes=[
            pltpu.VMEM(block.shape, F32),
            pltpu.VMEM((width, width), F32),
            pltpu.VMEM((width, width), F32),
            pltpu.VMEM((2 * width + 4, width, LANES), F32),
            pltpu.SemaphoreType.DMA((2 * orbs + 2,)),
        ],
        compiler_params=params,
        name="final",
    )(sums, high, low, phigh, plow)
    return next_block, alpha, beta


def solution(mesh):
    in_specs = (
        P(None, None, "gx", "gy", None),
        P(None, None, "gx", "gy", None),
        P(None, "gx", "gy", None),
        P("gx", "gy", None),
        P(),
        P(),
    )
    out_specs = (P(None, None, "gx", "gy", None), P(), P())
    return jax.shard_map(
        per_device, mesh=mesh, in_specs=in_specs, out_specs=out_specs, check_vma=False
    )
```

```python
import jax
import jax.numpy as jnp
from jax import lax
from jax.experimental import pallas as pl
from jax.experimental.pallas import tpu as pltpu
from jax.sharding import PartitionSpec as P

HIGH = lax.Precision.HIGHEST
F32 = jnp.float32
BF16 = jnp.bfloat16
LANES = 128
ROWS = 8
PARAMS = dict(vmem_limit_bytes=32 * 1024 * 1024)


def split(value):
    high = value.astype(BF16)
    low = (value - high.astype(F32)).astype(BF16)
    return high, low


def iota(shape, dim):
    return lax.broadcasted_iota(jnp.int32, shape, dim)


def dot(left, right, dims, precision=None):
    return lax.dot_general(
        left, right, (dims, ((), ())), precision=precision, preferred_element_type=F32
    )


def pick(table_ref, row, index):
    entries = jnp.broadcast_to(table_ref[row : row + 1, :], index.shape)
    return jnp.take_along_axis(entries, index, axis=1)


def bonds_of(table_ref, direction, index, orbs):
    base = direction * orbs * orbs
    return [
        [pick(table_ref, base + a * orbs + b, index) for b in range(orbs)] for a in range(orbs)
    ]


def kept_bonds(edge_ref, direction, orbs):
    base = direction * orbs * orbs
    return [[edge_ref[base + a * orbs + b] for b in range(orbs)] for a in range(orbs)]


def fill_table(table_ref, hop_ref, onsite_ref):
    orbs, kinds = hop_ref.shape[1], hop_ref.shape[3]
    for d in range(3):
        for a in range(orbs):
            base = (d * orbs + a) * orbs
            table_ref[base : base + orbs, :kinds] = hop_ref[d, a]
    base = 3 * orbs * orbs
    table_ref[base : base + orbs, : onsite_ref.shape[1]] = onsite_ref[...]


def times(bonds, field):
    return [sum(bonds[a][b] * field[b] for b in range(len(field))) for a in range(len(field))]


def times_transposed(bonds, field):
    return [sum(bonds[a][b] * field[a] for a in range(len(field))) for b in range(len(field))]


def pack_kernel(
    block_in,
    seed_in,
    level_in,
    hop_in,
    onsite_in,
    block_ref,
    seed_ref,
    level_ref,
    hop_ref,
    onsite_ref,
    xup_ref,
    yfar_ref,
    ynear_ref,
    xdown_ref,
    sems,
):
    orbs, width, nx, ny, _ = block_ref.shape
    yeven = lax.axis_index("gy") % 2 == 0
    pairs = [(block_in.at[o], block_ref.at[o]) for o in range(orbs)]
    pairs += [(seed_in, seed_ref), (level_in, level_ref), (hop_in, hop_ref), (onsite_in, onsite_ref)]
    loads = [pltpu.make_async_copy(*pair, sems.at[i]) for i, pair in enumerate(pairs)]
    for load in loads:
        load.start()
    for o in range(orbs):
        loads[o].wait()
        for n in range(width):
            spot = o * width + n
            xup_ref[spot] = block_ref[o, n, nx - 1]
            xdown_ref[spot] = block_ref[o, n, 0]
            top, bottom = block_ref[o, n, :, ny - 1, :], block_ref[o, n, :, 0, :]
            ynear_ref[spot] = jnp.where(yeven, top, bottom)
            yfar_ref[spot] = jnp.where(yeven, bottom, top)
    loads[orbs].wait()
    xup_ref[orbs * width] = seed_ref[0, nx - 1].astype(F32)
    for ref in (ynear_ref, yfar_ref):
        ref[orbs * width] = seed_ref[1, :, ny - 1, :].astype(F32)
    for load in loads[orbs + 1 :]:
        load.wait()


def kept_sums(total):
    rows, columns = total.shape
    same = (iota((rows, columns), 0) % ROWS) == (iota((rows, columns), 1) % ROWS)
    kept = jnp.where(same, total, 0.0)
    return kept.reshape(rows // ROWS, ROWS, columns).sum(axis=1)


def gathered(value, spots):
    high, low = split(value)
    last = (value - high.astype(F32) - low.astype(F32)).astype(BF16)
    pieces = dot(jnp.concatenate([high, low, last], 0), spots.astype(BF16), ((1,), (0,)))
    rows = value.shape[0]
    return pieces[:rows] + pieces[rows : 2 * rows] + pieces[2 * rows :]


def interior_kernel(
    prev_in,
    block_ref,
    seed_ref,
    level_ref,
    hop_ref,
    onsite_ref,
    part_ref,
    high_ref,
    low_ref,
    metric_ref,
    table_ref,
    edge_ref,
    gram_ref,
    prev_ref,
    sem,
):
    orbs, width, nx, ny, nz = block_ref.shape
    load = pltpu.make_async_copy(prev_in, prev_ref, sem)
    load.start()
    fill_table(table_ref, hop_ref, onsite_ref)
    row = iota((ny, nz), 0)
    side = width * ny

    def stencil(x, carry):
        before = jnp.maximum(x - 1, 0)
        inside = jnp.where(x > 0, 1.0, 0.0)
        energy = [pick(table_ref, 3 * orbs * orbs + o, level_ref[x]) for o in range(orbs)]
        bond_x = bonds_of(table_ref, 0, seed_ref[0, before], orbs)
        bond_x = [[inside * value for value in line] for line in bond_x]
        bond_y = bonds_of(table_ref, 1, seed_ref[1, x], orbs)
        bond_z = bonds_of(table_ref, 2, seed_ref[2, x], orbs)
        for n in range(width):
            here = [block_ref[o, n, x] for o in range(orbs)]
            behind = [block_ref[o, n, before] for o in range(orbs)]
            forward = times(bond_x, here)
            for o in range(orbs):
                part_ref[o, n, before] += forward[o]
            image = [energy[o] * here[o] for o in range(orbs)]
            image = [a + b for a, b in zip(image, times_transposed(bond_x, behind))]
            ahead = [jnp.where(row == ny - 1, 0.0, pltpu.roll(v, ny - 1, 0)) for v in here]
            image = [a + b for a, b in zip(image, times(bond_y, ahead))]
            carried = times_transposed(bond_y, here)
            image = [
                a + jnp.where(row == 0, 0.0, pltpu.roll(b, 1, 0)) for a, b in zip(image, carried)
            ]
            ahead = [pltpu.roll(v, nz - 1, 1) for v in here]
            image = [a + b for a, b in zip(image, times(bond_z, ahead))]
            carried = times_transposed(bond_z, here)
            image = [a + pltpu.roll(b, 1, 1) for a, b in zip(image, carried)]
            for o in range(orbs):
                part_ref[o, n, x] = image[o]
        return carry

    lax.fori_loop(0, nx, stencil, 0)
    for d, index in enumerate((seed_ref[0, nx - 1], seed_ref[1, :, ny - 1, :])):
        for i, bond in enumerate(sum(bonds_of(table_ref, d, index, orbs), [])):
            edge_ref[d * orbs * orbs + i] = bond
    load.wait()
    gram_ref[...] = jnp.zeros(gram_ref.shape, F32)

    def products(pair):
        for o in range(orbs):
            highs, lows = [], []
            for half in range(2):
                x = 2 * pair + half
                basis = jnp.concatenate(
                    [prev_ref[o, :, x].reshape(side, nz), block_ref[o, :, x].reshape(side, nz)], 0
                )
                high, low = split(basis)
                high_ref[o, x] = high
                low_ref[o, x] = low
                highs.append(high)
                lows.append(low)
            high = jnp.concatenate(highs, 1)
            low = jnp.concatenate(lows, 1)
            gram_ref[...] += dot(high, jnp.concatenate([high, low], 0), ((1,), (1,)))

    for pair in range(nx // 2):
        products(pair)
    crossed = gram_ref[:, 2 * side :]
    sums = kept_sums(gram_ref[:, : 2 * side] + crossed + crossed.T)
    spots = iota((LANES, LANES), 0) // ny
    lanes = iota((LANES, LANES), 1) % (LANES // 2)
    maps = [jnp.where(lanes == width * (3 + 2 * i) + spots, 1.0, 0.0) for i in range(2)]
    parts = [sums[i * width : (i + 1) * width] for i in range(2)]
    metric_ref[...] = gathered(jnp.concatenate(parts, 1), jnp.concatenate(maps, 0))


def placed(total, base):
    width = base.shape[0]
    sums = kept_sums(total)
    spots = (iota((LANES, LANES), 0) // ROWS) % width
    sums = gathered(sums, jnp.where(iota((LANES, LANES), 1) % width == spots, 1.0, 0.0))
    place = (iota(base.shape, 1) % (LANES // 2)) // width
    for i in range(3):
        base = base + jnp.where(place == i, sums[i * width : (i + 1) * width], 0.0)
    return base


def product_sums(bhigh, blow, high, low):
    both = dot(
        jnp.concatenate([bhigh, high, blow, low], 0), jnp.concatenate([high, low], 0), ((1,), (1,))
    )
    half = both.shape[0] // 2
    return both[:half] + both[half:]


def y_kernel(
    part_in,
    edge_ref,
    table_ref,
    up_ref,
    far_ref,
    near_ref,
    high_ref,
    low_ref,
    phigh_ref,
    plow_ref,
    total_ref,
    part_ref,
):
    orbs, width, nx, ny, nz = part_ref.shape
    side = width * ny
    last = orbs * width

    bond_low = bonds_of(table_ref, 0, up_ref[last].astype(jnp.int32), orbs)
    for n in range(width):
        back = times_transposed(bond_low, [up_ref[o * width + n] for o in range(orbs)])
        for o in range(orbs):
            part_ref[o, n, 0] += back[o]

    def add_faces(low_face, high_face):
        bond = kept_bonds(edge_ref, 1, orbs)
        bond_low = bonds_of(table_ref, 1, low_face[last].astype(jnp.int32), orbs)
        for n in range(width):
            forward = times(bond, [high_face[o * width + n] for o in range(orbs)])
            back = times_transposed(bond_low, [low_face[o * width + n] for o in range(orbs)])
            for o in range(orbs):
                part_ref[o, n, :, ny - 1, :] += forward[o]
                part_ref[o, n, :, 0, :] += back[o]

    even = lax.axis_index("gy") % 2 == 0
    pl.when(even)(lambda: add_faces(far_ref, near_ref))
    pl.when(jnp.logical_not(even))(lambda: add_faces(near_ref, far_ref))

    total_ref[...] = jnp.zeros(total_ref.shape, F32)
    for first in range(1, nx - 1, 2):
        for o in range(orbs):
            ins = [[], [], [], []]
            for x in (first, first + 1):
                high, low = split(part_ref[o, :, x].reshape(side, nz))
                phigh_ref[o, x] = high
                plow_ref[o, x] = low
                for group, value in zip(ins, (high_ref[o, x], low_ref[o, x], high, low)):
                    group.append(value)
            total_ref[...] += product_sums(*(jnp.concatenate(group, 1) for group in ins))


def x_kernel(
    part_ref,
    edge_ref,
    down_ref,
    high_ref,
    low_ref,
    total_ref,
    metric_ref,
    phigh_in,
    plow_in,
    phigh_ref,
    plow_ref,
    sums_ref,
    face_ref,
):
    orbs, width, nx, ny, nz = part_ref.shape
    bond = kept_bonds(edge_ref, 0, orbs)
    for n in range(width):
        forward = times(bond, [down_ref[o * width + n] for o in range(orbs)])
        for o in range(orbs):
            face_ref[o, n * ny : (n + 1) * ny, :nz] = part_ref[o, n, 0]
            face_ref[o, n * ny : (n + 1) * ny, nz:] = part_ref[o, n, nx - 1] + forward[o]
    total = total_ref[...]
    for o in range(orbs):
        high, low = split(face_ref[o])
        for i, x in enumerate((0, nx - 1)):
            phigh_ref[o, x] = high[:, i * nz : (i + 1) * nz]
            plow_ref[o, x] = low[:, i * nz : (i + 1) * nz]
        bhigh, blow = (
            jnp.concatenate([ref[o, 0], ref[o, nx - 1]], 1) for ref in (high_ref, low_ref)
        )
        total = total + product_sums(bhigh, blow, high, low)
    packed = placed(total, metric_ref[...])
    half = width // 2
    lanes = iota((half, LANES), 1)
    folded = jnp.where(lanes < LANES // 2, packed[:half], packed[half:])
    sums_ref[...] = jnp.broadcast_to(folded[None], sums_ref.shape)


def column(value, spot):
    return jnp.broadcast_to(value[:, spot : spot + 1], value.shape)


def line(value, spot):
    return jnp.broadcast_to(value[spot : spot + 1, :], value.shape)


def added(terms):
    while len(terms) > 1:
        terms = [sum(terms[i : i + 2][1:], terms[i]) for i in range(0, len(terms), 2)]
    return terms[0]


def final_kernel(
    count,
    sums_ref,
    high_ref,
    low_ref,
    phigh_ref,
    plow_ref,
    next_ref,
    alpha_out,
    beta_out,
    out_ref,
    alpha_ref,
    beta_ref,
    row_ref,
    sems,
):
    orbs, nx, side, nz = phigh_ref.shape
    width = side // ROWS
    shape = (width, LANES)
    rows, lanes = iota(shape, 0), iota(shape, 1)
    folded = jnp.sum(sums_ref[...], axis=0) / count
    sums = jnp.concatenate([folded, pltpu.roll(folded, LANES // 2, 1)], 0)

    def moved(start, length):
        value = sums if start == 0 else pltpu.roll(sums, LANES - start, 1)
        return jnp.where(lanes < length, value, 0.0)

    first = [moved(0, width), moved(width, width)]
    norms = moved(2 * width, width)
    metric = [moved(3 * width, 2 * width), moved(5 * width, 2 * width)]
    alpha_ref[...] = first[1][:, :width]
    stores = [pltpu.make_async_copy(alpha_ref, alpha_out, sems.at[2 * orbs])]
    stores[-1].start()
    ones = [jnp.where(lanes == rows + i * width, 1.0, 0.0) for i in range(2)]
    lack = [one - value for one, value in zip(ones, metric)]
    lack_columns = [[column(value, k) for k in range(2 * width)] for value in lack]

    slots = iter(range(row_ref.shape[0]))

    def lines_of(values):
        lines = []
        for value in values:
            slot = next(slots)
            row_ref[slot] = value
            lines += [jnp.broadcast_to(row_ref[slot, k : k + 1, :], shape) for k in range(width)]
        return lines

    def lacking(pair):
        lines = lines_of(pair)
        return [added([a * b for a, b in zip(columns, lines)]) for columns in lack_columns]

    one = lacking(first)
    two = lacking(one)
    three = lacking(two)
    weighed = [added(list(terms)) for terms in zip(first, one, two, three)]
    turned = jnp.concatenate(first, 0).T[:width]
    turned_columns = [
        jnp.broadcast_to(turned[:, k : k + 1], shape) for k in range(2 * width)
    ]
    weighed_lines = lines_of(weighed)
    gram = norms - added([a * b for a, b in zip(turned_columns, weighed_lines)])
    twice = [a + b for a, b in zip(ones, lack)]
    twice_lines = lines_of(twice)
    coeffs = added([a * b for a, b in zip(turned_columns, twice_lines)])
    table = gram + jnp.where(lanes == rows + width, 1.0, 0.0) - pltpu.roll(coeffs, 2 * width, 1)

    entry = {}
    for k in range(width):
        spread = lines_of([column(gram, k)])
        for j in range(k, width):
            entry[j, k] = spread[j]
    lines = lines_of([table])
    for k in range(width):
        inverse = 1.0 / entry[k, k]
        for j in range(k + 1, width):
            ratio = entry[j, k] * inverse
            for i in range(k + 1, j + 1):
                entry[j, i] = entry[j, i] - ratio * entry[i, k]
            lines[j] = lines[j] - ratio * lines[k]
    lines = [value * lax.rsqrt(entry[k, k]) for k, value in enumerate(lines)]
    upper = jnp.zeros(shape, F32)
    for k in range(width):
        upper = jnp.where((rows == k) & (lanes >= k), lines[k], upper)
    beta_ref[...] = upper[:, :width]
    stores.append(pltpu.make_async_copy(beta_ref, beta_out, sems.at[2 * orbs + 1]))
    stores[-1].start()

    same = rows == lanes % ROWS
    spots = [2 * width + lanes // ROWS, width + (lanes // ROWS) % width]
    grown = [
        jnp.concatenate(
            [jnp.where(same, jnp.take_along_axis(value, spot, axis=1), 0.0) for value in lines], 0
        )
        for spot in spots
    ]
    mixed_high, mixed_low = split(jnp.concatenate([grown[0], grown[1][:, :side]], 1))
    mixed = jnp.concatenate([mixed_high, mixed_low], 0)
    dims = ((1,), (0,))

    def chunk(o, pair):
        highs, lows = [], []
        for half in range(2):
            x = 2 * pair + half
            highs.append(jnp.concatenate([high_ref[o, x], phigh_ref[o, x]], 0))
            lows.append(jnp.concatenate([low_ref[o, x], plow_ref[o, x]], 0))
        both = dot(mixed, jnp.concatenate(highs, 1), dims)
        out = both[:side] + both[side:] + dot(mixed_high, jnp.concatenate(lows, 1), dims)
        for half in range(2):
            x = 2 * pair + half
            out_ref[o, :, x] = out[:, half * nz : (half + 1) * nz].reshape(width, ROWS, nz)

    for o in range(orbs):
        for pair in range(nx // 2):
            chunk(o, pair)
            if pair % 2:
                spot = pl.ds(2 * pair - 2, 4)
                place = 2 * o + pair // 2
                stores.append(
                    pltpu.make_async_copy(out_ref.at[o, :, spot], next_ref.at[o, :, spot], sems.at[place])
                )
                stores[-1].start()
    for store in stores:
        store.wait()


def shifted(value, axis, steps):
    count = lax.axis_size(axis)
    return lax.ppermute(value, axis, [(i, (i + steps) % count) for i in range(count)])


def swapped(value, axis, far):
    count = lax.axis_size(axis)
    return lax.ppermute(
        value, axis, [(i, (i + (1 if i % 2 == far else -1)) % count) for i in range(count)]
    )


def per_device(prev_block, block, hop_seed, levels, hop_table, onsite_table):
    orbs, width, nx, ny, nz = block.shape
    devices = lax.axis_size("gx") * lax.axis_size("gy")
    count = orbs * nx * ny * nz * devices
    fields = orbs * width
    hops = jnp.transpose(hop_table, (0, 2, 3, 1))
    onsite = onsite_table.T
    table_rows = 3 * orbs * orbs + ROWS
    outside = pl.BlockSpec(memory_space=pltpu.HBM)

    def stay(value):
        return pltpu.with_memory_space_constraint(value, pltpu.HBM)

    params = pltpu.CompilerParams(**PARAMS)

    block_here, seed_here, levels_here, hops_here, onsite_here, xup, yfar, ynear, xdown = pl.pallas_call(
        pack_kernel,
        in_specs=[outside] * 5,
        out_shape=[
            pltpu.VMEM(block.shape, F32),
            pltpu.VMEM(hop_seed.shape, jnp.int32),
            pltpu.VMEM(levels.shape, jnp.int32),
            pltpu.VMEM(hops.shape, F32),
            pltpu.VMEM(onsite.shape, F32),
            pltpu.VMEM((fields + 1, ny, nz), F32),
            pltpu.VMEM((fields + 1, nx, nz), F32),
            pltpu.VMEM((fields + 1, nx, nz), F32),
            pltpu.VMEM((fields, ny, nz), F32),
        ],
        scratch_shapes=[pltpu.SemaphoreType.DMA((orbs + 4,))],
        compiler_params=params,
        name="pack",
    )(stay(block), stay(hop_seed), stay(levels), stay(hops), stay(onsite))
    xup = shifted(xup, "gx", 1)
    yfar = swapped(yfar, "gy", 1)
    ynear = swapped(ynear, "gy", 0)
    xdown = shifted(xdown, "gx", -1)

    side = width * ny
    part, high, low, metric, table, edges = pl.pallas_call(
        interior_kernel,
        out_shape=[
            pltpu.VMEM(block.shape, F32),
            pltpu.VMEM((orbs, nx, 2 * side, nz), BF16),
            pltpu.VMEM((orbs, nx, 2 * side, nz), BF16),
            pltpu.VMEM((width, LANES), F32),
            pltpu.VMEM((table_rows, LANES), F32),
            pltpu.VMEM((2 * orbs * orbs, ny, nz), F32),
        ],
        in_specs=[outside] + [pl.BlockSpec(memory_space=pltpu.VMEM)] * 5,
        scratch_shapes=[
            pltpu.VMEM((2 * side, 4 * side), F32),
            pltpu.VMEM(block.shape, F32),
            pltpu.SemaphoreType.DMA(()),
        ],
        compiler_params=params,
        cost_estimate=pl.CostEstimate(flops=10**8, bytes_accessed=4 * 10**6, transcendentals=0),
        name="interior",
    )(stay(prev_block), block_here, seed_here, levels_here, hops_here, onsite_here)

    product_halves = [pltpu.VMEM((orbs, nx, side, nz), BF16)] * 2
    phigh, plow, total, part = pl.pallas_call(
        y_kernel,
        out_shape=product_halves
        + [pltpu.VMEM((3 * side, 2 * side), F32), pltpu.VMEM(block.shape, F32)],
        input_output_aliases={0: 3},
        compiler_params=params,
        cost_estimate=pl.CostEstimate(flops=10**8, bytes_accessed=4 * 10**6, transcendentals=0),
        name="y_faces",
    )(part, edges, table, xup, yfar, ynear, high, low)

    phigh, plow, sums = pl.pallas_call(
        x_kernel,
        out_shape=product_halves + [pltpu.VMEM((devices, width // 2, LANES), F32)],
        input_output_aliases={7: 0, 8: 1},
        scratch_shapes=[pltpu.VMEM((orbs, side, 2 * nz), F32)],
        compiler_params=params,
        name="x_faces",
    )(part, edges, xdown, high, low, total, metric, phigh, plow)

    sums = lax.all_to_all(sums, ("gx", "gy"), 0, 0)

    next_block, alpha, beta = pl.pallas_call(
        lambda *refs: final_kernel(count, *refs),
        out_shape=[
            jax.ShapeDtypeStruct(block.shape, F32),
            jax.ShapeDtypeStruct((width, width), F32),
            jax.ShapeDtypeStruct((width, width), F32),
        ],
        out_specs=[outside] * 3,
        scratch_shapes=[
            pltpu.VMEM(block.shape, F32),
            pltpu.VMEM((width, width), F32),
            pltpu.VMEM((width, width), F32),
            pltpu.VMEM((2 * width + 4, width, LANES), F32),
            pltpu.SemaphoreType.DMA((2 * orbs + 2,)),
        ],
        compiler_params=params,
        name="final",
    )(sums, high, low, phigh, plow)
    return next_block, alpha, beta


def solution(mesh):
    in_specs = (
        P(None, None, "gx", "gy", None),
        P(None, None, "gx", "gy", None),
        P(None, "gx", "gy", None),
        P("gx", "gy", None),
        P(),
        P(),
    )
    out_specs = (P(None, None, "gx", "gy", None), P(), P())
    return jax.shard_map(
        per_device, mesh=mesh, in_specs=in_specs, out_specs=out_specs, check_vma=False
    )
```

```python
import jax
import jax.numpy as jnp
from jax import lax
from jax.experimental import pallas as pl
from jax.experimental.pallas import tpu as pltpu
from jax.sharding import PartitionSpec as P

HIGH = lax.Precision.HIGHEST
F32 = jnp.float32
BF16 = jnp.bfloat16
LANES = 128
ROWS = 8
PARAMS = dict(vmem_limit_bytes=32 * 1024 * 1024)


def split(value):
    high = value.astype(BF16)
    low = (value - high.astype(F32)).astype(BF16)
    return high, low


def iota(shape, dim):
    return lax.broadcasted_iota(jnp.int32, shape, dim)


def dot(left, right, dims, precision=None):
    return lax.dot_general(
        left, right, (dims, ((), ())), precision=precision, preferred_element_type=F32
    )


def pick(table_ref, row, index):
    entries = jnp.broadcast_to(table_ref[row : row + 1, :], index.shape)
    return jnp.take_along_axis(entries, index, axis=1)


def bonds_of(table_ref, direction, index, orbs):
    base = direction * orbs * orbs
    return [
        [pick(table_ref, base + a * orbs + b, index) for b in range(orbs)] for a in range(orbs)
    ]


def kept_bonds(edge_ref, direction, orbs):
    base = direction * orbs * orbs
    return [[edge_ref[base + a * orbs + b] for b in range(orbs)] for a in range(orbs)]


def fill_table(table_ref, hop_ref, onsite_ref):
    orbs, kinds = hop_ref.shape[1], hop_ref.shape[3]
    for d in range(3):
        for a in range(orbs):
            base = (d * orbs + a) * orbs
            table_ref[base : base + orbs, :kinds] = hop_ref[d, a]
    base = 3 * orbs * orbs
    table_ref[base : base + orbs, : onsite_ref.shape[1]] = onsite_ref[...]


def times(bonds, field):
    return [sum(bonds[a][b] * field[b] for b in range(len(field))) for a in range(len(field))]


def times_transposed(bonds, field):
    return [sum(bonds[a][b] * field[a] for a in range(len(field))) for b in range(len(field))]


def pack_kernel(
    block_in,
    seed_in,
    level_in,
    hop_in,
    onsite_in,
    block_ref,
    seed_ref,
    level_ref,
    hop_ref,
    onsite_ref,
    xup_ref,
    yfar_ref,
    ynear_ref,
    xdown_ref,
    sems,
):
    orbs, width, nx, ny, _ = block_ref.shape
    yeven = lax.axis_index("gy") % 2 == 0
    pairs = [(block_in.at[o], block_ref.at[o]) for o in range(orbs)]
    pairs += [(seed_in, seed_ref), (level_in, level_ref), (hop_in, hop_ref), (onsite_in, onsite_ref)]
    loads = [pltpu.make_async_copy(*pair, sems.at[i]) for i, pair in enumerate(pairs)]
    for load in loads[orbs:] + loads[:orbs]:
        load.start()
    for o in range(orbs):
        loads[o].wait()
        for n in range(width):
            spot = o * width + n
            xup_ref[spot] = block_ref[o, n, nx - 1]
            xdown_ref[spot] = block_ref[o, n, 0]
            top, bottom = block_ref[o, n, :, ny - 1, :], block_ref[o, n, :, 0, :]
            ynear_ref[spot] = jnp.where(yeven, top, bottom)
            yfar_ref[spot] = jnp.where(yeven, bottom, top)
    loads[orbs].wait()
    xup_ref[orbs * width] = seed_ref[0, nx - 1].astype(F32)
    for ref in (ynear_ref, yfar_ref):
        ref[orbs * width] = seed_ref[1, :, ny - 1, :].astype(F32)
    for load in loads[orbs + 1 :]:
        load.wait()


def kept_sums(total):
    rows, columns = total.shape
    same = (iota((rows, columns), 0) % ROWS) == (iota((rows, columns), 1) % ROWS)
    kept = jnp.where(same, total, 0.0)
    return kept.reshape(rows // ROWS, ROWS, columns).sum(axis=1)


def gathered(value, spots):
    high, low = split(value)
    last = (value - high.astype(F32) - low.astype(F32)).astype(BF16)
    pieces = dot(jnp.concatenate([high, low, last], 0), spots.astype(BF16), ((1,), (0,)))
    rows = value.shape[0]
    return pieces[:rows] + pieces[rows : 2 * rows] + pieces[2 * rows :]


def interior_kernel(
    prev_in,
    block_ref,
    seed_ref,
    level_ref,
    hop_ref,
    onsite_ref,
    part_ref,
    high_ref,
    low_ref,
    metric_ref,
    table_ref,
    edge_ref,
    gram_ref,
    prev_ref,
    sem,
):
    orbs, width, nx, ny, nz = block_ref.shape
    load = pltpu.make_async_copy(prev_in, prev_ref, sem)
    load.start()
    fill_table(table_ref, hop_ref, onsite_ref)
    row = iota((ny, nz), 0)
    side = width * ny

    def stencil(x, carry):
        before = jnp.maximum(x - 1, 0)
        inside = jnp.where(x > 0, 1.0, 0.0)
        energy = [pick(table_ref, 3 * orbs * orbs + o, level_ref[x]) for o in range(orbs)]
        bond_x = bonds_of(table_ref, 0, seed_ref[0, before], orbs)
        bond_x = [[inside * value for value in line] for line in bond_x]
        bond_y = bonds_of(table_ref, 1, seed_ref[1, x], orbs)
        bond_z = bonds_of(table_ref, 2, seed_ref[2, x], orbs)
        for n in range(width):
            here = [block_ref[o, n, x] for o in range(orbs)]
            behind = [block_ref[o, n, before] for o in range(orbs)]
            forward = times(bond_x, here)
            for o in range(orbs):
                part_ref[o, n, before] += forward[o]
            image = [energy[o] * here[o] for o in range(orbs)]
            image = [a + b for a, b in zip(image, times_transposed(bond_x, behind))]
            ahead = [jnp.where(row == ny - 1, 0.0, pltpu.roll(v, ny - 1, 0)) for v in here]
            image = [a + b for a, b in zip(image, times(bond_y, ahead))]
            carried = times_transposed(bond_y, here)
            image = [
                a + jnp.where(row == 0, 0.0, pltpu.roll(b, 1, 0)) for a, b in zip(image, carried)
            ]
            ahead = [pltpu.roll(v, nz - 1, 1) for v in here]
            image = [a + b for a, b in zip(image, times(bond_z, ahead))]
            carried = times_transposed(bond_z, here)
            image = [a + pltpu.roll(b, 1, 1) for a, b in zip(image, carried)]
            for o in range(orbs):
                part_ref[o, n, x] = image[o]
        return carry

    lax.fori_loop(0, nx, stencil, 0)
    for d, index in enumerate((seed_ref[0, nx - 1], seed_ref[1, :, ny - 1, :])):
        for i, bond in enumerate(sum(bonds_of(table_ref, d, index, orbs), [])):
            edge_ref[d * orbs * orbs + i] = bond
    load.wait()
    gram_ref[...] = jnp.zeros(gram_ref.shape, F32)

    def products(pair):
        for o in range(orbs):
            highs, lows = [], []
            for half in range(2):
                x = 2 * pair + half
                basis = jnp.concatenate(
                    [prev_ref[o, :, x].reshape(side, nz), block_ref[o, :, x].reshape(side, nz)], 0
                )
                high, low = split(basis)
                high_ref[o, x] = high
                low_ref[o, x] = low
                highs.append(high)
                lows.append(low)
            high = jnp.concatenate(highs, 1)
            low = jnp.concatenate(lows, 1)
            gram_ref[...] += dot(high, jnp.concatenate([high, low], 0), ((1,), (1,)))

    for pair in range(nx // 2):
        products(pair)
    crossed = gram_ref[:, 2 * side :]
    sums = kept_sums(gram_ref[:, : 2 * side] + crossed + crossed.T)
    spots = iota((LANES, LANES), 0) // ny
    lanes = iota((LANES, LANES), 1) % (LANES // 2)
    maps = [jnp.where(lanes == width * (3 + 2 * i) + spots, 1.0, 0.0) for i in range(2)]
    parts = [sums[i * width : (i + 1) * width] for i in range(2)]
    metric_ref[...] = gathered(jnp.concatenate(parts, 1), jnp.concatenate(maps, 0))


def placed(total, base):
    width = base.shape[0]
    sums = kept_sums(total)
    spots = (iota((LANES, LANES), 0) // ROWS) % width
    sums = gathered(sums, jnp.where(iota((LANES, LANES), 1) % width == spots, 1.0, 0.0))
    place = (iota(base.shape, 1) % (LANES // 2)) // width
    for i in range(3):
        base = base + jnp.where(place == i, sums[i * width : (i + 1) * width], 0.0)
    return base


def product_sums(bhigh, blow, high, low):
    both = dot(
        jnp.concatenate([bhigh, high, blow, low], 0), jnp.concatenate([high, low], 0), ((1,), (1,))
    )
    half = both.shape[0] // 2
    return both[:half] + both[half:]


def y_kernel(
    part_in,
    edge_ref,
    table_ref,
    up_ref,
    far_ref,
    near_ref,
    high_ref,
    low_ref,
    phigh_ref,
    plow_ref,
    total_ref,
    part_ref,
):
    orbs, width, nx, ny, nz = part_ref.shape
    side = width * ny
    last = orbs * width

    bond_low = bonds_of(table_ref, 0, up_ref[last].astype(jnp.int32), orbs)
    for n in range(width):
        back = times_transposed(bond_low, [up_ref[o * width + n] for o in range(orbs)])
        for o in range(orbs):
            part_ref[o, n, 0] += back[o]

    def add_faces(low_face, high_face):
        bond = kept_bonds(edge_ref, 1, orbs)
        bond_low = bonds_of(table_ref, 1, low_face[last].astype(jnp.int32), orbs)
        for n in range(width):
            forward = times(bond, [high_face[o * width + n] for o in range(orbs)])
            back = times_transposed(bond_low, [low_face[o * width + n] for o in range(orbs)])
            for o in range(orbs):
                part_ref[o, n, :, ny - 1, :] += forward[o]
                part_ref[o, n, :, 0, :] += back[o]

    even = lax.axis_index("gy") % 2 == 0
    pl.when(even)(lambda: add_faces(far_ref, near_ref))
    pl.when(jnp.logical_not(even))(lambda: add_faces(near_ref, far_ref))

    total_ref[...] = jnp.zeros(total_ref.shape, F32)
    for first in range(1, nx - 1, 2):
        for o in range(orbs):
            ins = [[], [], [], []]
            for x in (first, first + 1):
                high, low = split(part_ref[o, :, x].reshape(side, nz))
                phigh_ref[o, x] = high
                plow_ref[o, x] = low
                for group, value in zip(ins, (high_ref[o, x], low_ref[o, x], high, low)):
                    group.append(value)
            total_ref[...] += product_sums(*(jnp.concatenate(group, 1) for group in ins))


def x_kernel(
    part_ref,
    edge_ref,
    down_ref,
    high_ref,
    low_ref,
    total_ref,
    metric_ref,
    phigh_in,
    plow_in,
    phigh_ref,
    plow_ref,
    sums_ref,
    face_ref,
):
    orbs, width, nx, ny, nz = part_ref.shape
    bond = kept_bonds(edge_ref, 0, orbs)
    for n in range(width):
        forward = times(bond, [down_ref[o * width + n] for o in range(orbs)])
        for o in range(orbs):
            face_ref[o, n * ny : (n + 1) * ny, :nz] = part_ref[o, n, 0]
            face_ref[o, n * ny : (n + 1) * ny, nz:] = part_ref[o, n, nx - 1] + forward[o]
    total = total_ref[...]
    for o in range(orbs):
        high, low = split(face_ref[o])
        for i, x in enumerate((0, nx - 1)):
            phigh_ref[o, x] = high[:, i * nz : (i + 1) * nz]
            plow_ref[o, x] = low[:, i * nz : (i + 1) * nz]
        bhigh, blow = (
            jnp.concatenate([ref[o, 0], ref[o, nx - 1]], 1) for ref in (high_ref, low_ref)
        )
        total = total + product_sums(bhigh, blow, high, low)
    packed = placed(total, metric_ref[...])
    half = width // 2
    lanes = iota((half, LANES), 1)
    folded = jnp.where(lanes < LANES // 2, packed[:half], packed[half:])
    sums_ref[...] = jnp.broadcast_to(folded[None], sums_ref.shape)


def column(value, spot):
    return jnp.broadcast_to(value[:, spot : spot + 1], value.shape)


def line(value, spot):
    return jnp.broadcast_to(value[spot : spot + 1, :], value.shape)


def added(terms):
    while len(terms) > 1:
        terms = [sum(terms[i : i + 2][1:], terms[i]) for i in range(0, len(terms), 2)]
    return terms[0]


def final_kernel(
    count,
    sums_ref,
    high_ref,
    low_ref,
    phigh_ref,
    plow_ref,
    next_ref,
    alpha_out,
    beta_out,
    out_ref,
    alpha_ref,
    beta_ref,
    sems,
):
    orbs, nx, side, nz = phigh_ref.shape
    width = side // ROWS
    shape = (width, LANES)
    rows, lanes = iota(shape, 0), iota(shape, 1)
    folded = jnp.sum(sums_ref[...], axis=0) / count
    sums = jnp.concatenate([folded, pltpu.roll(folded, LANES // 2, 1)], 0)

    def moved(start, length):
        value = sums if start == 0 else pltpu.roll(sums, LANES - start, 1)
        return jnp.where(lanes < length, value, 0.0)

    first = [moved(0, width), moved(width, width)]
    norms = moved(2 * width, width)
    metric = [moved(3 * width, 2 * width), moved(5 * width, 2 * width)]
    alpha_ref[...] = first[1][:, :width]
    stores = [pltpu.make_async_copy(alpha_ref, alpha_out, sems.at[2 * orbs])]
    stores[-1].start()
    ones = [jnp.where(lanes == rows + i * width, 1.0, 0.0) for i in range(2)]
    lack = [one - value for one, value in zip(ones, metric)]
    lack_columns = [[column(value, k) for k in range(2 * width)] for value in lack]

    def lacking(pair):
        lines = [line(value, k) for value in pair for k in range(width)]
        return [added([a * b for a, b in zip(columns, lines)]) for columns in lack_columns]

    one = lacking(first)
    two = lacking(one)
    three = lacking(two)
    weighed = [added(list(terms)) for terms in zip(first, one, two, three)]
    turned = jnp.concatenate(first, 0).T[:width]
    turned_columns = [
        jnp.broadcast_to(turned[:, k : k + 1], shape) for k in range(2 * width)
    ]
    weighed_lines = [line(value, k) for value in weighed for k in range(width)]
    gram = norms - added([a * b for a, b in zip(turned_columns, weighed_lines)])
    twice = [a + b for a, b in zip(ones, lack)]
    twice_lines = [line(value, k) for value in twice for k in range(width)]
    coeffs = added([a * b for a, b in zip(turned_columns, twice_lines)])
    table = gram + jnp.where(lanes == rows + width, 1.0, 0.0) - pltpu.roll(coeffs, 2 * width, 1)

    entry = {}
    for k in range(width):
        spread = column(gram, k)
        for j in range(k, width):
            entry[j, k] = line(spread, j)
    lines = [line(table, k) for k in range(width)]
    for k in range(width):
        inverse = 1.0 / entry[k, k]
        for j in range(k + 1, width):
            ratio = entry[j, k] * inverse
            for i in range(k + 1, j + 1):
                entry[j, i] = entry[j, i] - ratio * entry[i, k]
            lines[j] = lines[j] - ratio * lines[k]
    lines = [value * lax.rsqrt(entry[k, k]) for k, value in enumerate(lines)]
    upper = jnp.zeros(shape, F32)
    for k in range(width):
        upper = jnp.where((rows == k) & (lanes >= k), lines[k], upper)
    beta_ref[...] = upper[:, :width]
    stores.append(pltpu.make_async_copy(beta_ref, beta_out, sems.at[2 * orbs + 1]))
    stores[-1].start()

    same = rows == lanes % ROWS
    spots = [2 * width + lanes // ROWS, width + (lanes // ROWS) % width]
    grown = [
        jnp.concatenate(
            [jnp.where(same, jnp.take_along_axis(value, spot, axis=1), 0.0) for value in lines], 0
        )
        for spot in spots
    ]
    mixed_high, mixed_low = split(jnp.concatenate([grown[0], grown[1][:, :side]], 1))
    mixed = jnp.concatenate([mixed_high, mixed_low], 0)
    dims = ((1,), (0,))

    def chunk(o, pair):
        highs, lows = [], []
        for half in range(2):
            x = 2 * pair + half
            highs.append(jnp.concatenate([high_ref[o, x], phigh_ref[o, x]], 0))
            lows.append(jnp.concatenate([low_ref[o, x], plow_ref[o, x]], 0))
        both = dot(mixed, jnp.concatenate(highs, 1), dims)
        out = both[:side] + both[side:] + dot(mixed_high, jnp.concatenate(lows, 1), dims)
        for half in range(2):
            x = 2 * pair + half
            out_ref[o, :, x] = out[:, half * nz : (half + 1) * nz].reshape(width, ROWS, nz)

    for o in range(orbs):
        for pair in range(nx // 2):
            chunk(o, pair)
            if pair % 2:
                spot = pl.ds(2 * pair - 2, 4)
                place = 2 * o + pair // 2
                stores.append(
                    pltpu.make_async_copy(out_ref.at[o, :, spot], next_ref.at[o, :, spot], sems.at[place])
                )
                stores[-1].start()
    for store in stores:
        store.wait()


def shifted(value, axis, steps):
    count = lax.axis_size(axis)
    return lax.ppermute(value, axis, [(i, (i + steps) % count) for i in range(count)])


def swapped(value, axis, far):
    count = lax.axis_size(axis)
    return lax.ppermute(
        value, axis, [(i, (i + (1 if i % 2 == far else -1)) % count) for i in range(count)]
    )


def per_device(prev_block, block, hop_seed, levels, hop_table, onsite_table):
    orbs, width, nx, ny, nz = block.shape
    devices = lax.axis_size("gx") * lax.axis_size("gy")
    count = orbs * nx * ny * nz * devices
    fields = orbs * width
    hops = jnp.transpose(hop_table, (0, 2, 3, 1))
    onsite = onsite_table.T
    table_rows = 3 * orbs * orbs + ROWS
    outside = pl.BlockSpec(memory_space=pltpu.HBM)

    def stay(value):
        return pltpu.with_memory_space_constraint(value, pltpu.HBM)

    params = pltpu.CompilerParams(**PARAMS)

    block_here, seed_here, levels_here, hops_here, onsite_here, xup, yfar, ynear, xdown = pl.pallas_call(
        pack_kernel,
        in_specs=[outside] * 5,
        out_shape=[
            pltpu.VMEM(block.shape, F32),
            pltpu.VMEM(hop_seed.shape, jnp.int32),
            pltpu.VMEM(levels.shape, jnp.int32),
            pltpu.VMEM(hops.shape, F32),
            pltpu.VMEM(onsite.shape, F32),
            pltpu.VMEM((fields + 1, ny, nz), F32),
            pltpu.VMEM((fields + 1, nx, nz), F32),
            pltpu.VMEM((fields + 1, nx, nz), F32),
            pltpu.VMEM((fields, ny, nz), F32),
        ],
        scratch_shapes=[pltpu.SemaphoreType.DMA((orbs + 4,))],
        compiler_params=params,
        name="pack",
    )(stay(block), stay(hop_seed), stay(levels), stay(hops), stay(onsite))
    xup = shifted(xup, "gx", 1)
    yfar = swapped(yfar, "gy", 1)
    ynear = swapped(ynear, "gy", 0)
    xdown = shifted(xdown, "gx", -1)

    side = width * ny
    part, high, low, metric, table, edges = pl.pallas_call(
        interior_kernel,
        out_shape=[
            pltpu.VMEM(block.shape, F32),
            pltpu.VMEM((orbs, nx, 2 * side, nz), BF16),
            pltpu.VMEM((orbs, nx, 2 * side, nz), BF16),
            pltpu.VMEM((width, LANES), F32),
            pltpu.VMEM((table_rows, LANES), F32),
            pltpu.VMEM((2 * orbs * orbs, ny, nz), F32),
        ],
        in_specs=[outside] + [pl.BlockSpec(memory_space=pltpu.VMEM)] * 5,
        scratch_shapes=[
            pltpu.VMEM((2 * side, 4 * side), F32),
            pltpu.VMEM(block.shape, F32),
            pltpu.SemaphoreType.DMA(()),
        ],
        compiler_params=params,
        cost_estimate=pl.CostEstimate(flops=10**8, bytes_accessed=4 * 10**6, transcendentals=0),
        name="interior",
    )(stay(prev_block), block_here, seed_here, levels_here, hops_here, onsite_here)

    product_halves = [pltpu.VMEM((orbs, nx, side, nz), BF16)] * 2
    phigh, plow, total, part = pl.pallas_call(
        y_kernel,
        out_shape=product_halves
        + [pltpu.VMEM((3 * side, 2 * side), F32), pltpu.VMEM(block.shape, F32)],
        input_output_aliases={0: 3},
        compiler_params=params,
        cost_estimate=pl.CostEstimate(flops=10**8, bytes_accessed=4 * 10**6, transcendentals=0),
        name="y_faces",
    )(part, edges, table, xup, yfar, ynear, high, low)

    phigh, plow, sums = pl.pallas_call(
        x_kernel,
        out_shape=product_halves + [pltpu.VMEM((devices, width // 2, LANES), F32)],
        input_output_aliases={7: 0, 8: 1},
        scratch_shapes=[pltpu.VMEM((orbs, side, 2 * nz), F32)],
        compiler_params=params,
        name="x_faces",
    )(part, edges, xdown, high, low, total, metric, phigh, plow)

    sums = lax.all_to_all(sums, ("gx", "gy"), 0, 0)

    next_block, alpha, beta = pl.pallas_call(
        lambda *refs: final_kernel(count, *refs),
        out_shape=[
            jax.ShapeDtypeStruct(block.shape, F32),
            jax.ShapeDtypeStruct((width, width), F32),
            jax.ShapeDtypeStruct((width, width), F32),
        ],
        out_specs=[outside] * 3,
        scratch_shapes=[
            pltpu.VMEM(block.shape, F32),
            pltpu.VMEM((width, width), F32),
            pltpu.VMEM((width, width), F32),
            pltpu.SemaphoreType.DMA((2 * orbs + 2,)),
        ],
        compiler_params=params,
        name="final",
    )(sums, high, low, phigh, plow)
    return next_block, alpha, beta


def solution(mesh):
    in_specs = (
        P(None, None, "gx", "gy", None),
        P(None, None, "gx", "gy", None),
        P(None, "gx", "gy", None),
        P("gx", "gy", None),
        P(),
        P(),
    )
    out_specs = (P(None, None, "gx", "gy", None), P(), P())
    return jax.shard_map(
        per_device, mesh=mesh, in_specs=in_specs, out_specs=out_specs, check_vma=False
    )
```
